512 devices in a mesh: tm: 64 (over z, y_hi, core), freq: 8 (over x, y_lo).
Axes of the slice: x: 4, y: 8 (y_hi: 4, y_lo: 2; y = y_hi * 2 + y_lo), z: 8, core: 2. Of those that a mesh axis runs over, the one named last changes fastest.
Arguments:
- tokens: bfloat16 [2, 64, 512, 768], P(None, 'freq', 'tm'), may hold values from -6 to 6
- cotangent: bfloat16 [2, 64, 512, 768], P(None, 'freq', 'tm'), may hold values from -6 to 6
- qkv_plain: bfloat16 [768, 1152], P(None, 'freq'), may hold values from -0.21875 to 0.21875
- qkv_shift: bfloat16 [768, 1152], P(None, 'freq'), may hold values from -0.21875 to 0.21875
- proj_plain: bfloat16 [384, 768], P('freq'), may hold values from -0.3125 to 0.3125
- proj_shift: bfloat16 [384, 768], P('freq'), may hold values from -0.3125 to 0.3125
- table_plain: float32 [12, 225], replicated, may hold values from -5 to 305
- table_shift: float32 [12, 225], replicated, may hold values from -5 to 305
Outputs:
- grad_tokens: bfloat16 [2, 64, 512, 768], P(None, 'freq', 'tm')
- grad_proj_plain: float32 [384, 768], P('freq')
- grad_proj_shift: float32 [384, 768], P('freq')
The draws below stay inside these ranges and needn't reach their ends.
All inputs are finite; a program needn't handle non-finite values.
Results may differ from the reference program's by a relative error of at most 0.022.
Values may be sent and summed in bfloat16 or wider, within the bound.
No kernel may reach another device: no remote copies, remote signals or barrier semaphores. Data moves between devices by JAX's collectives and lax.ppermute only.
A program may use at most 64 MiB of HBM per device.

```python
import math
import jax
import jax.numpy as jnp
from jax import lax

D = 768
HEADS = 12
HEAD_DIM = 32
WIN = 8
SHIFT = 4
REL = 225
SAMPLES = 2
F = 64
TM = 512
TOKENS = 65536


def table_values(key, peak):
    base_key, strength_key = jax.random.split(key, 2)
    base = jnp.clip(jax.random.normal(base_key, (HEADS, REL), jnp.float32), -5.0, 5.0)
    order = jax.random.permutation(strength_key, HEADS).astype(jnp.float32)
    strength = peak * (120.0 + 180.0 * order / max(HEADS - 1, 1))
    column = jnp.arange(REL)[None, :]
    base = base + jnp.where(column == REL - 1, strength[:, None], 0.0)
    base = base + jnp.where(column == REL - 2, strength[:, None], 0.0)
    return base


def draw_table_plain(key, part):
    key = jax.random.fold_in(key, 11)
    return table_values(key, 0.0)


def draw_table_shift(key, part):
    key = jax.random.fold_in(key, 12)
    return table_values(key, 0.0)


def level_of(stream_key, dims, shards, smallest, high):
    gain = 1.0
    for axis_at, parts in shards:
        draws = jax.random.uniform(jax.random.fold_in(jax.random.fold_in(stream_key, 6), axis_at), (parts,), jnp.float32, smallest / len(shards), high / len(shards))
        gain = gain * jnp.repeat(jnp.exp(draws), dims[axis_at] // parts).reshape((-1,) + (1,) * (len(dims) - 1 - axis_at))
    return gain


def normal_values(stream_key, dims, width, limit, cuts=(), kind=jnp.bfloat16):
    entries = width * jax.random.normal(stream_key, dims, jnp.float32)
    if cuts:
        entries = entries * level_of(stream_key, dims, cuts, -0.22, 0.18)
    return jnp.clip(entries, -limit, limit).astype(kind)


def setup_inputs(seed: int = 0) -> dict:
    keys = jax.random.split(jax.random.key(seed), 9)
    return {
        "tokens": normal_values(keys[0], (SAMPLES, F, TM, D), 1.0, 6.0, ((1, 8), (2, 64))),
        "cotangent": normal_values(keys[1], (SAMPLES, F, TM, D), 1.0, 6.0, ((1, 8), (2, 64))),
        "qkv_plain": normal_values(keys[2], (D, 3 * HEADS * HEAD_DIM), D ** -0.5, 0.21875, ((1, 8),)),
        "qkv_shift": normal_values(keys[3], (D, 3 * HEADS * HEAD_DIM), D ** -0.5, 0.21875, ((1, 8),)),
        "proj_plain": normal_values(keys[4], (HEADS * HEAD_DIM, D), (HEADS * HEAD_DIM) ** -0.5, 0.3125, ((0, 8),)),
        "proj_shift": normal_values(keys[5], (HEADS * HEAD_DIM, D), (HEADS * HEAD_DIM) ** -0.5, 0.3125, ((0, 8),)),
        "table_plain": draw_table_plain(jax.random.fold_in(keys[8], 71), 0),
        "table_shift": draw_table_shift(jax.random.fold_in(keys[8], 71), 0),
    }


NEG = -1e+30
EPS = 1e-05

def layer_norm(values):
    center = values - lax.optimization_barrier(jnp.mean(values, axis=-1, keepdims=True))
    rstd = lax.rsqrt(lax.optimization_barrier(jnp.mean(center * center, axis=-1, keepdims=True)) + EPS)
    return (center * rstd, rstd)

def offset_index():
    spots = jnp.arange(WIN * WIN)
    rows = spots // WIN
    cols = spots % WIN
    return ((rows[:, None] - rows[None, :] + WIN - 1) * (2 * WIN - 1) + cols[:, None] - cols[None, :] + WIN - 1).astype(jnp.int32)

def to_windows(grid):
    return grid.reshape(F // WIN, WIN, TM // WIN, WIN, -1).transpose(0, 2, 1, 3, 4).reshape(-1, WIN * WIN, grid.shape[-1])

def from_windows(blocks):
    return blocks.reshape(F // WIN, TM // WIN, WIN, WIN, -1).transpose(0, 2, 1, 3, 4).reshape(F, TM, blocks.shape[-1])

def forward_windows(window_tokens, w_qkv, bias, allow):
    count = window_tokens.shape[0]
    spots = window_tokens.shape[1]
    normed, rstd = layer_norm(window_tokens.reshape(-1, D).astype(jnp.float32))
    packed = jnp.dot(normed.astype(jnp.bfloat16), w_qkv, preferred_element_type=jnp.float32).astype(jnp.bfloat16)
    packed = packed.reshape(count, spots, 3, HEADS, HEAD_DIM)
    query = packed[:, :, 0]
    key = packed[:, :, 1]
    value = packed[:, :, 2]
    scale = HEAD_DIM ** (-0.5)
    scores = jnp.einsum('nqhd,nkhd->nhqk', query.astype(jnp.float32), key.astype(jnp.float32)) * scale + bias[None]
    if allow is not None:
        scores = jnp.where(allow[:, None], scores, NEG)
    top = lax.optimization_barrier(jnp.max(scores, axis=-1, keepdims=True))
    expo = jnp.exp(scores - top)
    probs = expo / lax.optimization_barrier(jnp.sum(expo, axis=-1, keepdims=True))
    weights = probs.astype(jnp.bfloat16)
    mixed = jnp.einsum('nhqk,nkhd->nqhd', weights.astype(jnp.float32), value.astype(jnp.float32)).astype(jnp.bfloat16)
    mixed = mixed.reshape(count * spots, HEADS * HEAD_DIM)
    return (normed, rstd, query, key, value, probs, weights, mixed)

def backward_windows(saved, grad_out, w_qkv, w_proj, grad_scale):
    normed, rstd, query, key, value, probs, weights, mixed = saved
    count = query.shape[0]
    spots = query.shape[1]
    scale = HEAD_DIM ** (-0.5)
    local = jnp.dot(mixed.T, grad_out, preferred_element_type=jnp.float32) * grad_scale
    d_mixed = jnp.dot(grad_out, w_proj.T, preferred_element_type=jnp.float32).astype(jnp.bfloat16)
    d_mixed = d_mixed.reshape(count, spots, HEADS, HEAD_DIM)
    d_probs = jnp.einsum('nqhd,nkhd->nhqk', d_mixed.astype(jnp.float32), value.astype(jnp.float32))
    d_value = jnp.einsum('nhqk,nqhd->nkhd', weights.astype(jnp.float32), d_mixed.astype(jnp.float32)).astype(jnp.bfloat16)
    d_scores = (probs * (d_probs - lax.optimization_barrier(jnp.sum(probs * d_probs, axis=-1, keepdims=True)))).astype(jnp.bfloat16)
    d_query = (jnp.einsum('nhqk,nkhd->nqhd', d_scores.astype(jnp.float32), key.astype(jnp.float32)) * scale).astype(jnp.bfloat16)
    d_key = (jnp.einsum('nhqk,nqhd->nkhd', d_scores.astype(jnp.float32), query.astype(jnp.float32)) * scale).astype(jnp.bfloat16)
    d_packed = jnp.stack([d_query, d_key, d_value], axis=2).reshape(count * spots, 3 * HEADS * HEAD_DIM)
    d_normed = jnp.dot(d_packed, w_qkv.T, preferred_element_type=jnp.float32)
    d_input = rstd * (d_normed - lax.optimization_barrier(jnp.mean(d_normed, axis=-1, keepdims=True)) - normed * lax.optimization_barrier(jnp.mean(d_normed * normed, axis=-1, keepdims=True)))
    return (grad_out.astype(jnp.float32) + d_input, local)

def reference(tokens, cotangent, qkv_plain, qkv_shift, proj_plain, proj_shift, table_plain, table_shift):
    index = offset_index()
    bias_plain = table_plain[:, index]
    bias_shift = table_shift[:, index]
    along_f = jnp.arange(F)
    along_t = jnp.arange(TM)
    region_f = jnp.where(along_f < F - WIN, 0, jnp.where(along_f < F - SHIFT, 1, 2))
    region_t = jnp.where(along_t < TM - WIN, 0, jnp.where(along_t < TM - SHIFT, 1, 2))
    label = to_windows((region_f[:, None] * 3 + region_t[None, :])[:, :, None])[:, :, 0]
    allow = label[:, :, None] == label[:, None, :]
    grad_scale = 1.0 / math.sqrt(TOKENS)
    count = F // WIN * (TM // WIN)

    def one_sample(totals, pair):
        grid, grid_cot = pair
        window_tokens = to_windows(grid)
        saved_plain = forward_windows(window_tokens, qkv_plain, bias_plain, None)
        block_out = window_tokens.reshape(-1, D).astype(jnp.float32) + jnp.dot(saved_plain[-1], proj_plain, preferred_element_type=jnp.float32)
        block_out = from_windows(block_out.astype(jnp.bfloat16).reshape(count, WIN * WIN, D))
        shifted = jnp.roll(block_out, (-SHIFT, -SHIFT), axis=(0, 1))
        shifted_cot = jnp.roll(grid_cot, (-SHIFT, -SHIFT), axis=(0, 1))
        saved_shift = forward_windows(to_windows(shifted), qkv_shift, bias_shift, allow)
        d_shift, local_shift = backward_windows(saved_shift, to_windows(shifted_cot).reshape(-1, D), qkv_shift, proj_shift, grad_scale)
        d_shifted = from_windows(d_shift.astype(jnp.bfloat16).reshape(count, WIN * WIN, D))
        d_block = jnp.roll(d_shifted, (SHIFT, SHIFT), axis=(0, 1))
        d_tokens, local_plain = backward_windows(saved_plain, to_windows(d_block).reshape(-1, D), qkv_plain, proj_plain, grad_scale)
        grid_grad = from_windows(d_tokens.astype(jnp.bfloat16).reshape(count, WIN * WIN, D))
        return ((totals[0] + local_plain, totals[1] + local_shift), grid_grad)
    empty = jnp.zeros((HEADS * HEAD_DIM, D), jnp.float32)
    sums, grad_tokens = lax.scan(one_sample, (empty, empty), (tokens, cotangent))
    return (grad_tokens, sums[0], sums[1])
```

```python
import math

import jax
import jax.numpy as jnp
from jax import lax
from jax.sharding import PartitionSpec as P

D = 768
HEADS = 12
HEAD_DIM = 32
WIN = 8
REL = 225


NEG = -1e30
EPS = 1e-05


def from_behind(value, axis, steps):
    count = lax.axis_size(axis)
    pairs = [(source, (source + steps) % count) for source in range(count)]
    return lax.ppermute(value, axis, pairs)


def normalize(values):
    center = values - jnp.mean(values, axis=-1, keepdims=True)
    rstd = lax.rsqrt(jnp.mean(center * center, axis=-1, keepdims=True) + EPS)
    return (center * rstd, rstd)


def offset_bias(table):
    spots = jnp.arange(WIN * WIN)
    rows = spots // WIN
    cols = spots % WIN
    index = (
        (rows[:, None] - rows[None, :] + WIN - 1) * (2 * WIN - 1)
        + cols[:, None]
        - cols[None, :]
        + WIN
        - 1
    )
    onehot = (index.reshape(-1, 1) == jnp.arange(REL)[None, :]).astype(jnp.float32)
    bias = lax.dot_general(table, onehot, (((1,), (1,)), ((), ())), precision=lax.Precision.HIGHEST)
    return bias.reshape(HEADS, WIN * WIN, WIN * WIN)


def shift_mask(tile):
    spots = jnp.arange(tile * tile)
    rows = spots // tile
    cols = spots % tile
    last_freq = lax.axis_index("freq") == lax.axis_size("freq") - 1
    last_time = lax.axis_index("tm") == lax.axis_size("tm") - 1
    region_f = jnp.where(last_freq, 1 + (rows >= tile // 2).astype(jnp.int32), 0)
    region_t = jnp.where(last_time, 1 + (cols >= tile // 2).astype(jnp.int32), 0)
    label = region_f * 3 + region_t
    return label[:, None] == label[None, :]


def attend(window_tokens, w_qkv, bias, allow):
    samples = window_tokens.shape[0]
    spots = window_tokens.shape[1]
    normed, rstd = normalize(window_tokens.reshape(-1, D).astype(jnp.float32))
    packed = jnp.dot(normed.astype(jnp.bfloat16), w_qkv, preferred_element_type=jnp.float32).astype(
        jnp.bfloat16
    )
    packed = packed.reshape(samples, spots, 3, HEADS, HEAD_DIM)
    query = packed[:, :, 0]
    key = packed[:, :, 1]
    value = packed[:, :, 2]
    scale = HEAD_DIM ** (-0.5)
    scores = (
        jnp.einsum("sqhd,skhd->shqk", query, key, preferred_element_type=jnp.float32) * scale
        + bias[None]
    )
    if allow is not None:
        scores = jnp.where(allow[None, None], scores, NEG)
    top = jnp.max(scores, axis=-1, keepdims=True)
    expo = jnp.exp(scores - top)
    probs = expo / jnp.sum(expo, axis=-1, keepdims=True)
    weights = probs.astype(jnp.bfloat16)
    mixed = jnp.einsum(
        "shqk,skhd->sqhd", weights, value, preferred_element_type=jnp.float32
    ).astype(jnp.bfloat16)
    mixed = mixed.reshape(samples * spots, HEADS * HEAD_DIM)
    return (normed, rstd, query, key, value, probs, weights, mixed)


def attend_back(saved, grad_out, w_qkv, w_proj, grad_scale):
    normed, rstd, query, key, value, probs, weights, mixed = saved
    samples = query.shape[0]
    spots = query.shape[1]
    scale = HEAD_DIM ** (-0.5)
    local = (
        jnp.einsum("ti,td->id", mixed, grad_out, preferred_element_type=jnp.float32) * grad_scale
    )
    d_mixed = jnp.einsum("td,id->ti", grad_out, w_proj, preferred_element_type=jnp.float32).astype(
        jnp.bfloat16
    )
    d_mixed = d_mixed.reshape(samples, spots, HEADS, HEAD_DIM)
    d_probs = jnp.einsum("sqhd,skhd->shqk", d_mixed, value, preferred_element_type=jnp.float32)
    d_value = jnp.einsum(
        "shqk,sqhd->skhd", weights, d_mixed, preferred_element_type=jnp.float32
    ).astype(jnp.bfloat16)
    d_scores = (probs * (d_probs - jnp.sum(probs * d_probs, axis=-1, keepdims=True))).astype(
        jnp.bfloat16
    )
    d_query = (
        jnp.einsum("shqk,skhd->sqhd", d_scores, key, preferred_element_type=jnp.float32) * scale
    ).astype(jnp.bfloat16)
    d_key = (
        jnp.einsum("shqk,sqhd->skhd", d_scores, query, preferred_element_type=jnp.float32) * scale
    ).astype(jnp.bfloat16)
    d_packed = jnp.stack([d_query, d_key, d_value], axis=2).reshape(
        samples * spots, 3 * HEADS * HEAD_DIM
    )
    d_normed = jnp.einsum("tc,dc->td", d_packed, w_qkv, preferred_element_type=jnp.float32)
    d_input = rstd * (
        d_normed
        - jnp.mean(d_normed, axis=-1, keepdims=True)
        - normed * jnp.mean(d_normed * normed, axis=-1, keepdims=True)
    )
    return (grad_out.astype(jnp.float32) + d_input, local)


def to_shifted(tile_data):
    half = tile_data.shape[1] // 2
    below = from_behind(tile_data[:, :half], "freq", -1)
    rows_moved = jnp.concatenate([tile_data[:, half:], below], axis=1)
    right = from_behind(rows_moved[:, :, :half], "tm", -1)
    return jnp.concatenate([rows_moved[:, :, half:], right], axis=2)


def from_shifted(tile_data):
    half = tile_data.shape[1] // 2
    left = from_behind(tile_data[:, :, half:], "tm", 1)
    cols_moved = jnp.concatenate([left, tile_data[:, :, :half]], axis=2)
    above = from_behind(cols_moved[:, half:], "freq", 1)
    return jnp.concatenate([above, cols_moved[:, :half]], axis=1)


def tm_groups(bits):
    size = lax.axis_size("tm")
    step = {"core": 1, "y_hi": 2, "z": 8}[bits]
    count = {"core": 2, "y_hi": 4, "z": 8}[bits]
    groups = []
    for first in range(size):
        if (first // step) % count == 0:
            groups.append([first + step * i for i in range(count)])
    return groups


def swap(value, axis, groups=None):
    return lax.all_to_all(value, axis, 0, 0, axis_index_groups=groups)


def total(blocks):
    return jnp.sum(blocks.astype(jnp.float32), axis=0).astype(jnp.bfloat16)


def copies(value, count):
    return jnp.broadcast_to(value[None], (count,) + value.shape)


def gather_weights(qkv_plain, qkv_shift, proj_plain, proj_shift):
    core = lax.axis_index("tm") % 2
    mine = jnp.concatenate([qkv_plain.T, proj_plain, qkv_shift.T, proj_shift], axis=0)
    half = lax.dynamic_slice_in_dim(mine, core * (D // 2), D // 2, axis=1)
    own = swap(copies(half, 8), "freq")
    count = lax.axis_size("tm")
    other = lax.ppermute(own, "tm", [(i, i ^ 1) for i in range(count)])
    low = jnp.where(core == 0, own, other)
    high = jnp.where(core == 0, other, own)
    full = jnp.concatenate([low, high], axis=2)
    return (
        full[:, :144].reshape(1152, D).T,
        full[:, 192:336].reshape(1152, D).T,
        full[:, 144:192].reshape(384, D),
        full[:, 336:].reshape(384, D),
    )


def reduce_grads(plain, shift):
    both = jnp.stack([plain, shift]).astype(jnp.bfloat16)
    rows = both.reshape(2, 8, 2, 24, D).transpose(2, 1, 0, 3, 4)
    part = total(swap(rows, "tm", tm_groups("core")))
    part = total(swap(part, "freq"))
    part = total(swap(part.reshape(8, 6, D), "tm", tm_groups("z")))
    part = total(swap(copies(part, 4), "tm", tm_groups("y_hi")))
    part = swap(copies(part, 8), "tm", tm_groups("z")).reshape(2, 24, D)
    part = lax.all_gather(part, "tm", axis_index_groups=tm_groups("core"))
    part = part.transpose(1, 0, 2, 3).reshape(2, 48, D).astype(jnp.float32)
    return (part[0], part[1])


def shards(
    tokens, cotangent, qkv_plain, qkv_shift, proj_plain, proj_shift, table_plain, table_shift
):
    w_qkv_plain, w_qkv_shift, w_proj_plain, w_proj_shift = gather_weights(
        qkv_plain, qkv_shift, proj_plain, proj_shift
    )
    samples = tokens.shape[0]
    tile = tokens.shape[1]
    spots = tile * tile
    grad_scale = 1.0 / math.sqrt(samples * spots * lax.axis_size("tm") * lax.axis_size("freq"))
    saved_plain = attend(
        tokens.reshape(samples, spots, D), w_qkv_plain, offset_bias(table_plain), None
    )
    block_out = tokens.reshape(-1, D).astype(jnp.float32) + jnp.dot(
        saved_plain[-1], w_proj_plain, preferred_element_type=jnp.float32
    )
    block_out = block_out.astype(jnp.bfloat16).reshape(tokens.shape)
    shifted_in = to_shifted(block_out)
    shifted_cot = to_shifted(cotangent)
    saved_shift = attend(
        shifted_in.reshape(samples, spots, D),
        w_qkv_shift,
        offset_bias(table_shift),
        shift_mask(tile),
    )
    back_shift, local_shift = attend_back(
        saved_shift, shifted_cot.reshape(-1, D), w_qkv_shift, w_proj_shift, grad_scale
    )
    d_block = from_shifted(back_shift.astype(jnp.bfloat16).reshape(tokens.shape))
    back_plain, local_plain = attend_back(
        saved_plain, d_block.reshape(-1, D), w_qkv_plain, w_proj_plain, grad_scale
    )
    grad_plain, grad_shift = reduce_grads(local_plain, local_shift)
    return (back_plain.astype(jnp.bfloat16).reshape(tokens.shape), grad_plain, grad_shift)


def solution(mesh):
    placed = (
        P(None, "freq", "tm", None),
        P(None, "freq", "tm", None),
        P(None, "freq"),
        P(None, "freq"),
        P("freq", None),
        P("freq", None),
        P(),
        P(),
    )
    return jax.shard_map(
        shards,
        mesh=mesh,
        in_specs=placed,
        out_specs=(P(None, "freq", "tm", None), P("freq", None), P("freq", None)),
        check_vma=False,
    )
```

```python
import math

import jax
import jax.numpy as jnp
import numpy as np
from jax import lax
from jax.experimental import pallas as pl
from jax.experimental.pallas import tpu as pltpu
from jax.sharding import PartitionSpec as P

D = 768
HEADS = 12
HEAD_DIM = 32
WIN = 8
SPOTS = 64
REL = 225
WIDE = HEADS * HEAD_DIM
LANES = HEADS * SPOTS
HALF = D // 2
SHARE = 144
ROWS = 48

NEG = -1e30
EPS = 1e-05
SCALE = HEAD_DIM ** (-0.5)

NN = (((1,), (0,)), ((), ()))
NT = (((1,), (1,)), ((), ()))
TN = (((0,), (0,)), ((), ()))

F32 = jnp.float32
BF16 = jnp.bfloat16


def shifted_pick():
    pick = np.zeros((2 * SPOTS, 4 * 2 * SPOTS), np.float32)
    for s in range(2):
        for a in range(WIN):
            for b in range(WIN):
                window = 2 * (a >= 4) + (b >= 4)
                source = window * 128 + s * SPOTS + (a ^ 4) * WIN + (b ^ 4)
                pick[s * SPOTS + a * WIN + b, source] = 1.0
    return pick


def quadrant_pick():
    pick = np.zeros((2 * SPOTS, 2 * SPOTS), np.float32)
    for quad in range(4):
        for s in range(2):
            for a in range(4):
                for b in range(4):
                    row = quad * 32 + s * 16 + a * 4 + b
                    spot = (a + 4 * (quad // 2)) * WIN + b + 4 * (quad % 2)
                    pick[row, s * SPOTS + spot] = 1.0
    return pick


def offset_pick():
    pick = np.zeros((256, WIN * 128), np.float32)
    for d in range(WIN):
        for row in range(15):
            for b in range(WIN):
                pick[row * 15 + b - d + 7, d * 128 + row * WIN + b] = 1.0
    return pick


def dot(left, right, dims=NN):
    return lax.dot_general(left, right, dims, preferred_element_type=F32)


def normalize(values):
    center = values - jnp.mean(values, axis=-1, keepdims=True)
    rstd = lax.rsqrt(jnp.mean(center * center, axis=-1, keepdims=True) + EPS)
    return (center * rstd, rstd)


def lane(shape):
    return lax.broadcasted_iota(jnp.int32, shape, len(shape) - 1)


def head_mask():
    row = lax.broadcasted_iota(jnp.int32, (LANES, WIDE), 0)
    return jnp.where(row // SPOTS == lane((LANES, WIDE)) // HEAD_DIM, 1.0, 0.0).astype(BF16)


def expand(value, mask_ref):
    return jnp.concatenate([value] * HEADS, axis=0) * mask_ref[...]


def fold(full):
    head = lane((SPOTS, WIDE)) // HEAD_DIM
    out = jnp.zeros((SPOTS, WIDE), F32)
    for h in range(HEADS):
        out = out + jnp.where(head == h, full[h * SPOTS : (h + 1) * SPOTS], 0.0)
    return out


def softmax_down(scores):
    expo = jnp.exp(scores - jnp.max(scores, axis=0, keepdims=True))
    return expo / jnp.sum(expo, axis=0, keepdims=True)


def attention_back(query, key, value, d_mixed, probs, query_wide, mask_ref):
    weights = probs.astype(BF16)
    d_wide = expand(d_mixed, mask_ref)
    d_probs = dot(value, d_wide, NT)
    d_value = dot(weights, d_wide).astype(BF16)
    d_scores = (probs * (d_probs - jnp.sum(probs * d_probs, axis=0, keepdims=True))).astype(BF16)
    d_key = (dot(d_scores, query_wide) * SCALE).astype(BF16)
    d_query = (fold(dot(d_scores, key, TN)) * SCALE).astype(BF16)
    return (d_query, d_key, d_value)


def prepare(core_ref, tok, cot, qkv_p, qkv_s, proj_p, proj_s, quad, out_w, out_r, out_b, out_d):
    out_r[0:128] = tok[...]
    out_b[0:128] = tok[...]
    out_d[0:128] = tok[...]
    quads = dot(quad[...], cot[...]).astype(BF16)
    out_r[128:160] = quads[64:96]
    out_b[128:160] = quads[32:64]
    out_d[128:160] = quads[0:32]
    start = pl.multiple_of(core_ref[0] * HALF, 128)
    first = qkv_p[pl.ds(start, HALF), :].astype(F32).T.astype(BF16)
    third = qkv_s[pl.ds(start, HALF), :].astype(F32).T.astype(BF16)
    second = proj_p[:, pl.ds(start, HALF)]
    fourth = proj_s[:, pl.ds(start, HALF)]
    for i in range(8):
        out_w[i, 0:144] = first
        out_w[i, 144:192] = second
        out_w[i, 192:336] = third
        out_w[i, 336:384] = fourth


def biases(edge_ref, tables, pick, out_p, out_q, out_s, wide):
    values = tables[...]
    high = values.astype(BF16)
    rest = values - high.astype(F32)
    middle = rest.astype(BF16)
    low = (rest - middle.astype(F32)).astype(BF16)
    ones = pick[...]
    spread = (dot(high, ones) + dot(middle, ones)) + dot(low, ones)
    for row in range(2 * HEADS):
        for d in range(WIN):
            wide[row * WIN + d : row * WIN + d + 1] = spread[row : row + 1, d * 128 : (d + 1) * 128]
    left = lane((WIN, 128)) < SPOTS
    for c in range(WIN):
        move = (7 - c) * WIN
        for pair in range(HEADS // 2):
            for t, out in ((0, out_p), (1, out_s)):
                even = (t * HEADS + 2 * pair) * WIN
                first = pltpu.roll(wide[even : even + WIN], (128 - move) % 128, 1)
                second = pltpu.roll(wide[even + WIN : even + 2 * WIN], (SPOTS - move) % 128, 1)
                out[c * WIN : (c + 1) * WIN, pair * 128 : (pair + 1) * 128] = jnp.where(left, first, second)
    at = lane((SPOTS, LANES))
    plain = out_p[...]
    turned = jnp.where((at & 4) != 0, pltpu.roll(plain, 4, 1), pltpu.roll(plain, LANES - 4, 1))
    turned = jnp.where((at & 32) != 0, pltpu.roll(turned, 32, 1), pltpu.roll(turned, LANES - 32, 1))
    out_q[...] = turned
    key_at = lax.broadcasted_iota(jnp.int32, (SPOTS, LANES), 0)
    cross = at ^ key_at
    barred = (cross & 32) * edge_ref[0] + (cross & 4) * edge_ref[1]
    out_s[...] = jnp.where(barred != 0, NEG, out_s[...])


def project(rows_ref, w_mine, w_other, mine, other):
    return dot(rows_ref[:, pl.ds(mine, HALF)], w_mine, NT) + dot(
        rows_ref[:, pl.ds(other, HALF)], w_other, NT
    )


def sides(core_ref):
    mine = pl.multiple_of(core_ref[0] * HALF, 128)
    return (mine, pl.multiple_of(HALF - mine, 128))


def qkv_of(block):
    return block[:, 0:SHARE].reshape(3 * WIDE, HALF)


def proj_of(block):
    return block[:, SHARE : SHARE + ROWS].reshape(WIDE, HALF)


def input_grad(grad, normed, rstd, d_packed, w_mine, w_other, mine, other, sums):
    sums[:, pl.ds(mine, HALF)] = dot(d_packed, w_mine)
    sums[:, pl.ds(other, HALF)] = dot(d_packed, w_other)
    d_normed = sums[...]
    d_input = rstd * (
        d_normed
        - jnp.mean(d_normed, axis=-1, keepdims=True)
        - normed * jnp.mean(d_normed * normed, axis=-1, keepdims=True)
    )
    return (grad + d_input).astype(BF16)


def main_kernel(
    grad_scale,
    core_ref,
    tok,
    cot,
    right,
    below,
    diag,
    wp_mine,
    wp_other,
    ws_mine,
    ws_other,
    bias_q,
    bias_s,
    pick,
    pick_quad,
    quad,
    out_grad,
    out_local,
    rows,
    rows_small,
    grads,
    sums,
    mask,
):
    mine, other = sides(core_ref)
    mask[...] = head_mask()
    sources = (tok, right, below, diag)
    for w, source in enumerate(sources):
        for s in range(2):
            normed, _ = normalize(source[s * SPOTS : (s + 1) * SPOTS].astype(F32))
            rows[s * 256 + w * SPOTS : s * 256 + (w + 1) * SPOTS] = normed.astype(BF16)
    shifted = dot(pick[:, 0:128], tok[...])
    cot_in = dot(pick[:, 0:128], cot[...])
    for w in range(1, 4):
        shifted = shifted + dot(pick[:, w * 128 : (w + 1) * 128], sources[w][0:128])
        cot_in = cot_in + dot(pick_quad[:, (w - 1) * 32 : w * 32], sources[w][128:160])
    grads[...] = cot_in.astype(BF16)
    normed, _ = normalize(shifted)
    rows_small[...] = normed.astype(BF16)
    w_mine, w_other = qkv_of(wp_mine[...]), qkv_of(wp_other[...])
    query = project(rows_small, w_mine[:WIDE], w_other[:WIDE], mine, other).astype(BF16)
    key_value = project(rows, w_mine[WIDE:], w_other[WIDE:], mine, other).astype(BF16)
    at = lane((SPOTS, LANES))
    lower = (at & 32) != 0
    later = (at & 4) != 0
    mixed = []
    for s in range(2):
        key = key_value[s * 256 : (s + 1) * 256, :WIDE]
        value = key_value[s * 256 : (s + 1) * 256, WIDE:]
        full = dot(key, expand(query[s * SPOTS : (s + 1) * SPOTS], mask), NT)
        scores = jnp.where(
            lower,
            jnp.where(later, full[192:256], full[128:192]),
            jnp.where(later, full[64:128], full[0:64]),
        )
        probs = softmax_down(scores * SCALE + bias_q[...])
        quarters = [
            jnp.where(lower | later, 0.0, probs),
            jnp.where(lower, 0.0, jnp.where(later, probs, 0.0)),
            jnp.where(lower, jnp.where(later, 0.0, probs), 0.0),
            jnp.where(lower & later, probs, 0.0),
        ]
        wide = jnp.concatenate([q.astype(BF16) for q in quarters], axis=0)
        mixed.append(fold(dot(wide, value, TN)).astype(BF16))
    mixed_plain = jnp.concatenate(mixed, axis=0)
    sums[:, pl.ds(mine, HALF)] = dot(mixed_plain, proj_of(wp_mine[...]))
    sums[:, pl.ds(other, HALF)] = dot(mixed_plain, proj_of(wp_other[...]))
    block_out = (shifted + sums[...]).astype(BF16).astype(F32)
    normed, rstd = normalize(block_out)
    rows_small[...] = normed.astype(BF16)
    w_mine, w_other = qkv_of(ws_mine[...]), qkv_of(ws_other[...])
    packed = project(rows_small, w_mine, w_other, mine, other).astype(BF16)
    d_mixed = project(grads, proj_of(ws_mine[...]), proj_of(ws_other[...]), mine, other).astype(BF16)
    mixed, d_packed = [], []
    for s in range(2):
        part = packed[s * SPOTS : (s + 1) * SPOTS]
        query, key, value = part[:, :WIDE], part[:, WIDE : 2 * WIDE], part[:, 2 * WIDE :]
        query_wide = expand(query, mask)
        probs = softmax_down(dot(key, query_wide, NT) * SCALE + bias_s[...])
        mixed.append(fold(dot(probs.astype(BF16), value, TN)).astype(BF16))
        back = attention_back(
            query, key, value, d_mixed[s * SPOTS : (s + 1) * SPOTS], probs, query_wide, mask
        )
        d_packed.append(jnp.concatenate(back, axis=1))
    mixed_shift = jnp.concatenate(mixed, axis=0)
    d_packed = jnp.concatenate(d_packed, axis=0)
    grad = input_grad(
        grads[...].astype(F32), normed, rstd, d_packed, w_mine, w_other, mine, other, sums
    )
    out_grad[...] = dot(quad[...], grad).astype(BF16)
    local_plain = (dot(mixed_plain, grad, TN) * grad_scale).astype(BF16)
    local_shift = (dot(mixed_shift, grads[...], TN) * grad_scale).astype(BF16)
    for side in range(2):
        for i in range(8):
            at_rows = slice(i * ROWS, (i + 1) * ROWS)
            at_lanes = slice(side * HALF, (side + 1) * HALF)
            out_local[side, i, 0] = local_plain[at_rows, at_lanes]
            out_local[side, i, 1] = local_shift[at_rows, at_lanes]


def plain_back(
    core_ref, tok, g_own, g_left, g_above, g_diag, wp_mine, wp_other, bias_p, pick, out, rows, grads, sums, mask
):
    mine, other = sides(core_ref)
    mask[...] = head_mask()
    normed, rstd = normalize(tok[...].astype(F32))
    rows[...] = normed.astype(BF16)
    w_mine, w_other = qkv_of(wp_mine[...]), qkv_of(wp_other[...])
    packed = project(rows, w_mine, w_other, mine, other).astype(BF16)
    gathered = (
        dot(pick[:, 0:32], g_diag[...])
        + dot(pick[:, 32:64], g_above[...])
        + dot(pick[:, 64:96], g_left[...])
        + dot(pick[:, 96:128], g_own[...])
    )
    grads[...] = gathered.astype(BF16)
    d_mixed = project(grads, proj_of(wp_mine[...]), proj_of(wp_other[...]), mine, other).astype(BF16)
    d_packed = []
    for s in range(2):
        part = packed[s * SPOTS : (s + 1) * SPOTS]
        query, key, value = part[:, :WIDE], part[:, WIDE : 2 * WIDE], part[:, 2 * WIDE :]
        query_wide = expand(query, mask)
        probs = softmax_down(dot(key, query_wide, NT) * SCALE + bias_p[...])
        back = attention_back(
            query, key, value, d_mixed[s * SPOTS : (s + 1) * SPOTS], probs, query_wide, mask
        )
        d_packed.append(jnp.concatenate(back, axis=1))
    d_packed = jnp.concatenate(d_packed, axis=0)
    out[...] = input_grad(gathered, normed, rstd, d_packed, w_mine, w_other, mine, other, sums)


VMEM = pl.BlockSpec(memory_space=pltpu.VMEM)
SMEM = pl.BlockSpec(memory_space=pltpu.SMEM)


def params():
    return pltpu.CompilerParams(vmem_limit_bytes=50 * 1024 * 1024)


def cost(flops, size):
    return pl.CostEstimate(flops=flops, bytes_accessed=size, transcendentals=0)


def tm_groups(bits):
    size = lax.axis_size("tm")
    step = {"core": 1, "y_hi": 2, "z": 8}[bits]
    count = {"core": 2, "y_hi": 4, "z": 8}[bits]
    groups = []
    for first in range(size):
        if (first // step) % count == 0:
            groups.append([first + step * i for i in range(count)])
    return groups


def swap(value, axis, groups=None):
    return lax.all_to_all(value, axis, 0, 0, axis_index_groups=groups)


def total(blocks):
    return jnp.sum(blocks.astype(F32), axis=0).astype(BF16)


def copies(value, count):
    return jnp.broadcast_to(value[None], (count,) + value.shape)


def from_offset(value, along_tm, along_freq):
    n_tm, n_freq = lax.axis_size("tm"), lax.axis_size("freq")
    pairs = []
    for t in range(n_tm):
        for f in range(n_freq):
            source = ((t + along_tm) % n_tm) * n_freq + (f + along_freq) % n_freq
            pairs.append((source, t * n_freq + f))
    return lax.ppermute(value, ("tm", "freq"), pairs)


def reduce_grads(local):
    part = total(swap(local, "tm", tm_groups("core")))
    part = total(swap(part, "freq"))
    part = total(swap(part.reshape(8, 12, HALF), "tm", tm_groups("z")))
    part = total(swap(copies(part, 4), "tm", tm_groups("y_hi")))
    part = swap(copies(part, 8), "tm", tm_groups("z")).reshape(2, ROWS, HALF)
    part = lax.all_gather(part, "tm", axis_index_groups=tm_groups("core"))
    part = jnp.concatenate([part[0], part[1]], axis=-1).astype(F32)
    return (part[0], part[1])


def shards(
    tokens, cotangent, qkv_plain, qkv_shift, proj_plain, proj_shift, table_plain, table_shift
):
    core = (lax.axis_index("tm") % 2).astype(jnp.int32).reshape(1)
    last_freq = lax.axis_index("freq") == lax.axis_size("freq") - 1
    last_time = lax.axis_index("tm") == lax.axis_size("tm") - 1
    edge = jnp.stack([last_freq, last_time]).astype(jnp.int32)
    grad_scale = 1.0 / math.sqrt(128 * lax.axis_size("tm") * lax.axis_size("freq"))
    pick = jnp.asarray(shifted_pick(), BF16)
    quad = jnp.asarray(quadrant_pick(), BF16)
    pick_quad = jnp.asarray(quadrant_pick()[32:].T, BF16)
    pick_back = jnp.asarray(quadrant_pick().T, BF16)
    tok = tokens.reshape(128, D)
    cot = cotangent.reshape(128, D)

    message = jax.ShapeDtypeStruct((160, D), BF16)
    weights, to_left, to_above, to_diag = pl.pallas_call(
        prepare,
        out_shape=(jax.ShapeDtypeStruct((8, 384, HALF), BF16), message, message, message),
        in_specs=[SMEM] + [VMEM] * 7,
        out_specs=[VMEM] * 4,
        compiler_params=params(),
        name="prepare",
    )(core, tok, cot, qkv_plain, qkv_shift, proj_plain, proj_shift, quad)

    right = from_offset(to_left, 1, 0)
    below = from_offset(to_above, 0, 1)
    diag = from_offset(to_diag, 1, 1)
    w_mine = swap(weights, "freq")
    n_tm = lax.axis_size("tm")
    w_other = lax.ppermute(w_mine, "tm", [(i, i ^ 1) for i in range(n_tm)])

    tables = jnp.concatenate([table_plain, table_shift], axis=0)
    tables = jnp.pad(tables, ((0, 8), (0, 256 - REL)))
    table = jax.ShapeDtypeStruct((SPOTS, LANES), F32)
    bias_p, bias_q, bias_s = pl.pallas_call(
        biases,
        out_shape=(table, table, table),
        in_specs=[SMEM, VMEM, VMEM],
        out_specs=[VMEM] * 3,
        scratch_shapes=[pltpu.VMEM((2 * HEADS * WIN, 128), F32)],
        compiler_params=params(),
        name="biases",
    )(edge, tables, jnp.asarray(offset_pick(), BF16))

    plain_block = pl.BlockSpec((8, 192, HALF), lambda i: (0, 0, 0))
    shift_block = pl.BlockSpec((8, 192, HALF), lambda i: (0, 1, 0))
    quads, local = pl.pallas_call(
        lambda *refs: main_kernel(grad_scale, *refs),
        grid=(1,),
        out_shape=(
            jax.ShapeDtypeStruct((128, D), BF16),
            jax.ShapeDtypeStruct((2, 8, 2, ROWS, HALF), BF16),
        ),
        in_specs=[SMEM]
        + [VMEM] * 5
        + [plain_block, plain_block, shift_block, shift_block]
        + [VMEM] * 5,
        out_specs=[VMEM] * 2,
        scratch_shapes=[
            pltpu.VMEM((512, D), BF16),
            pltpu.VMEM((128, D), BF16),
            pltpu.VMEM((128, D), BF16),
            pltpu.VMEM((128, D), F32),
            pltpu.VMEM((LANES, WIDE), BF16),
        ],
        compiler_params=params(),
        cost_estimate=cost(4_000_000_000, 6_000_000),
        name="main",
    )(
        core, tok, cot, right, below, diag,
        w_mine, w_other, w_mine, w_other, bias_q, bias_s, pick, pick_quad, quad,
    )

    left = from_offset(quads[32:64], -1, 0)
    above = from_offset(quads[64:96], 0, -1)
    corner = from_offset(quads[96:128], -1, -1)
    grad_tokens = pl.pallas_call(
        plain_back,
        grid=(1,),
        out_shape=jax.ShapeDtypeStruct((128, D), BF16),
        in_specs=[SMEM] + [VMEM] * 5 + [plain_block, plain_block] + [VMEM] * 2,
        out_specs=VMEM,
        scratch_shapes=[
            pltpu.VMEM((128, D), BF16),
            pltpu.VMEM((128, D), BF16),
            pltpu.VMEM((128, D), F32),
            pltpu.VMEM((LANES, WIDE), BF16),
        ],
        compiler_params=params(),
        cost_estimate=cost(4_000_000_000, 4_000_000),
        name="plain_back",
    )(core, tok, quads[0:32], left, above, corner, w_mine, w_other, bias_p, pick_back)
    grad_plain, grad_shift = reduce_grads(local)
    return (grad_tokens.reshape(tokens.shape), grad_plain, grad_shift)


def solution(mesh):
    placed = (
        P(None, "freq", "tm", None),
        P(None, "freq", "tm", None),
        P(None, "freq"),
        P(None, "freq"),
        P("freq", None),
        P("freq", None),
        P(),
        P(),
    )
    return jax.shard_map(
        shards,
        mesh=mesh,
        in_specs=placed,
        out_specs=(P(None, "freq", "tm", None), P("freq", None), P("freq", None)),
        check_vma=False,
    )
```

```python
import math

import jax
import jax.numpy as jnp
import numpy as np
from jax import lax
from jax.experimental import pallas as pl
from jax.experimental.pallas import tpu as pltpu
from jax.sharding import PartitionSpec as P

D = 768
HEADS = 12
HEAD_DIM = 32
WIN = 8
SPOTS = 64
REL = 225
WIDE = HEADS * HEAD_DIM
LANES = HEADS * SPOTS
HALF = D // 2
SHARE = 144
ROWS = 48

NEG = -1e30
EPS = 1e-05
SCALE = HEAD_DIM ** (-0.5)

NN = (((1,), (0,)), ((), ()))
NT = (((1,), (1,)), ((), ()))
TN = (((0,), (0,)), ((), ()))

F32 = jnp.float32
BF16 = jnp.bfloat16


def shifted_pick():
    pick = np.zeros((2 * SPOTS, 4 * 2 * SPOTS), np.float32)
    for s in range(2):
        for a in range(WIN):
            for b in range(WIN):
                window = 2 * (a >= 4) + (b >= 4)
                source = window * 128 + s * SPOTS + (a ^ 4) * WIN + (b ^ 4)
                pick[s * SPOTS + a * WIN + b, source] = 1.0
    return pick


def quadrant_pick():
    pick = np.zeros((2 * SPOTS, 2 * SPOTS), np.float32)
    for quad in range(4):
        for s in range(2):
            for a in range(4):
                for b in range(4):
                    row = quad * 32 + s * 16 + a * 4 + b
                    spot = (a + 4 * (quad // 2)) * WIN + b + 4 * (quad % 2)
                    pick[row, s * SPOTS + spot] = 1.0
    return pick


def offset_pick():
    pick = np.zeros((256, WIN * 128), np.float32)
    for d in range(WIN):
        for row in range(15):
            for b in range(WIN):
                pick[row * 15 + b - d + 7, d * 128 + row * WIN + b] = 1.0
    return pick


def dot(left, right, dims=NN):
    return lax.dot_general(left, right, dims, preferred_element_type=F32)


def normalize(values):
    center = values - jnp.mean(values, axis=-1, keepdims=True)
    rstd = lax.rsqrt(jnp.mean(center * center, axis=-1, keepdims=True) + EPS)
    return (center * rstd, rstd)


def lane(shape):
    return lax.broadcasted_iota(jnp.int32, shape, len(shape) - 1)


def head_mask():
    row = lax.broadcasted_iota(jnp.int32, (LANES, WIDE), 0)
    return jnp.where(row // SPOTS == lane((LANES, WIDE)) // HEAD_DIM, 1.0, 0.0).astype(BF16)


def expand(value, mask_ref):
    return jnp.concatenate([value] * HEADS, axis=0) * mask_ref[...]


def fold(full):
    head = lane((SPOTS, WIDE)) // HEAD_DIM
    out = jnp.zeros((SPOTS, WIDE), F32)
    for h in range(HEADS):
        out = out + jnp.where(head == h, full[h * SPOTS : (h + 1) * SPOTS], 0.0)
    return out


def softmax_down(scores):
    expo = jnp.exp(scores - jnp.max(scores, axis=0, keepdims=True))
    return expo / jnp.sum(expo, axis=0, keepdims=True)


def attention_back(query, key, value, d_mixed, probs, query_wide, mask_ref):
    weights = probs.astype(BF16)
    d_wide = expand(d_mixed, mask_ref)
    d_probs = dot(value, d_wide, NT)
    d_value = dot(weights, d_wide).astype(BF16)
    d_scores = (probs * (d_probs - jnp.sum(probs * d_probs, axis=0, keepdims=True))).astype(BF16)
    d_key = (dot(d_scores, query_wide) * SCALE).astype(BF16)
    d_query = (fold(dot(d_scores, key, TN)) * SCALE).astype(BF16)
    return (d_query, d_key, d_value)


def prepare(core_ref, tok, cot, qkv_p, qkv_s, proj_p, proj_s, quad, out_w, out_r, out_b, out_d, block, sems):
    start = pl.multiple_of(core_ref[0] * HALF, 128)
    block[0:144] = qkv_p[:, pl.ds(start, HALF)]
    block[144:192] = proj_p[:, pl.ds(start, HALF)]
    block[192:336] = qkv_s[:, pl.ds(start, HALF)]
    block[336:384] = proj_s[:, pl.ds(start, HALF)]
    sends = [pltpu.make_async_copy(block, out_w.at[i], sems.at[i]) for i in range(8)]
    for send in sends:
        send.start()
    quads = dot(quad[...], cot[...]).astype(BF16)
    for out, first in ((out_r, 64), (out_b, 32), (out_d, 0)):
        out[0:128] = tok[...]
        out[128:160] = quads[first : first + 32]
    for send in sends:
        send.wait()


def biases(edge_ref, tables, pick, out_p, out_q, out_s, wide):
    values = tables[...]
    high = values.astype(BF16)
    rest = values - high.astype(F32)
    middle = rest.astype(BF16)
    low = (rest - middle.astype(F32)).astype(BF16)
    ones = pick[...]
    spread = (dot(high, ones) + dot(middle, ones)) + dot(low, ones)
    for row in range(2 * HEADS):
        for d in range(WIN):
            wide[row * WIN + d : row * WIN + d + 1] = spread[row : row + 1, d * 128 : (d + 1) * 128]
    left = lane((WIN, 128)) < SPOTS
    for c in range(WIN):
        move = (7 - c) * WIN
        for pair in range(HEADS // 2):
            for t, out in ((0, out_p), (1, out_s)):
                even = (t * HEADS + 2 * pair) * WIN
                first = pltpu.roll(wide[even : even + WIN], (128 - move) % 128, 1)
                second = pltpu.roll(wide[even + WIN : even + 2 * WIN], (SPOTS - move) % 128, 1)
                out[c * WIN : (c + 1) * WIN, pair * 128 : (pair + 1) * 128] = jnp.where(left, first, second)
    at = lane((SPOTS, LANES))
    plain = out_p[...]
    turned = jnp.where((at & 4) != 0, pltpu.roll(plain, 4, 1), pltpu.roll(plain, LANES - 4, 1))
    turned = jnp.where((at & 32) != 0, pltpu.roll(turned, 32, 1), pltpu.roll(turned, LANES - 32, 1))
    out_q[...] = turned
    key_at = lax.broadcasted_iota(jnp.int32, (SPOTS, LANES), 0)
    cross = at ^ key_at
    barred = (cross & 32) * edge_ref[0] + (cross & 4) * edge_ref[1]
    out_s[...] = jnp.where(barred != 0, NEG, out_s[...])


def project(rows_ref, w_mine, w_other, mine, other):
    return dot(rows_ref[:, pl.ds(mine, HALF)], w_mine, NT) + dot(
        rows_ref[:, pl.ds(other, HALF)], w_other, NT
    )


def sides(core_ref):
    mine = pl.multiple_of(core_ref[0] * HALF, 128)
    return (mine, pl.multiple_of(HALF - mine, 128))


def qkv_of(ref, first):
    return ref[:, first : first + SHARE].reshape(3 * WIDE, HALF)


def proj_of(ref, first):
    return ref[:, first + SHARE : first + SHARE + ROWS].reshape(WIDE, HALF)


def input_grad(grad, normed, rstd, d_packed, w_mine, w_other, mine, other, sums):
    sums[:, pl.ds(mine, HALF)] = dot(d_packed, w_mine)
    sums[:, pl.ds(other, HALF)] = dot(d_packed, w_other)
    d_normed = sums[...]
    d_input = rstd * (
        d_normed
        - jnp.mean(d_normed, axis=-1, keepdims=True)
        - normed * jnp.mean(d_normed * normed, axis=-1, keepdims=True)
    )
    return (grad + d_input).astype(BF16)


def main_kernel(
    grad_scale,
    core_ref,
    tok,
    cot,
    right,
    below,
    diag,
    w_mine_ref,
    w_other_ref,
    bias_q,
    bias_s,
    pick,
    pick_quad,
    quad,
    out_grad,
    out_keep,
    out_send,
    rows,
    rows_small,
    grads,
    sums,
    mask,
):
    mine, other = sides(core_ref)
    mask[...] = head_mask()
    sources = (tok, right, below, diag)
    for w, source in enumerate(sources):
        for s in range(2):
            normed, _ = normalize(source[s * SPOTS : (s + 1) * SPOTS].astype(F32))
            rows[s * 256 + w * SPOTS : s * 256 + (w + 1) * SPOTS] = normed.astype(BF16)
    shifted = dot(pick[:, 0:128], tok[...])
    cot_in = dot(pick[:, 0:128], cot[...])
    for w in range(1, 4):
        shifted = shifted + dot(pick[:, w * 128 : (w + 1) * 128], sources[w][0:128])
        cot_in = cot_in + dot(pick_quad[:, (w - 1) * 32 : w * 32], sources[w][128:160])
    grads[...] = cot_in.astype(BF16)
    normed, _ = normalize(shifted)
    rows_small[...] = normed.astype(BF16)
    w_mine, w_other = qkv_of(w_mine_ref, 0), qkv_of(w_other_ref, 0)
    query = project(rows_small, w_mine[:WIDE], w_other[:WIDE], mine, other).astype(BF16)
    key_value = project(rows, w_mine[WIDE:], w_other[WIDE:], mine, other).astype(BF16)
    at = lane((SPOTS, LANES))
    lower = (at & 32) != 0
    later = (at & 4) != 0
    mixed = []
    for s in range(2):
        key = key_value[s * 256 : (s + 1) * 256, :WIDE]
        value = key_value[s * 256 : (s + 1) * 256, WIDE:]
        full = dot(key, expand(query[s * SPOTS : (s + 1) * SPOTS], mask), NT)
        scores = jnp.where(
            lower,
            jnp.where(later, full[192:256], full[128:192]),
            jnp.where(later, full[64:128], full[0:64]),
        )
        probs = softmax_down(scores * SCALE + bias_q[...])
        quarters = [
            jnp.where(lower | later, 0.0, probs),
            jnp.where(lower, 0.0, jnp.where(later, probs, 0.0)),
            jnp.where(lower, jnp.where(later, 0.0, probs), 0.0),
            jnp.where(lower & later, probs, 0.0),
        ]
        wide = jnp.concatenate([q.astype(BF16) for q in quarters], axis=0)
        mixed.append(fold(dot(wide, value, TN)).astype(BF16))
    mixed_plain = jnp.concatenate(mixed, axis=0)
    sums[:, pl.ds(mine, HALF)] = dot(mixed_plain, proj_of(w_mine_ref, 0))
    sums[:, pl.ds(other, HALF)] = dot(mixed_plain, proj_of(w_other_ref, 0))
    block_out = (shifted + sums[...]).astype(BF16).astype(F32)
    normed, rstd = normalize(block_out)
    rows_small[...] = normed.astype(BF16)
    w_mine, w_other = qkv_of(w_mine_ref, 192), qkv_of(w_other_ref, 192)
    packed = project(rows_small, w_mine, w_other, mine, other).astype(BF16)
    d_mixed = project(grads, proj_of(w_mine_ref, 192), proj_of(w_other_ref, 192), mine, other).astype(BF16)
    mixed, d_packed = [], []
    for s in range(2):
        part = packed[s * SPOTS : (s + 1) * SPOTS]
        query, key, value = part[:, :WIDE], part[:, WIDE : 2 * WIDE], part[:, 2 * WIDE :]
        query_wide = expand(query, mask)
        probs = softmax_down(dot(key, query_wide, NT) * SCALE + bias_s[...])
        mixed.append(fold(dot(probs.astype(BF16), value, TN)).astype(BF16))
        back = attention_back(
            query, key, value, d_mixed[s * SPOTS : (s + 1) * SPOTS], probs, query_wide, mask
        )
        d_packed.append(jnp.concatenate(back, axis=1))
    mixed_shift = jnp.concatenate(mixed, axis=0)
    d_packed = jnp.concatenate(d_packed, axis=0)
    grad = input_grad(
        grads[...].astype(F32), normed, rstd, d_packed, w_mine, w_other, mine, other, sums
    )
    out_grad[...] = dot(quad[...], grad).astype(BF16)
    rows_small[...] = grad
    for out, start in ((out_keep, mine), (out_send, other)):
        part = dot(mixed_plain, rows_small[:, pl.ds(start, HALF)], TN) * grad_scale
        out[:, 0] = part.astype(BF16).reshape(8, ROWS, HALF)
        part = dot(mixed_shift, grads[:, pl.ds(start, HALF)], TN) * grad_scale
        out[:, 1] = part.astype(BF16).reshape(8, ROWS, HALF)


def sum_copies(parts, out):
    value = jnp.sum(parts[...].astype(F32), axis=0).astype(BF16)
    for i in range(out.shape[0]):
        out[i] = value


def finish(parts, out_plain, out_shift):
    for i, out in enumerate((out_plain, out_shift)):
        out[:, 0:HALF] = parts[0, i].astype(F32)
        out[:, HALF:D] = parts[1, i].astype(F32)


def plain_back(
    core_ref, tok, g_own, g_left, g_above, g_diag, w_mine_ref, w_other_ref, bias_p, pick, out, rows, grads, sums, mask
):
    mine, other = sides(core_ref)
    mask[...] = head_mask()
    normed, rstd = normalize(tok[...].astype(F32))
    rows[...] = normed.astype(BF16)
    w_mine, w_other = qkv_of(w_mine_ref, 0), qkv_of(w_other_ref, 0)
    packed = project(rows, w_mine, w_other, mine, other).astype(BF16)
    gathered = (
        dot(pick[:, 0:32], g_diag[...])
        + dot(pick[:, 32:64], g_above[...])
        + dot(pick[:, 64:96], g_left[...])
        + dot(pick[:, 96:128], g_own[...])
    )
    grads[...] = gathered.astype(BF16)
    d_mixed = project(grads, proj_of(w_mine_ref, 0), proj_of(w_other_ref, 0), mine, other).astype(BF16)
    d_packed = []
    for s in range(2):
        part = packed[s * SPOTS : (s + 1) * SPOTS]
        query, key, value = part[:, :WIDE], part[:, WIDE : 2 * WIDE], part[:, 2 * WIDE :]
        query_wide = expand(query, mask)
        probs = softmax_down(dot(key, query_wide, NT) * SCALE + bias_p[...])
        back = attention_back(
            query, key, value, d_mixed[s * SPOTS : (s + 1) * SPOTS], probs, query_wide, mask
        )
        d_packed.append(jnp.concatenate(back, axis=1))
    d_packed = jnp.concatenate(d_packed, axis=0)
    out[...] = input_grad(gathered, normed, rstd, d_packed, w_mine, w_other, mine, other, sums)


VMEM = pl.BlockSpec(memory_space=pltpu.VMEM)
SMEM = pl.BlockSpec(memory_space=pltpu.SMEM)


def params(size=32):
    return pltpu.CompilerParams(vmem_limit_bytes=size * 1024 * 1024)


def cost(flops, size):
    return pl.CostEstimate(flops=flops, bytes_accessed=size, transcendentals=0)


def tm_groups(bits):
    size = lax.axis_size("tm")
    step = {"core": 1, "y_hi": 2, "z": 8}[bits]
    count = {"core": 2, "y_hi": 4, "z": 8}[bits]
    groups = []
    for first in range(size):
        if (first // step) % count == 0:
            groups.append([first + step * i for i in range(count)])
    return groups


def swap(value, axis, groups=None):
    return lax.all_to_all(value, axis, 0, 0, axis_index_groups=groups)


def total(blocks):
    return jnp.sum(blocks.astype(F32), axis=0).astype(BF16)


def from_offset(value, along_tm, along_freq):
    n_tm, n_freq = lax.axis_size("tm"), lax.axis_size("freq")
    pairs = []
    for t in range(n_tm):
        for f in range(n_freq):
            source = ((t + along_tm) % n_tm) * n_freq + (f + along_freq) % n_freq
            pairs.append((source, t * n_freq + f))
    return lax.ppermute(value, ("tm", "freq"), pairs)


def other_core(value):
    return lax.ppermute(value, "tm", [(i, i ^ 1) for i in range(lax.axis_size("tm"))])


def summed(parts, count):
    return pl.pallas_call(
        sum_copies,
        out_shape=jax.ShapeDtypeStruct((count,) + parts.shape[1:], BF16),
        in_specs=[VMEM],
        out_specs=VMEM,
        compiler_params=params(),
        name="sum_copies",
    )(parts)


def shards(
    tokens, cotangent, qkv_plain, qkv_shift, proj_plain, proj_shift, table_plain, table_shift
):
    core = (lax.axis_index("tm") % 2).astype(jnp.int32).reshape(1)
    last_freq = lax.axis_index("freq") == lax.axis_size("freq") - 1
    last_time = lax.axis_index("tm") == lax.axis_size("tm") - 1
    edge = jnp.stack([last_freq, last_time]).astype(jnp.int32)
    grad_scale = 1.0 / math.sqrt(128 * lax.axis_size("tm") * lax.axis_size("freq"))
    pick = jnp.asarray(shifted_pick(), BF16)
    quad = jnp.asarray(quadrant_pick(), BF16)
    pick_quad = jnp.asarray(quadrant_pick()[32:].T, BF16)
    pick_back = jnp.asarray(quadrant_pick().T, BF16)
    tok = tokens.reshape(128, D)
    cot = cotangent.reshape(128, D)

    message = jax.ShapeDtypeStruct((160, D), BF16)
    weights, to_left, to_above, to_diag = pl.pallas_call(
        prepare,
        out_shape=(jax.ShapeDtypeStruct((8, 384, HALF), BF16), message, message, message),
        in_specs=[SMEM] + [VMEM] * 7,
        out_specs=[pl.BlockSpec(memory_space=pl.ANY)] + [VMEM] * 3,
        scratch_shapes=[pltpu.VMEM((384, HALF), BF16), pltpu.SemaphoreType.DMA((8,))],
        compiler_params=params(60),
        name="prepare",
    )(core, tok, cot, qkv_plain.T, qkv_shift.T, proj_plain, proj_shift, quad)

    right = from_offset(to_left, 1, 0)
    below = from_offset(to_above, 0, 1)
    diag = from_offset(to_diag, 1, 1)
    w_mine = swap(weights, "freq")

    tables = jnp.concatenate([table_plain, table_shift], axis=0)
    tables = jnp.pad(tables, ((0, 8), (0, 256 - REL)))
    table = jax.ShapeDtypeStruct((SPOTS, LANES), F32)
    bias_p, bias_q, bias_s = pl.pallas_call(
        biases,
        out_shape=(table, table, table),
        in_specs=[SMEM, VMEM, VMEM],
        out_specs=[VMEM] * 3,
        scratch_shapes=[pltpu.VMEM((2 * HEADS * WIN, 128), F32)],
        compiler_params=params(),
        name="biases",
    )(edge, tables, jnp.asarray(offset_pick(), BF16))

    w_mine, right, below, diag, bias_p, bias_q, bias_s = lax.optimization_barrier(
        (w_mine, right, below, diag, bias_p, bias_q, bias_s)
    )
    w_other = other_core(w_mine)
    quads, keep, send = pl.pallas_call(
        lambda *refs: main_kernel(grad_scale, *refs),
        out_shape=(
            jax.ShapeDtypeStruct((128, D), BF16),
            jax.ShapeDtypeStruct((8, 2, ROWS, HALF), BF16),
            jax.ShapeDtypeStruct((8, 2, ROWS, HALF), BF16),
        ),
        in_specs=[SMEM] + [VMEM] * 12,
        out_specs=[VMEM] * 3,
        scratch_shapes=[
            pltpu.VMEM((512, D), BF16),
            pltpu.VMEM((128, D), BF16),
            pltpu.VMEM((128, D), BF16),
            pltpu.VMEM((128, D), F32),
            pltpu.VMEM((LANES, WIDE), BF16),
        ],
        compiler_params=params(),
        cost_estimate=cost(4_000_000_000, 6_000_000),
        name="main",
    )(
        core, tok, cot, right, below, diag,
        w_mine, w_other, bias_q, bias_s, pick, pick_quad, quad,
    )

    part = (keep.astype(F32) + other_core(send).astype(F32)).astype(BF16)
    part, quads = lax.optimization_barrier((part, quads))
    part = swap(part, "freq")
    left = from_offset(quads[32:64], -1, 0)
    above = from_offset(quads[64:96], 0, -1)
    corner = from_offset(quads[96:128], -1, -1)
    part, left, above, corner = lax.optimization_barrier((part, left, above, corner))
    part = total(part).reshape(8, 12, HALF)
    part, left, above, corner = lax.optimization_barrier((part, left, above, corner))
    part = swap(part, "tm", tm_groups("z"))
    grad_tokens = pl.pallas_call(
        plain_back,
        out_shape=jax.ShapeDtypeStruct((128, D), BF16),
        in_specs=[SMEM] + [VMEM] * 9,
        out_specs=VMEM,
        scratch_shapes=[
            pltpu.VMEM((128, D), BF16),
            pltpu.VMEM((128, D), BF16),
            pltpu.VMEM((128, D), F32),
            pltpu.VMEM((LANES, WIDE), BF16),
        ],
        compiler_params=params(),
        cost_estimate=cost(4_000_000_000, 4_000_000),
        name="plain_back",
    )(core, tok, quads[0:32], left, above, corner, w_mine, w_other, bias_p, pick_back)
    part, grad_tokens = lax.optimization_barrier((part, grad_tokens))
    part = swap(summed(part, 4), "tm", tm_groups("y_hi"))
    part = swap(summed(part, 8), "tm", tm_groups("z")).reshape(2, ROWS, HALF)
    part = lax.all_gather(part, "tm", axis_index_groups=tm_groups("core"))
    grad_plain, grad_shift = pl.pallas_call(
        finish,
        out_shape=(jax.ShapeDtypeStruct((ROWS, D), F32),) * 2,
        in_specs=[VMEM],
        out_specs=[VMEM] * 2,
        compiler_params=params(),
        name="finish",
    )(part)
    return (grad_tokens.reshape(tokens.shape), grad_plain, grad_shift)


def solution(mesh):
    placed = (
        P(None, "freq", "tm", None),
        P(None, "freq", "tm", None),
        P(None, "freq"),
        P(None, "freq"),
        P("freq", None),
        P("freq", None),
        P(),
        P(),
    )
    return jax.shard_map(
        shards,
        mesh=mesh,
        in_specs=placed,
        out_specs=(P(None, "freq", "tm", None), P("freq", None), P("freq", None)),
        check_vma=False,
    )
```

```python
import math

import jax
import jax.numpy as jnp
from jax import lax
from jax.experimental import pallas as pl
from jax.experimental.pallas import tpu as pltpu
from jax.sharding import PartitionSpec as P

D = 768
HEADS = 12
HEAD_DIM = 32
WIN = 8
SPOTS = 64
REL = 225
WIDE = HEADS * HEAD_DIM
LANES = HEADS * SPOTS
HALF = D // 2
SHARE = 144
ROWS = 48

NEG = -1e30
EPS = 1e-05
SCALE = HEAD_DIM ** (-0.5)

NN = (((1,), (0,)), ((), ()))
NT = (((1,), (1,)), ((), ()))
TN = (((0,), (0,)), ((), ()))

F32 = jnp.float32
BF16 = jnp.bfloat16


def offset_pick():
    column = lane((256, WIN * 128))
    entry = ((column >> 3) & 15) * 15 + (column & 7) - (column >> 7) + 7
    row = lax.broadcasted_iota(jnp.int32, (256, WIN * 128), 0)
    return jnp.where(row == entry, 1.0, 0.0).astype(BF16)


def dot(left, right, dims=NN):
    return lax.dot_general(left, right, dims, preferred_element_type=F32)


def normalize(values):
    center = values - jnp.mean(values, axis=-1, keepdims=True)
    rstd = lax.rsqrt(jnp.mean(center * center, axis=-1, keepdims=True) + EPS)
    return (center * rstd, rstd)


def lane(shape):
    return lax.broadcasted_iota(jnp.int32, shape, len(shape) - 1)


def quadrant_pick(transposed=False):
    row = lax.broadcasted_iota(jnp.int32, (128, 128), 1 if transposed else 0)
    column = lax.broadcasted_iota(jnp.int32, (128, 128), 0 if transposed else 1)
    high = (row & 64) >> 1
    low = (row & 32) >> 3
    spot = high + low + ((row & 12) << 1) + (row & 3) + ((row & 16) << 2)
    return jnp.where(spot == column, 1.0, 0.0).astype(BF16)


def head_mask():
    row = lax.broadcasted_iota(jnp.int32, (LANES, WIDE), 0)
    return jnp.where(row // SPOTS == lane((LANES, WIDE)) // HEAD_DIM, 1.0, 0.0).astype(BF16)


def expand(value, mask_ref):
    return jnp.concatenate([value] * HEADS, axis=0) * mask_ref[...]


def fold(full):
    head = lane((SPOTS, WIDE)) // HEAD_DIM
    out = jnp.zeros((SPOTS, WIDE), F32)
    for h in range(HEADS):
        out = out + jnp.where(head == h, full[h * SPOTS : (h + 1) * SPOTS], 0.0)
    return out


def softmax_down(scores):
    expo = jnp.exp(scores - jnp.max(scores, axis=0, keepdims=True))
    return expo / jnp.sum(expo, axis=0, keepdims=True)


def attention_back(query, key, value, d_mixed, probs, query_wide, mask_ref):
    weights = probs.astype(BF16)
    d_wide = expand(d_mixed, mask_ref)
    d_probs = dot(value, d_wide, NT)
    d_value = dot(weights, d_wide).astype(BF16)
    d_scores = (probs * (d_probs - jnp.sum(probs * d_probs, axis=0, keepdims=True))).astype(BF16)
    d_key = (dot(d_scores, query_wide) * SCALE).astype(BF16)
    d_query = (fold(dot(d_scores, key, TN)) * SCALE).astype(BF16)
    return (d_query, d_key, d_value)


def prepare(core_ref, cot, qkv_p, qkv_s, proj_p, proj_s, out_w, out_o, out_r, out_b, out_d, block, sems):
    start = pl.multiple_of(core_ref[0] * HALF, 128)
    block[0:144] = qkv_p[:, pl.ds(start, HALF)]
    block[144:192] = proj_p[:, pl.ds(start, HALF)]
    block[192:336] = qkv_s[:, pl.ds(start, HALF)]
    block[336:384] = proj_s[:, pl.ds(start, HALF)]
    sends = [pltpu.make_async_copy(block, out_w.at[i], sems.at[i]) for i in range(8)]
    for send in sends:
        send.start()
    quads = dot(quadrant_pick(), cot[...]).astype(BF16)
    for out, first in ((out_o, 96), (out_r, 64), (out_b, 32), (out_d, 0)):
        out[...] = quads[first : first + 32]
    for send in sends:
        send.wait()


def biases(edge_ref, table_p, table_s, out_p, out_s, tables, wide):
    tables[...] = jnp.zeros_like(tables)
    tables[0:HEADS, 0:REL] = table_p[...]
    tables[HEADS : 2 * HEADS, 0:REL] = table_s[...]
    values = tables[...]
    high = values.astype(BF16)
    rest = values - high.astype(F32)
    middle = rest.astype(BF16)
    low = (rest - middle.astype(F32)).astype(BF16)
    ones = offset_pick()
    spread = (dot(high, ones) + dot(middle, ones)) + dot(low, ones)
    for row in range(2 * HEADS):
        for d in range(WIN):
            wide[row * WIN + d : row * WIN + d + 1] = spread[row : row + 1, d * 128 : (d + 1) * 128]
    left = lane((WIN, 128)) < SPOTS
    for c in range(WIN):
        move = (7 - c) * WIN
        for pair in range(HEADS // 2):
            for t, out in ((0, out_p), (1, out_s)):
                even = (t * HEADS + 2 * pair) * WIN
                first = pltpu.roll(wide[even : even + WIN], (128 - move) % 128, 1)
                second = pltpu.roll(wide[even + WIN : even + 2 * WIN], (SPOTS - move) % 128, 1)
                out[c * WIN : (c + 1) * WIN, pair * 128 : (pair + 1) * 128] = jnp.where(left, first, second)
    at = lane((SPOTS, LANES))
    key_at = lax.broadcasted_iota(jnp.int32, (SPOTS, LANES), 0)
    cross = at ^ key_at
    barred = (cross & 32) * edge_ref[0] + (cross & 4) * edge_ref[1]
    out_s[...] = jnp.where(barred != 0, NEG, out_s[...])


def project(rows_ref, w_mine, w_other, mine, other):
    return dot(rows_ref[:, pl.ds(mine, HALF)], w_mine, NT) + dot(
        rows_ref[:, pl.ds(other, HALF)], w_other, NT
    )


def sides(core_ref):
    mine = pl.multiple_of(core_ref[0] * HALF, 128)
    return (mine, pl.multiple_of(HALF - mine, 128))


def qkv_of(ref, first):
    return ref[:, first : first + SHARE].reshape(3 * WIDE, HALF)


def proj_of(ref, first):
    return ref[:, first + SHARE : first + SHARE + ROWS].reshape(WIDE, HALF)


def input_grad(grad, normed, rstd, d_packed, w_mine, w_other, mine, other, sums):
    sums[:, pl.ds(mine, HALF)] = dot(d_packed, w_mine)
    sums[:, pl.ds(other, HALF)] = dot(d_packed, w_other)
    d_normed = sums[...]
    d_input = rstd * (
        d_normed
        - jnp.mean(d_normed, axis=-1, keepdims=True)
        - normed * jnp.mean(d_normed * normed, axis=-1, keepdims=True)
    )
    return (grad + d_input).astype(BF16)


def plain_forward(
    core_ref, tok, w_mine_ref, w_other_ref, bias_p, out_o, out_r, out_b, out_d, rows, sums, mask
):
    mine, other = sides(core_ref)
    mask[...] = head_mask()
    inputs = tok[...].astype(F32)
    rows[...] = normalize(inputs)[0].astype(BF16)
    w_mine, w_other = qkv_of(w_mine_ref, 0), qkv_of(w_other_ref, 0)
    packed = project(rows, w_mine, w_other, mine, other).astype(BF16)
    mixed = []
    for s in range(2):
        part = packed[s * SPOTS : (s + 1) * SPOTS]
        query, key, value = part[:, :WIDE], part[:, WIDE : 2 * WIDE], part[:, 2 * WIDE :]
        probs = softmax_down(dot(key, expand(query, mask), NT) * SCALE + bias_p[...])
        mixed.append(fold(dot(probs.astype(BF16), value, TN)).astype(BF16))
    mixed = jnp.concatenate(mixed, axis=0)
    sums[:, pl.ds(mine, HALF)] = dot(mixed, proj_of(w_mine_ref, 0))
    sums[:, pl.ds(other, HALF)] = dot(mixed, proj_of(w_other_ref, 0))
    block_out = (inputs + sums[...]).astype(BF16)
    pick = quadrant_pick()
    outs = (out_d, out_b, out_r, out_o)
    for whole, first in ((block_out, 0), (mixed, D)):
        quads = dot(pick, whole).astype(BF16)
        for i, out in enumerate(outs):
            out[:, first : first + whole.shape[1]] = quads[i * 32 : (i + 1) * 32]


def main_kernel(
    grad_scale,
    core_ref,
    cot_own,
    cot_right,
    cot_below,
    cot_diag,
    own,
    right,
    below,
    diag,
    w_mine_ref,
    w_other_ref,
    bias_s,
    out_own,
    out_right,
    out_below,
    out_diag,
    out_keep,
    out_send,
    staged,
    staged_cot,
    rows_small,
    grads,
    sums,
    mask,
):
    mine, other = sides(core_ref)
    mask[...] = head_mask()
    for i, (part, cot) in enumerate(
        ((own, cot_own), (right, cot_right), (below, cot_below), (diag, cot_diag))
    ):
        staged[i * 32 : (i + 1) * 32] = part[...]
        staged_cot[i * 32 : (i + 1) * 32] = cot[...]
    pick = quadrant_pick(True)
    grads[...] = dot(pick, staged_cot[...]).astype(BF16)
    block_out = dot(pick, staged[:, 0:D])
    mixed_plain = dot(pick, staged[:, D : D + WIDE]).astype(BF16)
    normed, rstd = normalize(block_out)
    rows_small[...] = normed.astype(BF16)
    w_mine, w_other = qkv_of(w_mine_ref, 192), qkv_of(w_other_ref, 192)
    packed = project(rows_small, w_mine, w_other, mine, other).astype(BF16)
    d_mixed = project(grads, proj_of(w_mine_ref, 192), proj_of(w_other_ref, 192), mine, other).astype(BF16)
    mixed, d_packed = [], []
    for s in range(2):
        part = packed[s * SPOTS : (s + 1) * SPOTS]
        query, key, value = part[:, :WIDE], part[:, WIDE : 2 * WIDE], part[:, 2 * WIDE :]
        query_wide = expand(query, mask)
        probs = softmax_down(dot(key, query_wide, NT) * SCALE + bias_s[...])
        mixed.append(fold(dot(probs.astype(BF16), value, TN)).astype(BF16))
        back = attention_back(
            query, key, value, d_mixed[s * SPOTS : (s + 1) * SPOTS], probs, query_wide, mask
        )
        d_packed.append(jnp.concatenate(back, axis=1))
    mixed_shift = jnp.concatenate(mixed, axis=0)
    d_packed = jnp.concatenate(d_packed, axis=0)
    grad = input_grad(
        grads[...].astype(F32), normed, rstd, d_packed, w_mine, w_other, mine, other, sums
    )
    quads = dot(quadrant_pick(), grad).astype(BF16)
    for i, out in enumerate((out_own, out_right, out_below, out_diag)):
        out[...] = quads[i * 32 : (i + 1) * 32]
    rows_small[...] = grad
    for out, start in ((out_keep, mine), (out_send, other)):
        part = dot(mixed_plain, rows_small[:, pl.ds(start, HALF)], TN) * grad_scale
        out[:, 0] = part.astype(BF16).reshape(8, ROWS, HALF)
        part = dot(mixed_shift, grads[:, pl.ds(start, HALF)], TN) * grad_scale
        out[:, 1] = part.astype(BF16).reshape(8, ROWS, HALF)


def sum_copies(parts, out):
    value = jnp.sum(parts[...].astype(F32), axis=0).astype(BF16)
    for i in range(out.shape[0]):
        out[i] = value


def finish(parts, out_plain, out_shift):
    for i, out in enumerate((out_plain, out_shift)):
        out[:, 0:HALF] = parts[0, i].astype(F32)
        out[:, HALF:D] = parts[1, i].astype(F32)


def plain_back(
    core_ref, tok, g_own, g_left, g_above, g_diag, w_mine_ref, w_other_ref, bias_p, out, staged, rows, grads, sums, mask
):
    mine, other = sides(core_ref)
    mask[...] = head_mask()
    normed, rstd = normalize(tok[...].astype(F32))
    rows[...] = normed.astype(BF16)
    w_mine, w_other = qkv_of(w_mine_ref, 0), qkv_of(w_other_ref, 0)
    packed = project(rows, w_mine, w_other, mine, other).astype(BF16)
    for i, part in enumerate((g_diag, g_above, g_left, g_own)):
        staged[i * 32 : (i + 1) * 32] = part[...]
    gathered = dot(quadrant_pick(True), staged[...])
    grads[...] = gathered.astype(BF16)
    d_mixed = project(grads, proj_of(w_mine_ref, 0), proj_of(w_other_ref, 0), mine, other).astype(BF16)
    d_packed = []
    for s in range(2):
        part = packed[s * SPOTS : (s + 1) * SPOTS]
        query, key, value = part[:, :WIDE], part[:, WIDE : 2 * WIDE], part[:, 2 * WIDE :]
        query_wide = expand(query, mask)
        probs = softmax_down(dot(key, query_wide, NT) * SCALE + bias_p[...])
        back = attention_back(
            query, key, value, d_mixed[s * SPOTS : (s + 1) * SPOTS], probs, query_wide, mask
        )
        d_packed.append(jnp.concatenate(back, axis=1))
    d_packed = jnp.concatenate(d_packed, axis=0)
    out[...] = input_grad(gathered, normed, rstd, d_packed, w_mine, w_other, mine, other, sums)


VMEM = pl.BlockSpec(memory_space=pltpu.VMEM)
SMEM = pl.BlockSpec(memory_space=pltpu.SMEM)


def params(size=32):
    return pltpu.CompilerParams(vmem_limit_bytes=size * 1024 * 1024)


def cost(flops, size):
    return pl.CostEstimate(flops=flops, bytes_accessed=size, transcendentals=0)


def tm_groups(bits):
    size = lax.axis_size("tm")
    step = {"core": 1, "y_hi": 2, "z": 8}[bits]
    count = {"core": 2, "y_hi": 4, "z": 8}[bits]
    groups = []
    for first in range(size):
        if (first // step) % count == 0:
            groups.append([first + step * i for i in range(count)])
    return groups


def swap(value, axis, groups=None):
    return lax.all_to_all(value, axis, 0, 0, axis_index_groups=groups)


def total(blocks):
    return jnp.sum(blocks.astype(F32), axis=0).astype(BF16)


def from_offset(value, along_tm, along_freq):
    n_tm, n_freq = lax.axis_size("tm"), lax.axis_size("freq")
    pairs = []
    for t in range(n_tm):
        for f in range(n_freq):
            source = ((t + along_tm) % n_tm) * n_freq + (f + along_freq) % n_freq
            pairs.append((source, t * n_freq + f))
    return lax.ppermute(value, ("tm", "freq"), pairs)


def other_core(value):
    return lax.ppermute(value, "tm", [(i, i ^ 1) for i in range(lax.axis_size("tm"))])


def summed(parts, count):
    return pl.pallas_call(
        sum_copies,
        out_shape=jax.ShapeDtypeStruct((count,) + parts.shape[1:], BF16),
        in_specs=[VMEM],
        out_specs=VMEM,
        compiler_params=params(),
        name="sum_copies",
    )(parts)


def shards(
    tokens, cotangent, qkv_plain, qkv_shift, proj_plain, proj_shift, table_plain, table_shift
):
    core = (lax.axis_index("tm") % 2).astype(jnp.int32).reshape(1)
    last_freq = lax.axis_index("freq") == lax.axis_size("freq") - 1
    last_time = lax.axis_index("tm") == lax.axis_size("tm") - 1
    edge = jnp.stack([last_freq, last_time]).astype(jnp.int32)
    grad_scale = 1.0 / math.sqrt(128 * lax.axis_size("tm") * lax.axis_size("freq"))
    tok = tokens.reshape(128, D)
    cot = cotangent.reshape(128, D)

    piece = jax.ShapeDtypeStruct((32, D), BF16)
    weights, cot_own, to_left, to_above, to_diag = pl.pallas_call(
        prepare,
        out_shape=(jax.ShapeDtypeStruct((8, 384, HALF), BF16), piece, piece, piece, piece),
        in_specs=[SMEM] + [VMEM] * 5,
        out_specs=[pl.BlockSpec(memory_space=pl.ANY)] + [VMEM] * 4,
        scratch_shapes=[pltpu.VMEM((384, HALF), BF16), pltpu.SemaphoreType.DMA((8,))],
        compiler_params=params(60),
        name="prepare",
    )(core, cot, qkv_plain.T, qkv_shift.T, proj_plain, proj_shift)

    w_mine = swap(weights, "freq")
    cot_right = from_offset(to_left, 1, 0)
    cot_below = from_offset(to_above, 0, 1)
    cot_diag = from_offset(to_diag, 1, 1)

    table = jax.ShapeDtypeStruct((SPOTS, LANES), F32)
    bias_p, bias_s = pl.pallas_call(
        biases,
        out_shape=(table, table),
        in_specs=[SMEM, VMEM, VMEM],
        out_specs=[VMEM] * 2,
        scratch_shapes=[pltpu.VMEM((32, 256), F32), pltpu.VMEM((2 * HEADS * WIN, 128), F32)],
        compiler_params=params(),
        name="biases",
    )(edge, table_plain, table_shift)

    w_mine, bias_p, bias_s, cot_right, cot_below, cot_diag = lax.optimization_barrier(
        (w_mine, bias_p, bias_s, cot_right, cot_below, cot_diag)
    )
    w_other = other_core(w_mine)
    packet = jax.ShapeDtypeStruct((32, D + WIDE), BF16)
    own, to_left, to_above, to_diag = pl.pallas_call(
        plain_forward,
        out_shape=(packet,) * 4,
        in_specs=[SMEM] + [VMEM] * 4,
        out_specs=[VMEM] * 4,
        scratch_shapes=[
            pltpu.VMEM((128, D), BF16),
            pltpu.VMEM((128, D), F32),
            pltpu.VMEM((LANES, WIDE), BF16),
        ],
        compiler_params=params(),
        cost_estimate=cost(1_000_000_000, 4_000_000),
        name="plain_forward",
    )(core, tok, w_mine, w_other, bias_p)
    right = from_offset(to_left, 1, 0)
    below = from_offset(to_above, 0, 1)
    diag = from_offset(to_diag, 1, 1)
    half = jax.ShapeDtypeStruct((8, 2, ROWS, HALF), BF16)
    g_own, to_right, to_below, to_diag, keep, send = pl.pallas_call(
        lambda *refs: main_kernel(grad_scale, *refs),
        out_shape=(piece,) * 4 + (half, half),
        in_specs=[SMEM] + [VMEM] * 11,
        out_specs=[VMEM] * 6,
        scratch_shapes=[
            pltpu.VMEM((128, D + WIDE), BF16),
            pltpu.VMEM((128, D), BF16),
            pltpu.VMEM((128, D), BF16),
            pltpu.VMEM((128, D), BF16),
            pltpu.VMEM((128, D), F32),
            pltpu.VMEM((LANES, WIDE), BF16),
        ],
        compiler_params=params(),
        cost_estimate=cost(4_000_000_000, 6_000_000),
        name="main",
    )(
        core, cot_own, cot_right, cot_below, cot_diag,
        own, right, below, diag, w_mine, w_other, bias_s,
    )

    part = (keep.astype(F32) + other_core(send).astype(F32)).astype(BF16)
    part, to_right, to_below, to_diag = lax.optimization_barrier(
        (part, to_right, to_below, to_diag)
    )
    part = swap(part, "freq")
    left = from_offset(to_right, -1, 0)
    above = from_offset(to_below, 0, -1)
    corner = from_offset(to_diag, -1, -1)
    part = swap(total(part).reshape(8, 12, HALF), "tm", tm_groups("z"))
    part, left, above, corner = lax.optimization_barrier((part, left, above, corner))
    part = swap(summed(part, 4), "tm", tm_groups("y_hi"))
    grad_tokens = pl.pallas_call(
        plain_back,
        out_shape=jax.ShapeDtypeStruct((128, D), BF16),
        in_specs=[SMEM] + [VMEM] * 8,
        out_specs=VMEM,
        scratch_shapes=[
            pltpu.VMEM((128, D), BF16),
            pltpu.VMEM((128, D), BF16),
            pltpu.VMEM((128, D), BF16),
            pltpu.VMEM((128, D), F32),
            pltpu.VMEM((LANES, WIDE), BF16),
        ],
        compiler_params=params(),
        cost_estimate=cost(4_000_000_000, 4_000_000),
        name="plain_back",
    )(core, tok, g_own, left, above, corner, w_mine, w_other, bias_p)
    part, grad_tokens = lax.optimization_barrier((part, grad_tokens))
    part = swap(summed(part, 8), "tm", tm_groups("z")).reshape(2, ROWS, HALF)
    part = lax.all_gather(part, "tm", axis_index_groups=tm_groups("core"))
    grad_plain, grad_shift = pl.pallas_call(
        finish,
        out_shape=(jax.ShapeDtypeStruct((ROWS, D), F32),) * 2,
        in_specs=[VMEM],
        out_specs=[VMEM] * 2,
        compiler_params=params(),
        name="finish",
    )(part)
    return (grad_tokens.reshape(tokens.shape), grad_plain, grad_shift)


def solution(mesh):
    placed = (
        P(None, "freq", "tm", None),
        P(None, "freq", "tm", None),
        P(None, "freq"),
        P(None, "freq"),
        P("freq", None),
        P("freq", None),
        P(),
        P(),
    )
    return jax.shard_map(
        shards,
        mesh=mesh,
        in_specs=placed,
        out_specs=(P(None, "freq", "tm", None), P("freq", None), P("freq", None)),
        check_vma=False,
    )
```

```python
import math

import jax
import jax.numpy as jnp
from jax import lax
from jax.experimental import pallas as pl
from jax.experimental.pallas import tpu as pltpu
from jax.sharding import PartitionSpec as P

D = 768
HEADS = 12
HEAD_DIM = 32
WIN = 8
SPOTS = 64
REL = 225
WIDE = HEADS * HEAD_DIM
LANES = HEADS * SPOTS
HALF = D // 2
SHARE = 144
ROWS = 48

NEG = -1e30
EPS = 1e-05
SCALE = HEAD_DIM ** (-0.5)

NN = (((1,), (0,)), ((), ()))
NT = (((1,), (1,)), ((), ()))
TN = (((0,), (0,)), ((), ()))

F32 = jnp.float32
BF16 = jnp.bfloat16


def offset_pick():
    column = lane((256, WIN * 128))
    entry = ((column >> 3) & 15) * 15 + (column & 7) - (column >> 7) + 7
    row = lax.broadcasted_iota(jnp.int32, (256, WIN * 128), 0)
    return jnp.where(row == entry, 1.0, 0.0).astype(BF16)


def dot(left, right, dims=NN):
    return lax.dot_general(left, right, dims, preferred_element_type=F32)


def normalize(values):
    center = values - jnp.mean(values, axis=-1, keepdims=True)
    rstd = lax.rsqrt(jnp.mean(center * center, axis=-1, keepdims=True) + EPS)
    return (center * rstd, rstd)


def lane(shape):
    return lax.broadcasted_iota(jnp.int32, shape, len(shape) - 1)


def quadrant_pick(transposed=False):
    row = lax.broadcasted_iota(jnp.int32, (128, 128), 1 if transposed else 0)
    column = lax.broadcasted_iota(jnp.int32, (128, 128), 0 if transposed else 1)
    high = (row & 64) >> 1
    low = (row & 32) >> 3
    spot = high + low + ((row & 12) << 1) + (row & 3) + ((row & 16) << 2)
    return jnp.where(spot == column, 1.0, 0.0).astype(BF16)


def head_mask():
    row = lax.broadcasted_iota(jnp.int32, (LANES, WIDE), 0)
    return jnp.where(row // SPOTS == lane((LANES, WIDE)) // HEAD_DIM, 1.0, 0.0).astype(BF16)


def expand(value, mask_ref):
    return jnp.concatenate([value] * HEADS, axis=0) * mask_ref[...]


def fold(full):
    head = lane((SPOTS, WIDE)) // HEAD_DIM
    out = jnp.zeros((SPOTS, WIDE), F32)
    for h in range(HEADS):
        out = out + jnp.where(head == h, full[h * SPOTS : (h + 1) * SPOTS], 0.0)
    return out


def softmax_down(scores):
    expo = jnp.exp(scores - jnp.max(scores, axis=0, keepdims=True))
    return expo / jnp.sum(expo, axis=0, keepdims=True)


def attention_back(query, key, value, d_mixed, probs, query_wide, mask_ref):
    weights = probs.astype(BF16)
    d_wide = expand(d_mixed, mask_ref)
    d_probs = dot(value, d_wide, NT)
    d_value = dot(weights, d_wide).astype(BF16)
    d_scores = (probs * (d_probs - jnp.sum(probs * d_probs, axis=0, keepdims=True))).astype(BF16)
    d_key = (dot(d_scores, query_wide) * SCALE).astype(BF16)
    d_query = (fold(dot(d_scores, key, TN)) * SCALE).astype(BF16)
    return (d_query, d_key, d_value)


def copy_all(pairs, sems, first=0):
    moves = [
        pltpu.make_async_copy(source, target, sems.at[first + i])
        for i, (source, target) in enumerate(pairs)
    ]
    for move in moves:
        move.start()
    return moves


def wait_all(moves):
    for move in moves:
        move.wait()


def prepare(core_ref, qkv, proj, out, block, sems):
    start = pl.multiple_of(core_ref[0] * HALF, 128)
    block[0:SHARE] = qkv[:, pl.ds(start, HALF)]
    block[SHARE : SHARE + ROWS] = proj[:, pl.ds(start, HALF)]
    wait_all(copy_all([(block, out.at[i]) for i in range(8)], sems))


def biases(edge_ref, table_p, table_s, to_p, to_s, out_p, out_s, tables, wide, sems):
    tables[...] = jnp.zeros_like(tables)
    tables[0:HEADS, 0:REL] = table_p[...]
    tables[HEADS : 2 * HEADS, 0:REL] = table_s[...]
    values = tables[...]
    high = values.astype(BF16)
    rest = values - high.astype(F32)
    middle = rest.astype(BF16)
    low = (rest - middle.astype(F32)).astype(BF16)
    ones = offset_pick()
    spread = (dot(high, ones) + dot(middle, ones)) + dot(low, ones)
    for row in range(2 * HEADS):
        for d in range(WIN):
            wide[row * WIN + d : row * WIN + d + 1] = spread[row : row + 1, d * 128 : (d + 1) * 128]
    left = lane((WIN, 128)) < SPOTS
    for c in range(WIN):
        move = (7 - c) * WIN
        for pair in range(HEADS // 2):
            for t, out in ((0, out_p), (1, out_s)):
                even = (t * HEADS + 2 * pair) * WIN
                first = pltpu.roll(wide[even : even + WIN], (128 - move) % 128, 1)
                second = pltpu.roll(wide[even + WIN : even + 2 * WIN], (SPOTS - move) % 128, 1)
                out[c * WIN : (c + 1) * WIN, pair * 128 : (pair + 1) * 128] = jnp.where(left, first, second)
    at = lane((SPOTS, LANES))
    key_at = lax.broadcasted_iota(jnp.int32, (SPOTS, LANES), 0)
    cross = at ^ key_at
    barred = (cross & 32) * edge_ref[0] + (cross & 4) * edge_ref[1]
    out_s[...] = jnp.where(barred != 0, NEG, out_s[...])
    wait_all(copy_all([(out_p, to_p), (out_s, to_s)], sems))


def project(rows_ref, w_mine, w_other, mine, other):
    return dot(rows_ref[:, pl.ds(mine, HALF)], w_mine, NT) + dot(
        rows_ref[:, pl.ds(other, HALF)], w_other, NT
    )


def sides(core_ref):
    mine = pl.multiple_of(core_ref[0] * HALF, 128)
    return (mine, pl.multiple_of(HALF - mine, 128))


def qkv_of(ref):
    return ref[:, 0:SHARE].reshape(3 * WIDE, HALF)


def proj_of(ref):
    return ref[:, SHARE : SHARE + ROWS].reshape(WIDE, HALF)


def input_grad(grad, normed, rstd, d_packed, w_mine, w_other, mine, other, sums):
    sums[:, pl.ds(mine, HALF)] = dot(d_packed, w_mine)
    sums[:, pl.ds(other, HALF)] = dot(d_packed, w_other)
    d_normed = sums[...]
    d_input = rstd * (
        d_normed
        - jnp.mean(d_normed, axis=-1, keepdims=True)
        - normed * jnp.mean(d_normed * normed, axis=-1, keepdims=True)
    )
    return (grad + d_input).astype(BF16)


def plain_forward(
    core_ref,
    tok_far,
    cot_far,
    bias_far,
    w_mine_ref,
    w_other_ref,
    out_o,
    out_r,
    out_b,
    out_d,
    tok,
    cot,
    bias_p,
    packets,
    rows,
    sums,
    mask,
    sems,
):
    mine, other = sides(core_ref)
    loads = copy_all([(tok_far, tok), (bias_far, bias_p), (cot_far, cot)], sems)
    mask[...] = head_mask()
    loads[0].wait()
    inputs = tok[...].astype(F32)
    rows[...] = normalize(inputs)[0].astype(BF16)
    w_mine, w_other = qkv_of(w_mine_ref), qkv_of(w_other_ref)
    packed = project(rows, w_mine, w_other, mine, other).astype(BF16)
    loads[1].wait()
    mixed = []
    for s in range(2):
        part = packed[s * SPOTS : (s + 1) * SPOTS]
        query, key, value = part[:, :WIDE], part[:, WIDE : 2 * WIDE], part[:, 2 * WIDE :]
        probs = softmax_down(dot(key, expand(query, mask), NT) * SCALE + bias_p[...])
        mixed.append(fold(dot(probs.astype(BF16), value, TN)).astype(BF16))
    mixed = jnp.concatenate(mixed, axis=0)
    sums[:, pl.ds(mine, HALF)] = dot(mixed, proj_of(w_mine_ref))
    sums[:, pl.ds(other, HALF)] = dot(mixed, proj_of(w_other_ref))
    block_out = (inputs + sums[...]).astype(BF16)
    pick = quadrant_pick()
    loads[2].wait()
    for whole, first in ((block_out, 0), (mixed, D), (cot[...], D + WIDE)):
        packets[:, first : first + whole.shape[1]] = dot(pick, whole).astype(BF16)
    outs = (out_d, out_b, out_r, out_o)
    wait_all(copy_all([(packets.at[i * 32 : (i + 1) * 32], out) for i, out in enumerate(outs)], sems, 3))


def main_kernel(
    grad_scale,
    core_ref,
    own_far,
    bias_far,
    right,
    below,
    diag,
    w_mine_ref,
    w_other_ref,
    to_own,
    to_column,
    to_below,
    to_local,
    bias_s,
    quads,
    out_local,
    staged,
    rows_small,
    grads,
    sums,
    mask,
    sems,
):
    mine, other = sides(core_ref)
    loads = copy_all([(own_far, staged.at[0:32]), (bias_far, bias_s)], sems)
    mask[...] = head_mask()
    for i, part in ((1, right), (2, below), (3, diag)):
        staged[i * 32 : (i + 1) * 32] = part[...]
    wait_all(loads)
    pick = quadrant_pick(True)
    grads[...] = dot(pick, staged[:, D + WIDE :]).astype(BF16)
    block_out = dot(pick, staged[:, 0:D])
    mixed_plain = dot(pick, staged[:, D : D + WIDE]).astype(BF16)
    normed, rstd = normalize(block_out)
    rows_small[...] = normed.astype(BF16)
    w_mine, w_other = qkv_of(w_mine_ref), qkv_of(w_other_ref)
    packed = project(rows_small, w_mine, w_other, mine, other).astype(BF16)
    d_mixed = project(grads, proj_of(w_mine_ref), proj_of(w_other_ref), mine, other).astype(BF16)
    mixed, d_packed = [], []
    for s in range(2):
        part = packed[s * SPOTS : (s + 1) * SPOTS]
        query, key, value = part[:, :WIDE], part[:, WIDE : 2 * WIDE], part[:, 2 * WIDE :]
        query_wide = expand(query, mask)
        probs = softmax_down(dot(key, query_wide, NT) * SCALE + bias_s[...])
        mixed.append(fold(dot(probs.astype(BF16), value, TN)).astype(BF16))
        back = attention_back(
            query, key, value, d_mixed[s * SPOTS : (s + 1) * SPOTS], probs, query_wide, mask
        )
        d_packed.append(jnp.concatenate(back, axis=1))
    mixed_shift = jnp.concatenate(mixed, axis=0)
    d_packed = jnp.concatenate(d_packed, axis=0)
    grad = input_grad(
        grads[...].astype(F32), normed, rstd, d_packed, w_mine, w_other, mine, other, sums
    )
    quads[...] = dot(quadrant_pick(), grad).astype(BF16)
    stores = copy_all(
        [
            (quads.at[0:32], to_own),
            (quads.at[32:64], to_column.at[0:32]),
            (quads.at[96:128], to_column.at[32:64]),
            (quads.at[64:96], to_below),
        ],
        sems,
        2,
    )
    local_shift = dot(mixed_shift, grads[...], TN) * grad_scale
    out_local[:, 1] = local_shift.astype(BF16).reshape(8, ROWS, D)
    local_plain = dot(mixed_plain, grad, TN) * grad_scale
    out_local[:, 0] = local_plain.astype(BF16).reshape(8, ROWS, D)
    wait_all(copy_all([(out_local, to_local)], sems, 6))
    wait_all(stores)


def sum_split(core_ref, parts, out_keep, out_send, total):
    mine, other = sides(core_ref)
    total[...] = jnp.sum(parts[...].astype(F32), axis=0)
    out_keep[...] = total[:, :, pl.ds(mine, HALF)]
    out_send[...] = total[:, :, pl.ds(other, HALF)].astype(BF16)


def pair_copies(keep, arrived, out):
    value = (keep[...] + arrived[...].astype(F32)).astype(BF16)
    for i in range(out.shape[0]):
        out[i] = value


def sum_copies(parts, out):
    value = jnp.sum(parts[...].astype(F32), axis=0).astype(BF16)
    for i in range(out.shape[0]):
        out[i] = value


def finish(parts, out_plain, out_shift):
    for i, out in enumerate((out_plain, out_shift)):
        out[:, 0:HALF] = parts[0, i].astype(F32)
        out[:, HALF:D] = parts[1, i].astype(F32)


def plain_back(
    core_ref,
    tok_far,
    own_far,
    bias_far,
    mine_far,
    other_far,
    column,
    row,
    out,
    tok,
    bias_p,
    w_mine_ref,
    w_other_ref,
    staged,
    rows,
    grads,
    sums,
    mask,
    sems,
):
    mine, other = sides(core_ref)
    loads = copy_all(
        [
            (tok_far, tok),
            (mine_far, w_mine_ref),
            (other_far, w_other_ref),
            (own_far, staged.at[96:128]),
            (bias_far, bias_p),
        ],
        sems,
    )
    mask[...] = head_mask()
    staged[0:32] = row[32:64]
    staged[32:64] = row[0:32]
    staged[64:96] = column[0:32]
    loads[0].wait()
    normed, rstd = normalize(tok[...].astype(F32))
    rows[...] = normed.astype(BF16)
    wait_all(loads[1:])
    w_mine, w_other = qkv_of(w_mine_ref), qkv_of(w_other_ref)
    packed = project(rows, w_mine, w_other, mine, other).astype(BF16)
    gathered = dot(quadrant_pick(True), staged[...])
    grads[...] = gathered.astype(BF16)
    d_mixed = project(grads, proj_of(w_mine_ref), proj_of(w_other_ref), mine, other).astype(BF16)
    d_packed = []
    for s in range(2):
        part = packed[s * SPOTS : (s + 1) * SPOTS]
        query, key, value = part[:, :WIDE], part[:, WIDE : 2 * WIDE], part[:, 2 * WIDE :]
        query_wide = expand(query, mask)
        probs = softmax_down(dot(key, query_wide, NT) * SCALE + bias_p[...])
        back = attention_back(
            query, key, value, d_mixed[s * SPOTS : (s + 1) * SPOTS], probs, query_wide, mask
        )
        d_packed.append(jnp.concatenate(back, axis=1))
    d_packed = jnp.concatenate(d_packed, axis=0)
    out[...] = input_grad(gathered, normed, rstd, d_packed, w_mine, w_other, mine, other, sums)


VMEM = pl.BlockSpec(memory_space=pltpu.VMEM)
SMEM = pl.BlockSpec(memory_space=pltpu.SMEM)
HBM = pl.BlockSpec(memory_space=pltpu.HBM)


def params(size=32):
    return pltpu.CompilerParams(vmem_limit_bytes=size * 1024 * 1024)


def far(value):
    return pltpu.with_memory_space_constraint(value, pltpu.HBM)


def cost(flops, size):
    return pl.CostEstimate(flops=flops, bytes_accessed=size, transcendentals=0)


def tm_groups(bits):
    size = lax.axis_size("tm")
    step = {"core": 1, "y_hi": 2, "z": 8}[bits]
    count = {"core": 2, "y_hi": 4, "z": 8}[bits]
    groups = []
    for first in range(size):
        if (first // step) % count == 0:
            groups.append([first + step * i for i in range(count)])
    return groups


def swap(value, axis, groups=None):
    return lax.all_to_all(value, axis, 0, 0, axis_index_groups=groups)


def from_offset(value, along_tm, along_freq):
    n_tm, n_freq = lax.axis_size("tm"), lax.axis_size("freq")
    pairs = []
    for t in range(n_tm):
        for f in range(n_freq):
            source = ((t + along_tm) % n_tm) * n_freq + (f + along_freq) % n_freq
            pairs.append((source, t * n_freq + f))
    return lax.ppermute(value, ("tm", "freq"), pairs)


def other_core(value):
    return lax.ppermute(value, "tm", [(i, i ^ 1) for i in range(lax.axis_size("tm"))])


def summed(parts, count):
    return pl.pallas_call(
        sum_copies,
        out_shape=jax.ShapeDtypeStruct((count,) + parts.shape[1:], BF16),
        in_specs=[VMEM],
        out_specs=VMEM,
        compiler_params=params(),
        name="sum_copies",
    )(parts)


def shards(
    tokens, cotangent, qkv_plain, qkv_shift, proj_plain, proj_shift, table_plain, table_shift
):
    core = (lax.axis_index("tm") % 2).astype(jnp.int32).reshape(1)
    last_freq = lax.axis_index("freq") == lax.axis_size("freq") - 1
    last_time = lax.axis_index("tm") == lax.axis_size("tm") - 1
    edge = jnp.stack([last_freq, last_time]).astype(jnp.int32)
    grad_scale = 1.0 / math.sqrt(128 * lax.axis_size("tm") * lax.axis_size("freq"))
    tok = tokens.reshape(128, D)
    cot = cotangent.reshape(128, D)

    def share(qkv, proj):
        return pl.pallas_call(
            prepare,
            out_shape=pltpu.HBM((8, SHARE + ROWS, HALF), BF16),
            in_specs=[SMEM, VMEM, VMEM],
            out_specs=HBM,
            scratch_shapes=[
                pltpu.VMEM((SHARE + ROWS, HALF), BF16),
                pltpu.SemaphoreType.DMA((8,)),
            ],
            compiler_params=params(60),
            name="prepare",
        )(core, qkv.T, proj)

    first_mine = swap(share(qkv_plain, proj_plain), "freq")
    second_share = share(qkv_shift, proj_shift)
    table = pltpu.HBM((SPOTS, LANES), F32)
    bias_p, bias_s = pl.pallas_call(
        biases,
        out_shape=(table, table),
        in_specs=[SMEM, VMEM, VMEM],
        out_specs=[HBM] * 2,
        scratch_shapes=[
            pltpu.VMEM((SPOTS, LANES), F32),
            pltpu.VMEM((SPOTS, LANES), F32),
            pltpu.VMEM((32, 256), F32),
            pltpu.VMEM((2 * HEADS * WIN, 128), F32),
            pltpu.SemaphoreType.DMA((2,)),
        ],
        compiler_params=params(),
        name="biases",
    )(edge, table_plain, table_shift)

    first_mine, second_share, bias_p, bias_s = lax.optimization_barrier(
        (first_mine, second_share, bias_p, bias_s)
    )
    second_mine = swap(second_share, "freq")
    first_other = other_core(first_mine)
    packet = pltpu.HBM((32, 2 * D + WIDE), BF16)
    own, to_left, to_above, to_diag = pl.pallas_call(
        plain_forward,
        out_shape=(packet,) * 4,
        in_specs=[SMEM] + [HBM] * 3 + [VMEM] * 2,
        out_specs=[HBM] * 4,
        scratch_shapes=[
            pltpu.VMEM((128, D), BF16),
            pltpu.VMEM((128, D), BF16),
            pltpu.VMEM((SPOTS, LANES), F32),
            pltpu.VMEM((128, 2 * D + WIDE), BF16),
            pltpu.VMEM((128, D), BF16),
            pltpu.VMEM((128, D), F32),
            pltpu.VMEM((LANES, WIDE), BF16),
            pltpu.SemaphoreType.DMA((7,)),
        ],
        compiler_params=params(),
        cost_estimate=cost(1_000_000, 1_000_000),
        name="plain_forward",
    )(core, far(tok), far(cot), far(bias_p), first_mine, first_other)
    right = from_offset(to_left, 1, 0)
    below = from_offset(to_above, 0, 1)
    diag = from_offset(to_diag, 1, 1)
    second_mine, right, below, diag = lax.optimization_barrier(
        (second_mine, right, below, diag)
    )
    second_other = other_core(second_mine)
    piece = pltpu.HBM((32, D), BF16)
    column = pltpu.HBM((64, D), BF16)
    local = pltpu.HBM((8, 2, ROWS, D), BF16)
    g_own, to_right, to_below, local = pl.pallas_call(
        lambda *refs: main_kernel(grad_scale, *refs),
        out_shape=(piece, column, piece, local),
        in_specs=[SMEM] + [HBM] * 2 + [VMEM] * 5,
        out_specs=[HBM] * 4,
        scratch_shapes=[
            pltpu.VMEM((SPOTS, LANES), F32),
            pltpu.VMEM((128, D), BF16),
            pltpu.VMEM((8, 2, ROWS, D), BF16),
            pltpu.VMEM((128, 2 * D + WIDE), BF16),
            pltpu.VMEM((128, D), BF16),
            pltpu.VMEM((128, D), BF16),
            pltpu.VMEM((128, D), F32),
            pltpu.VMEM((LANES, WIDE), BF16),
            pltpu.SemaphoreType.DMA((7,)),
        ],
        compiler_params=params(),
        cost_estimate=cost(1_000_000, 1_000_000),
        name="main",
    )(core, far(own), far(bias_s), right, below, diag, second_mine, second_other)

    local, to_right, to_below = lax.optimization_barrier((local, to_right, to_below))
    part = swap(local, "freq")
    column = from_offset(to_right, -1, 0)
    half = (2, ROWS, HALF)
    keep, send = pl.pallas_call(
        sum_split,
        out_shape=(jax.ShapeDtypeStruct(half, F32), jax.ShapeDtypeStruct(half, BF16)),
        in_specs=[SMEM, VMEM],
        out_specs=[VMEM] * 2,
        scratch_shapes=[pltpu.VMEM((2, ROWS, D), F32)],
        compiler_params=params(),
        name="sum_split",
    )(core, part)
    part = pl.pallas_call(
        pair_copies,
        out_shape=jax.ShapeDtypeStruct((8,) + half, BF16),
        in_specs=[VMEM] * 2,
        out_specs=VMEM,
        compiler_params=params(),
        name="pair_copies",
    )(keep, other_core(send))
    part, column, to_below = lax.optimization_barrier((part, column, to_below))
    part = swap(part, "tm", tm_groups("z"))
    row = from_offset(jnp.concatenate([to_below, column[32:64]], axis=0), 0, -1)
    part, row = lax.optimization_barrier((part, row))
    part = swap(summed(part, 4), "tm", tm_groups("y_hi"))
    grad_tokens = pl.pallas_call(
        plain_back,
        out_shape=jax.ShapeDtypeStruct((128, D), BF16),
        in_specs=[SMEM] + [HBM] * 5 + [VMEM] * 2,
        out_specs=VMEM,
        scratch_shapes=[
            pltpu.VMEM((128, D), BF16),
            pltpu.VMEM((SPOTS, LANES), F32),
            pltpu.VMEM((8, SHARE + ROWS, HALF), BF16),
            pltpu.VMEM((8, SHARE + ROWS, HALF), BF16),
            pltpu.VMEM((128, D), BF16),
            pltpu.VMEM((128, D), BF16),
            pltpu.VMEM((128, D), BF16),
            pltpu.VMEM((128, D), F32),
            pltpu.VMEM((LANES, WIDE), BF16),
            pltpu.SemaphoreType.DMA((5,)),
        ],
        compiler_params=params(),
        cost_estimate=cost(4_000_000_000, 4_000_000),
        name="plain_back",
    )(core, far(tok), far(g_own), far(bias_p), far(first_mine), far(first_other), column, row)
    part, grad_tokens = lax.optimization_barrier((part, grad_tokens))
    part = summed(part, 1)[0]
    part = lax.all_gather(part, "tm", axis_index_groups=tm_groups("core"))
    grad_plain, grad_shift = pl.pallas_call(
        finish,
        out_shape=(jax.ShapeDtypeStruct((ROWS, D), F32),) * 2,
        in_specs=[VMEM],
        out_specs=[VMEM] * 2,
        compiler_params=params(),
        name="finish",
    )(part)
    return (grad_tokens.reshape(tokens.shape), grad_plain, grad_shift)


def solution(mesh):
    placed = (
        P(None, "freq", "tm", None),
        P(None, "freq", "tm", None),
        P(None, "freq"),
        P(None, "freq"),
        P("freq", None),
        P("freq", None),
        P(),
        P(),
    )
    return jax.shard_map(
        shards,
        mesh=mesh,
        in_specs=placed,
        out_specs=(P(None, "freq", "tm", None), P("freq", None), P("freq", None)),
        check_vma=False,
    )
```

```python
import math

import jax
import jax.numpy as jnp
from jax import lax
from jax.experimental import pallas as pl
from jax.experimental.pallas import tpu as pltpu
from jax.sharding import PartitionSpec as P

D = 768
HEADS = 12
HEAD_DIM = 32
WIN = 8
SPOTS = 64
REL = 225
WIDE = HEADS * HEAD_DIM
LANES = HEADS * SPOTS
HALF = D // 2
SHARE = 144
ROWS = 48

NEG = -1e30
EPS = 1e-05
SCALE = HEAD_DIM ** (-0.5)

NN = (((1,), (0,)), ((), ()))
NT = (((1,), (1,)), ((), ()))
TN = (((0,), (0,)), ((), ()))

F32 = jnp.float32
BF16 = jnp.bfloat16


def offset_pick():
    column = lane((256, WIN * 128))
    entry = ((column >> 3) & 15) * 15 + (column & 7) - (column >> 7) + 7
    row = lax.broadcasted_iota(jnp.int32, (256, WIN * 128), 0)
    return jnp.where(row == entry, 1.0, 0.0).astype(BF16)


def dot(left, right, dims=NN):
    return lax.dot_general(left, right, dims, preferred_element_type=F32)


def normalize(values):
    center = values - jnp.mean(values, axis=-1, keepdims=True)
    rstd = lax.rsqrt(jnp.mean(center * center, axis=-1, keepdims=True) + EPS)
    return (center * rstd, rstd)


def lane(shape):
    return lax.broadcasted_iota(jnp.int32, shape, len(shape) - 1)


def quadrant_pick(transposed=False):
    row = lax.broadcasted_iota(jnp.int32, (128, 128), 1 if transposed else 0)
    column = lax.broadcasted_iota(jnp.int32, (128, 128), 0 if transposed else 1)
    high = (row & 64) >> 1
    low = (row & 32) >> 3
    spot = high + low + ((row & 12) << 1) + (row & 3) + ((row & 16) << 2)
    return jnp.where(spot == column, 1.0, 0.0).astype(BF16)


def head_mask():
    row = lax.broadcasted_iota(jnp.int32, (LANES, WIDE), 0)
    return jnp.where(row // SPOTS == lane((LANES, WIDE)) // HEAD_DIM, 1.0, 0.0).astype(BF16)


def expand(value, mask_ref):
    return jnp.concatenate([value] * HEADS, axis=0) * mask_ref[...]


def fold(full):
    head = lane((SPOTS, WIDE)) // HEAD_DIM
    out = jnp.zeros((SPOTS, WIDE), F32)
    for h in range(HEADS):
        out = out + jnp.where(head == h, full[h * SPOTS : (h + 1) * SPOTS], 0.0)
    return out


def softmax_down(scores):
    expo = jnp.exp(scores - jnp.max(scores, axis=0, keepdims=True))
    return expo / jnp.sum(expo, axis=0, keepdims=True)


def attention_back(query, key, value, d_mixed, probs, query_wide, mask_ref):
    weights = probs.astype(BF16)
    d_wide = expand(d_mixed, mask_ref)
    d_probs = dot(value, d_wide, NT)
    d_value = dot(weights, d_wide).astype(BF16)
    d_scores = (probs * (d_probs - jnp.sum(probs * d_probs, axis=0, keepdims=True))).astype(BF16)
    d_key = (dot(d_scores, query_wide) * SCALE).astype(BF16)
    d_query = (fold(dot(d_scores, key, TN)) * SCALE).astype(BF16)
    return (d_query, d_key, d_value)


def copy_all(pairs, sems, first=0):
    moves = [
        pltpu.make_async_copy(source, target, sems.at[first + i])
        for i, (source, target) in enumerate(pairs)
    ]
    for move in moves:
        move.start()
    return moves


def wait_all(moves):
    for move in moves:
        move.wait()


def prepare(core_ref, qkv, proj, out, sems):
    start = pl.multiple_of(core_ref[0] * HALF, 128)
    pairs = []
    for i in range(8):
        pairs.append((qkv.at[:, pl.ds(start, HALF)], out.at[i, 0:SHARE]))
        pairs.append((proj.at[:, pl.ds(start, HALF)], out.at[i, SHARE : SHARE + ROWS]))
    wait_all(copy_all(pairs, sems))


def biases(edge_ref, table_p, table_s, to_p, to_s, out_p, out_s, tables, wide, sems):
    tables[...] = jnp.zeros_like(tables)
    tables[0:HEADS, 0:REL] = table_p[...]
    tables[HEADS : 2 * HEADS, 0:REL] = table_s[...]
    values = tables[...]
    high = values.astype(BF16)
    rest = values - high.astype(F32)
    middle = rest.astype(BF16)
    low = (rest - middle.astype(F32)).astype(BF16)
    ones = offset_pick()
    spread = (dot(high, ones) + dot(middle, ones)) + dot(low, ones)
    for row in range(2 * HEADS):
        for d in range(WIN):
            wide[row * WIN + d : row * WIN + d + 1] = spread[row : row + 1, d * 128 : (d + 1) * 128]
    left = lane((WIN, 128)) < SPOTS
    for c in range(WIN):
        move = (7 - c) * WIN
        for pair in range(HEADS // 2):
            for t, out in ((0, out_p), (1, out_s)):
                even = (t * HEADS + 2 * pair) * WIN
                first = pltpu.roll(wide[even : even + WIN], (128 - move) % 128, 1)
                second = pltpu.roll(wide[even + WIN : even + 2 * WIN], (SPOTS - move) % 128, 1)
                out[c * WIN : (c + 1) * WIN, pair * 128 : (pair + 1) * 128] = jnp.where(left, first, second)
    at = lane((SPOTS, LANES))
    key_at = lax.broadcasted_iota(jnp.int32, (SPOTS, LANES), 0)
    cross = at ^ key_at
    barred = (cross & 32) * edge_ref[0] + (cross & 4) * edge_ref[1]
    out_s[...] = jnp.where(barred != 0, NEG, out_s[...])
    wait_all(copy_all([(out_p, to_p), (out_s, to_s)], sems))


def project(rows_ref, w_mine, w_other, mine, other):
    return dot(rows_ref[:, pl.ds(mine, HALF)], w_mine, NT) + dot(
        rows_ref[:, pl.ds(other, HALF)], w_other, NT
    )


def sides(core_ref):
    mine = pl.multiple_of(core_ref[0] * HALF, 128)
    return (mine, pl.multiple_of(HALF - mine, 128))


def qkv_of(ref):
    return ref[:, 0:SHARE].reshape(3 * WIDE, HALF)


def proj_of(ref):
    return ref[:, SHARE : SHARE + ROWS].reshape(WIDE, HALF)


def input_grad(grad, normed, rstd, d_packed, w_mine, w_other, mine, other, sums):
    sums[:, pl.ds(mine, HALF)] = dot(d_packed, w_mine)
    sums[:, pl.ds(other, HALF)] = dot(d_packed, w_other)
    d_normed = sums[...]
    d_input = rstd * (
        d_normed
        - jnp.mean(d_normed, axis=-1, keepdims=True)
        - normed * jnp.mean(d_normed * normed, axis=-1, keepdims=True)
    )
    return (grad + d_input).astype(BF16)


def plain_forward(
    core_ref,
    tok_far,
    cot_far,
    bias_far,
    w_mine_ref,
    w_other_ref,
    out_o,
    out_r,
    out_b,
    out_d,
    tok,
    cot,
    bias_p,
    own,
    above,
    rows,
    sums,
    mask,
    sems,
):
    mine, other = sides(core_ref)
    loads = copy_all([(tok_far, tok), (bias_far, bias_p), (cot_far, cot)], sems)
    mask[...] = head_mask()
    loads[0].wait()
    inputs = tok[...].astype(F32)
    rows[...] = normalize(inputs)[0].astype(BF16)
    w_mine, w_other = qkv_of(w_mine_ref), qkv_of(w_other_ref)
    packed = project(rows, w_mine, w_other, mine, other).astype(BF16)
    loads[1].wait()
    mixed = []
    for s in range(2):
        part = packed[s * SPOTS : (s + 1) * SPOTS]
        query, key, value = part[:, :WIDE], part[:, WIDE : 2 * WIDE], part[:, 2 * WIDE :]
        probs = softmax_down(dot(key, expand(query, mask), NT) * SCALE + bias_p[...])
        mixed.append(fold(dot(probs.astype(BF16), value, TN)).astype(BF16))
    mixed = jnp.concatenate(mixed, axis=0)
    sums[:, pl.ds(mine, HALF)] = dot(mixed, proj_of(w_mine_ref))
    sums[:, pl.ds(other, HALF)] = dot(mixed, proj_of(w_other_ref))
    block_out = (inputs + sums[...]).astype(BF16)
    pick = quadrant_pick()
    loads[2].wait()
    for whole, first in ((block_out, 0), (mixed, D), (cot[...], D + WIDE)):
        quads = dot(pick, whole).astype(BF16)
        for i, out in enumerate((out_d, above, out_r, own)):
            out[:, first : first + whole.shape[1]] = quads[i * 32 : (i + 1) * 32]
    wait_all(copy_all([(own, out_o), (above, out_b)], sems, 3))


def main_kernel(
    grad_scale,
    core_ref,
    own_far,
    bias_far,
    right,
    below,
    diag,
    w_mine_ref,
    w_other_ref,
    to_own,
    to_column,
    to_below,
    to_local,
    bias_s,
    quads,
    out_plain,
    out_shift,
    staged,
    rows_small,
    grads,
    sums,
    mask,
    sems,
):
    mine, other = sides(core_ref)
    loads = copy_all([(own_far, staged.at[0:32]), (bias_far, bias_s)], sems)
    mask[...] = head_mask()
    for i, part in ((1, right), (2, below), (3, diag)):
        staged[i * 32 : (i + 1) * 32] = part[...]
    wait_all(loads)
    pick = quadrant_pick(True)
    grads[...] = dot(pick, staged[:, D + WIDE :]).astype(BF16)
    block_out = dot(pick, staged[:, 0:D])
    mixed_plain = dot(pick, staged[:, D : D + WIDE]).astype(BF16)
    normed, rstd = normalize(block_out)
    rows_small[...] = normed.astype(BF16)
    w_mine, w_other = qkv_of(w_mine_ref), qkv_of(w_other_ref)
    packed = project(rows_small, w_mine, w_other, mine, other).astype(BF16)
    d_mixed = project(grads, proj_of(w_mine_ref), proj_of(w_other_ref), mine, other).astype(BF16)
    mixed, forward, d_packed = [], [], []
    for s in range(2):
        part = packed[s * SPOTS : (s + 1) * SPOTS]
        query, key, value = part[:, :WIDE], part[:, WIDE : 2 * WIDE], part[:, 2 * WIDE :]
        query_wide = expand(query, mask)
        probs = softmax_down(dot(key, query_wide, NT) * SCALE + bias_s[...])
        mixed.append(fold(dot(probs.astype(BF16), value, TN)).astype(BF16))
        forward.append((query, key, value, query_wide, probs))
    mixed_shift = jnp.concatenate(mixed, axis=0)
    local_shift = dot(mixed_shift, grads[...], TN) * grad_scale
    out_shift[...] = local_shift.astype(BF16).reshape(8, ROWS, D)
    early = copy_all([(out_shift, to_local.at[:, 1])], sems, 6)
    for s in range(2):
        query, key, value, query_wide, probs = forward[s]
        back = attention_back(
            query, key, value, d_mixed[s * SPOTS : (s + 1) * SPOTS], probs, query_wide, mask
        )
        d_packed.append(jnp.concatenate(back, axis=1))
    d_packed = jnp.concatenate(d_packed, axis=0)
    grad = input_grad(
        grads[...].astype(F32), normed, rstd, d_packed, w_mine, w_other, mine, other, sums
    )
    quads[...] = dot(quadrant_pick(), grad).astype(BF16)
    stores = copy_all(
        [
            (quads.at[0:32], to_own),
            (quads.at[32:64], to_column.at[0:32]),
            (quads.at[96:128], to_column.at[32:64]),
            (quads.at[64:96], to_below),
        ],
        sems,
        2,
    )
    local_plain = dot(mixed_plain, grad, TN) * grad_scale
    out_plain[...] = local_plain.astype(BF16).reshape(8, ROWS, D)
    stores += copy_all([(out_plain, to_local.at[:, 0])], sems, 7)
    wait_all(stores + early)


def sum_split(core_ref, parts, out_keep, out_send, total):
    mine, other = sides(core_ref)
    total[...] = jnp.sum(parts[...].astype(F32), axis=0)
    out_keep[...] = total[:, :, pl.ds(mine, HALF)]
    out_send[...] = total[:, :, pl.ds(other, HALF)].astype(BF16)


def pair_copies(keep, arrived, out):
    value = (keep[...] + arrived[...].astype(F32)).astype(BF16)
    for i in range(out.shape[0]):
        out[i] = value


def sum_copies(parts, out):
    value = jnp.sum(parts[...].astype(F32), axis=0).astype(BF16)
    for i in range(out.shape[0]):
        out[i] = value


def finish(parts, out_plain, out_shift):
    for i, out in enumerate((out_plain, out_shift)):
        out[:, 0:HALF] = parts[0, i].astype(F32)
        out[:, HALF:D] = parts[1, i].astype(F32)


def plain_back(
    core_ref,
    tok_far,
    own_far,
    bias_far,
    mine_far,
    other_far,
    column,
    row,
    out,
    tok,
    bias_p,
    w_mine_ref,
    w_other_ref,
    staged,
    rows,
    grads,
    sums,
    mask,
    sems,
):
    mine, other = sides(core_ref)
    loads = copy_all(
        [
            (tok_far, tok),
            (mine_far, w_mine_ref),
            (other_far, w_other_ref),
            (own_far, staged.at[96:128]),
            (bias_far, bias_p),
        ],
        sems,
    )
    mask[...] = head_mask()
    staged[0:32] = row[32:64]
    staged[32:64] = row[0:32]
    staged[64:96] = column[0:32]
    loads[0].wait()
    normed, rstd = normalize(tok[...].astype(F32))
    rows[...] = normed.astype(BF16)
    wait_all(loads[1:])
    w_mine, w_other = qkv_of(w_mine_ref), qkv_of(w_other_ref)
    packed = project(rows, w_mine, w_other, mine, other).astype(BF16)
    gathered = dot(quadrant_pick(True), staged[...])
    grads[...] = gathered.astype(BF16)
    d_mixed = project(grads, proj_of(w_mine_ref), proj_of(w_other_ref), mine, other).astype(BF16)
    d_packed = []
    for s in range(2):
        part = packed[s * SPOTS : (s + 1) * SPOTS]
        query, key, value = part[:, :WIDE], part[:, WIDE : 2 * WIDE], part[:, 2 * WIDE :]
        query_wide = expand(query, mask)
        probs = softmax_down(dot(key, query_wide, NT) * SCALE + bias_p[...])
        back = attention_back(
            query, key, value, d_mixed[s * SPOTS : (s + 1) * SPOTS], probs, query_wide, mask
        )
        d_packed.append(jnp.concatenate(back, axis=1))
    d_packed = jnp.concatenate(d_packed, axis=0)
    out[...] = input_grad(gathered, normed, rstd, d_packed, w_mine, w_other, mine, other, sums)


VMEM = pl.BlockSpec(memory_space=pltpu.VMEM)
SMEM = pl.BlockSpec(memory_space=pltpu.SMEM)
HBM = pl.BlockSpec(memory_space=pltpu.HBM)


def params(size=32):
    return pltpu.CompilerParams(vmem_limit_bytes=size * 1024 * 1024)


def far(value):
    return pltpu.with_memory_space_constraint(value, pltpu.HBM)


def cost(flops, size):
    return pl.CostEstimate(flops=flops, bytes_accessed=size, transcendentals=0)


def tm_groups(bits):
    size = lax.axis_size("tm")
    step = {"core": 1, "y_hi": 2, "z": 8}[bits]
    count = {"core": 2, "y_hi": 4, "z": 8}[bits]
    groups = []
    for first in range(size):
        if (first // step) % count == 0:
            groups.append([first + step * i for i in range(count)])
    return groups


def swap(value, axis, groups=None):
    return lax.all_to_all(value, axis, 0, 0, axis_index_groups=groups)


def from_offset(value, along_tm, along_freq):
    n_tm, n_freq = lax.axis_size("tm"), lax.axis_size("freq")
    pairs = []
    for t in range(n_tm):
        for f in range(n_freq):
            source = ((t + along_tm) % n_tm) * n_freq + (f + along_freq) % n_freq
            pairs.append((source, t * n_freq + f))
    return lax.ppermute(value, ("tm", "freq"), pairs)


def other_core(value):
    return lax.ppermute(value, "tm", [(i, i ^ 1) for i in range(lax.axis_size("tm"))])


def summed(parts, count):
    return pl.pallas_call(
        sum_copies,
        out_shape=jax.ShapeDtypeStruct((count,) + parts.shape[1:], BF16),
        in_specs=[VMEM],
        out_specs=VMEM,
        compiler_params=params(),
        name="sum_copies",
    )(parts)


def shards(
    tokens, cotangent, qkv_plain, qkv_shift, proj_plain, proj_shift, table_plain, table_shift
):
    core = (lax.axis_index("tm") % 2).astype(jnp.int32).reshape(1)
    last_freq = lax.axis_index("freq") == lax.axis_size("freq") - 1
    last_time = lax.axis_index("tm") == lax.axis_size("tm") - 1
    edge = jnp.stack([last_freq, last_time]).astype(jnp.int32)
    grad_scale = 1.0 / math.sqrt(128 * lax.axis_size("tm") * lax.axis_size("freq"))
    tok = tokens.reshape(128, D)
    cot = cotangent.reshape(128, D)

    def share(qkv, proj):
        return pl.pallas_call(
            prepare,
            out_shape=pltpu.HBM((8, SHARE + ROWS, HALF), BF16),
            in_specs=[SMEM, HBM, HBM],
            out_specs=HBM,
            scratch_shapes=[pltpu.SemaphoreType.DMA((16,))],
            compiler_params=params(),
            name="prepare",
        )(core, far(qkv.T), far(proj))

    first_mine = swap(share(qkv_plain, proj_plain), "freq")
    second_share = share(qkv_shift, proj_shift)
    table = pltpu.HBM((SPOTS, LANES), F32)
    bias_p, bias_s = pl.pallas_call(
        biases,
        out_shape=(table, table),
        in_specs=[SMEM, VMEM, VMEM],
        out_specs=[HBM] * 2,
        scratch_shapes=[
            pltpu.VMEM((SPOTS, LANES), F32),
            pltpu.VMEM((SPOTS, LANES), F32),
            pltpu.VMEM((32, 256), F32),
            pltpu.VMEM((2 * HEADS * WIN, 128), F32),
            pltpu.SemaphoreType.DMA((2,)),
        ],
        compiler_params=params(),
        name="biases",
    )(edge, table_plain, table_shift)

    first_mine, second_share, bias_p, bias_s = lax.optimization_barrier(
        (first_mine, second_share, bias_p, bias_s)
    )
    first_other = other_core(first_mine)
    second_mine = swap(second_share, "freq")
    packet = pltpu.HBM((32, 2 * D + WIDE), BF16)
    near = jax.ShapeDtypeStruct((32, 2 * D + WIDE), BF16)
    own, to_left, to_above, to_diag = pl.pallas_call(
        plain_forward,
        out_shape=(packet, near, packet, near),
        in_specs=[SMEM] + [HBM] * 3 + [VMEM] * 2,
        out_specs=[HBM, VMEM, HBM, VMEM],
        scratch_shapes=[
            pltpu.VMEM((128, D), BF16),
            pltpu.VMEM((128, D), BF16),
            pltpu.VMEM((SPOTS, LANES), F32),
            pltpu.VMEM((32, 2 * D + WIDE), BF16),
            pltpu.VMEM((32, 2 * D + WIDE), BF16),
            pltpu.VMEM((128, D), BF16),
            pltpu.VMEM((128, D), F32),
            pltpu.VMEM((LANES, WIDE), BF16),
            pltpu.SemaphoreType.DMA((5,)),
        ],
        compiler_params=params(),
        cost_estimate=cost(1_000_000, 1_000_000),
        name="plain_forward",
    )(core, far(tok), far(cot), far(bias_p), first_mine, first_other)
    right = from_offset(to_left, 1, 0)
    below = from_offset(to_above, 0, 1)
    diag = from_offset(to_diag, 1, 1)
    second_mine, right, diag = lax.optimization_barrier((second_mine, right, diag))
    second_other = other_core(second_mine)
    piece = pltpu.HBM((32, D), BF16)
    column = pltpu.HBM((64, D), BF16)
    local = pltpu.HBM((8, 2, ROWS, D), BF16)
    g_own, to_right, to_below, local = pl.pallas_call(
        lambda *refs: main_kernel(grad_scale, *refs),
        out_shape=(piece, column, piece, local),
        in_specs=[SMEM] + [HBM] * 2 + [VMEM] * 5,
        out_specs=[HBM] * 4,
        scratch_shapes=[
            pltpu.VMEM((SPOTS, LANES), F32),
            pltpu.VMEM((128, D), BF16),
            pltpu.VMEM((8, ROWS, D), BF16),
            pltpu.VMEM((8, ROWS, D), BF16),
            pltpu.VMEM((128, 2 * D + WIDE), BF16),
            pltpu.VMEM((128, D), BF16),
            pltpu.VMEM((128, D), BF16),
            pltpu.VMEM((128, D), F32),
            pltpu.VMEM((LANES, WIDE), BF16),
            pltpu.SemaphoreType.DMA((8,)),
        ],
        compiler_params=params(),
        cost_estimate=cost(1_000_000, 1_000_000),
        name="main",
    )(core, far(own), far(bias_s), right, below, diag, second_mine, second_other)

    local, to_right, to_below = lax.optimization_barrier((local, to_right, to_below))
    part = swap(local, "freq")
    column = from_offset(to_right, -1, 0)
    half = (2, ROWS, HALF)
    keep, send = pl.pallas_call(
        sum_split,
        out_shape=(jax.ShapeDtypeStruct(half, F32), jax.ShapeDtypeStruct(half, BF16)),
        in_specs=[SMEM, VMEM],
        out_specs=[VMEM] * 2,
        scratch_shapes=[pltpu.VMEM((2, ROWS, D), F32)],
        compiler_params=params(),
        name="sum_split",
    )(core, part)
    part = pl.pallas_call(
        pair_copies,
        out_shape=jax.ShapeDtypeStruct((8,) + half, BF16),
        in_specs=[VMEM] * 2,
        out_specs=VMEM,
        compiler_params=params(),
        name="pair_copies",
    )(keep, other_core(send))
    part, column, to_below = lax.optimization_barrier((part, column, to_below))
    part = swap(part, "tm", tm_groups("z"))
    row = from_offset(jnp.concatenate([to_below, column[32:64]], axis=0), 0, -1)
    part, row = lax.optimization_barrier((part, row))
    part = swap(summed(part, 4), "tm", tm_groups("y_hi"))
    grad_tokens = pl.pallas_call(
        plain_back,
        out_shape=jax.ShapeDtypeStruct((128, D), BF16),
        in_specs=[SMEM] + [HBM] * 5 + [VMEM] * 2,
        out_specs=VMEM,
        scratch_shapes=[
            pltpu.VMEM((128, D), BF16),
            pltpu.VMEM((SPOTS, LANES), F32),
            pltpu.VMEM((8, SHARE + ROWS, HALF), BF16),
            pltpu.VMEM((8, SHARE + ROWS, HALF), BF16),
            pltpu.VMEM((128, D), BF16),
            pltpu.VMEM((128, D), BF16),
            pltpu.VMEM((128, D), BF16),
            pltpu.VMEM((128, D), F32),
            pltpu.VMEM((LANES, WIDE), BF16),
            pltpu.SemaphoreType.DMA((5,)),
        ],
        compiler_params=params(),
        cost_estimate=cost(4_000_000_000, 4_000_000),
        name="plain_back",
    )(core, far(tok), far(g_own), far(bias_p), far(first_mine), far(first_other), column, row)
    part, grad_tokens = lax.optimization_barrier((part, grad_tokens))
    part = summed(part, 1)[0]
    part = lax.all_gather(part, "tm", axis_index_groups=tm_groups("core"))
    grad_plain, grad_shift = pl.pallas_call(
        finish,
        out_shape=(jax.ShapeDtypeStruct((ROWS, D), F32),) * 2,
        in_specs=[VMEM],
        out_specs=[VMEM] * 2,
        compiler_params=params(),
        name="finish",
    )(part)
    return (grad_tokens.reshape(tokens.shape), grad_plain, grad_shift)


def solution(mesh):
    placed = (
        P(None, "freq", "tm", None),
        P(None, "freq", "tm", None),
        P(None, "freq"),
        P(None, "freq"),
        P("freq", None),
        P("freq", None),
        P(),
        P(),
    )
    return jax.shard_map(
        shards,
        mesh=mesh,
        in_specs=placed,
        out_specs=(P(None, "freq", "tm", None), P("freq", None), P("freq", None)),
        check_vma=False,
    )
```

```python
import math

import jax
import jax.numpy as jnp
from jax import lax
from jax.experimental import pallas as pl
from jax.experimental.pallas import tpu as pltpu
from jax.sharding import PartitionSpec as P

D = 768
HEADS = 12
HEAD_DIM = 32
WIN = 8
SPOTS = 64
REL = 225
WIDE = HEADS * HEAD_DIM
LANES = HEADS * SPOTS
HALF = D // 2
SHARE = 144
ROWS = 48

NEG = -1e30
EPS = 1e-05
SCALE = HEAD_DIM ** (-0.5)

NN = (((1,), (0,)), ((), ()))
NT = (((1,), (1,)), ((), ()))
TN = (((0,), (0,)), ((), ()))

F32 = jnp.float32
BF16 = jnp.bfloat16


def offset_pick():
    column = lane((256, WIN * 128))
    entry = ((column >> 3) & 15) * 15 + (column & 7) - (column >> 7) + 7
    row = lax.broadcasted_iota(jnp.int32, (256, WIN * 128), 0)
    return jnp.where(row == entry, 1.0, 0.0).astype(BF16)


def dot(left, right, dims=NN):
    return lax.dot_general(left, right, dims, preferred_element_type=F32)


def normalize(values):
    center = values - jnp.mean(values, axis=-1, keepdims=True)
    rstd = lax.rsqrt(jnp.mean(center * center, axis=-1, keepdims=True) + EPS)
    return (center * rstd, rstd)


def lane(shape):
    return lax.broadcasted_iota(jnp.int32, shape, len(shape) - 1)


def quadrant_pick(transposed=False):
    row = lax.broadcasted_iota(jnp.int32, (128, 128), 1 if transposed else 0)
    column = lax.broadcasted_iota(jnp.int32, (128, 128), 0 if transposed else 1)
    high = (row & 64) >> 1
    low = (row & 32) >> 3
    spot = high + low + ((row & 12) << 1) + (row & 3) + ((row & 16) << 2)
    return jnp.where(spot == column, 1.0, 0.0).astype(BF16)


def head_mask():
    row = lax.broadcasted_iota(jnp.int32, (LANES, WIDE), 0)
    return jnp.where(row // SPOTS == lane((LANES, WIDE)) // HEAD_DIM, 1.0, 0.0).astype(BF16)


def expand(value, mask_ref):
    return jnp.concatenate([value] * HEADS, axis=0) * mask_ref[...]


def fold(full):
    head = lane((SPOTS, WIDE)) // HEAD_DIM
    out = jnp.zeros((SPOTS, WIDE), F32)
    for h in range(HEADS):
        out = out + jnp.where(head == h, full[h * SPOTS : (h + 1) * SPOTS], 0.0)
    return out


def softmax_down(scores):
    expo = jnp.exp(scores - jnp.max(scores, axis=0, keepdims=True))
    return expo / jnp.sum(expo, axis=0, keepdims=True)


def attention_back(query, key, value, d_mixed, probs, query_wide, mask_ref):
    weights = probs.astype(BF16)
    d_wide = expand(d_mixed, mask_ref)
    d_probs = dot(value, d_wide, NT)
    d_value = dot(weights, d_wide).astype(BF16)
    d_scores = (probs * (d_probs - jnp.sum(probs * d_probs, axis=0, keepdims=True))).astype(BF16)
    d_key = (dot(d_scores, query_wide) * SCALE).astype(BF16)
    d_query = (fold(dot(d_scores, key, TN)) * SCALE).astype(BF16)
    return (d_query, d_key, d_value)


def copy_all(pairs, sems, first=0):
    moves = [
        pltpu.make_async_copy(source, target, sems.at[first + i])
        for i, (source, target) in enumerate(pairs)
    ]
    for move in moves:
        move.start()
    return moves


def wait_all(moves):
    for move in moves:
        move.wait()


def prepare(core_ref, qkv_p, proj_p, qkv_s, proj_s, out_first, out_second, block, second, sems):
    start = pl.multiple_of(core_ref[0] * HALF, 128)
    second[0:SHARE] = qkv_s[:, pl.ds(start, HALF)]
    second[SHARE : SHARE + ROWS] = proj_s[:, pl.ds(start, HALF)]
    block[0:SHARE] = qkv_p[:, pl.ds(start, HALF)]
    block[SHARE : SHARE + ROWS] = proj_p[:, pl.ds(start, HALF)]
    moves = [(second, out_second)] + [(block, out_first.at[i]) for i in range(8)]
    wait_all(copy_all(moves, sems))


def biases(edge_ref, table_p, table_s, to_p, to_s, out_p, out_s, tables, wide, sems):
    tables[...] = jnp.zeros_like(tables)
    tables[0:HEADS, 0:REL] = table_p[...]
    tables[HEADS : 2 * HEADS, 0:REL] = table_s[...]
    values = tables[...]
    high = values.astype(BF16)
    rest = values - high.astype(F32)
    middle = rest.astype(BF16)
    low = (rest - middle.astype(F32)).astype(BF16)
    ones = offset_pick()
    spread = (dot(high, ones) + dot(middle, ones)) + dot(low, ones)
    for row in range(2 * HEADS):
        for d in range(WIN):
            wide[row * WIN + d : row * WIN + d + 1] = spread[row : row + 1, d * 128 : (d + 1) * 128]
    left = lane((WIN, 128)) < SPOTS
    for c in range(WIN):
        move = (7 - c) * WIN
        for pair in range(HEADS // 2):
            for t, out in ((0, out_p), (1, out_s)):
                even = (t * HEADS + 2 * pair) * WIN
                first = pltpu.roll(wide[even : even + WIN], (128 - move) % 128, 1)
                second = pltpu.roll(wide[even + WIN : even + 2 * WIN], (SPOTS - move) % 128, 1)
                out[c * WIN : (c + 1) * WIN, pair * 128 : (pair + 1) * 128] = jnp.where(left, first, second)
    at = lane((SPOTS, LANES))
    key_at = lax.broadcasted_iota(jnp.int32, (SPOTS, LANES), 0)
    cross = at ^ key_at
    barred = (cross & 32) * edge_ref[0] + (cross & 4) * edge_ref[1]
    out_s[...] = jnp.where(barred != 0, NEG, out_s[...])
    wait_all(copy_all([(out_p, to_p), (out_s, to_s)], sems))


def project(rows_ref, w_mine, w_other, mine, other):
    return dot(rows_ref[:, pl.ds(mine, HALF)], w_mine, NT) + dot(
        rows_ref[:, pl.ds(other, HALF)], w_other, NT
    )


def sides(core_ref):
    mine = pl.multiple_of(core_ref[0] * HALF, 128)
    return (mine, pl.multiple_of(HALF - mine, 128))


def qkv_of(ref):
    return ref[:, 0:SHARE].reshape(3 * WIDE, HALF)


def proj_of(ref):
    return ref[:, SHARE : SHARE + ROWS].reshape(WIDE, HALF)


def input_grad(grad, normed, rstd, d_packed, w_mine, w_other, mine, other, sums):
    sums[:, pl.ds(mine, HALF)] = dot(d_packed, w_mine)
    sums[:, pl.ds(other, HALF)] = dot(d_packed, w_other)
    d_normed = sums[...]
    d_input = rstd * (
        d_normed
        - jnp.mean(d_normed, axis=-1, keepdims=True)
        - normed * jnp.mean(d_normed * normed, axis=-1, keepdims=True)
    )
    return (grad + d_input).astype(BF16)


def plain_forward(
    core_ref,
    tok_far,
    cot_far,
    bias_far,
    w_mine_ref,
    w_other_ref,
    out_o,
    out_r,
    out_b,
    out_d,
    tok,
    cot,
    bias_p,
    packets,
    rows,
    sums,
    mask,
    sems,
):
    mine, other = sides(core_ref)
    loads = copy_all([(tok_far, tok), (bias_far, bias_p), (cot_far, cot)], sems)
    mask[...] = head_mask()
    loads[0].wait()
    inputs = tok[...].astype(F32)
    rows[...] = normalize(inputs)[0].astype(BF16)
    w_mine, w_other = qkv_of(w_mine_ref), qkv_of(w_other_ref)
    packed = project(rows, w_mine, w_other, mine, other).astype(BF16)
    loads[1].wait()
    mixed = []
    for s in range(2):
        part = packed[s * SPOTS : (s + 1) * SPOTS]
        query, key, value = part[:, :WIDE], part[:, WIDE : 2 * WIDE], part[:, 2 * WIDE :]
        probs = softmax_down(dot(key, expand(query, mask), NT) * SCALE + bias_p[...])
        mixed.append(fold(dot(probs.astype(BF16), value, TN)).astype(BF16))
    mixed = jnp.concatenate(mixed, axis=0)
    sums[:, pl.ds(mine, HALF)] = dot(mixed, proj_of(w_mine_ref))
    sums[:, pl.ds(other, HALF)] = dot(mixed, proj_of(w_other_ref))
    block_out = (inputs + sums[...]).astype(BF16)
    pick = quadrant_pick()
    loads[2].wait()
    for whole, first in ((block_out, 0), (mixed, D), (cot[...], D + WIDE)):
        packets[:, first : first + whole.shape[1]] = dot(pick, whole).astype(BF16)
    outs = (out_d, out_b, out_r, out_o)
    wait_all(copy_all([(packets.at[i * 32 : (i + 1) * 32], out) for i, out in enumerate(outs)], sems, 3))


def main_kernel(
    grad_scale,
    core_ref,
    own_far,
    bias_far,
    mine_far,
    right,
    below,
    diag,
    w_other_ref,
    to_own,
    to_column,
    to_below,
    to_local,
    w_mine_ref,
    bias_s,
    quads,
    out_local,
    staged,
    rows_small,
    grads,
    sums,
    mask,
    sems,
):
    mine, other = sides(core_ref)
    loads = copy_all(
        [(own_far, staged.at[0:32]), (mine_far, w_mine_ref), (bias_far, bias_s)], sems
    )
    mask[...] = head_mask()
    for i, part in ((1, right), (2, below), (3, diag)):
        staged[i * 32 : (i + 1) * 32] = part[...]
    loads[0].wait()
    pick = quadrant_pick(True)
    grads[...] = dot(pick, staged[:, D + WIDE :]).astype(BF16)
    block_out = dot(pick, staged[:, 0:D])
    mixed_plain = dot(pick, staged[:, D : D + WIDE]).astype(BF16)
    normed, rstd = normalize(block_out)
    rows_small[...] = normed.astype(BF16)
    wait_all(loads[1:])
    w_mine, w_other = qkv_of(w_mine_ref), qkv_of(w_other_ref)
    packed = project(rows_small, w_mine, w_other, mine, other).astype(BF16)
    d_mixed = project(grads, proj_of(w_mine_ref), proj_of(w_other_ref), mine, other).astype(BF16)
    mixed, d_packed = [], []
    for s in range(2):
        part = packed[s * SPOTS : (s + 1) * SPOTS]
        query, key, value = part[:, :WIDE], part[:, WIDE : 2 * WIDE], part[:, 2 * WIDE :]
        query_wide = expand(query, mask)
        probs = softmax_down(dot(key, query_wide, NT) * SCALE + bias_s[...])
        mixed.append(fold(dot(probs.astype(BF16), value, TN)).astype(BF16))
        back = attention_back(
            query, key, value, d_mixed[s * SPOTS : (s + 1) * SPOTS], probs, query_wide, mask
        )
        d_packed.append(jnp.concatenate(back, axis=1))
    mixed_shift = jnp.concatenate(mixed, axis=0)
    d_packed = jnp.concatenate(d_packed, axis=0)
    grad = input_grad(
        grads[...].astype(F32), normed, rstd, d_packed, w_mine, w_other, mine, other, sums
    )
    quads[...] = dot(quadrant_pick(), grad).astype(BF16)
    stores = copy_all(
        [
            (quads.at[0:32], to_own),
            (quads.at[32:64], to_column.at[0:32]),
            (quads.at[96:128], to_column.at[32:64]),
            (quads.at[64:96], to_below),
        ],
        sems,
        3,
    )
    local_shift = dot(mixed_shift, grads[...], TN) * grad_scale
    out_local[:, 1] = local_shift.astype(BF16).reshape(8, ROWS, D)
    local_plain = dot(mixed_plain, grad, TN) * grad_scale
    out_local[:, 0] = local_plain.astype(BF16).reshape(8, ROWS, D)
    wait_all(copy_all([(out_local, to_local)], sems, 7))
    wait_all(stores)


def sum_split(core_ref, parts, out_keep, out_send, total):
    mine, other = sides(core_ref)
    total[...] = jnp.sum(parts[...].astype(F32), axis=0)
    out_keep[...] = total[:, :, pl.ds(mine, HALF)]
    out_send[...] = total[:, :, pl.ds(other, HALF)].astype(BF16)


def pair_copies(keep, arrived, out):
    value = (keep[...] + arrived[...].astype(F32)).astype(BF16)
    for i in range(out.shape[0]):
        out[i] = value


def sum_copies(parts, out):
    value = jnp.sum(parts[...].astype(F32), axis=0).astype(BF16)
    for i in range(out.shape[0]):
        out[i] = value


def finish(parts, out_plain, out_shift):
    for i, out in enumerate((out_plain, out_shift)):
        out[:, 0:HALF] = parts[0, i].astype(F32)
        out[:, HALF:D] = parts[1, i].astype(F32)


def plain_back(
    core_ref,
    tok_far,
    own_far,
    bias_far,
    mine_far,
    other_far,
    column,
    row,
    out,
    tok,
    bias_p,
    w_mine_ref,
    w_other_ref,
    staged,
    rows,
    grads,
    sums,
    mask,
    sems,
):
    mine, other = sides(core_ref)
    loads = copy_all(
        [
            (tok_far, tok),
            (mine_far, w_mine_ref),
            (other_far, w_other_ref),
            (own_far, staged.at[96:128]),
            (bias_far, bias_p),
        ],
        sems,
    )
    mask[...] = head_mask()
    staged[0:32] = row[32:64]
    staged[32:64] = row[0:32]
    staged[64:96] = column[0:32]
    loads[0].wait()
    normed, rstd = normalize(tok[...].astype(F32))
    rows[...] = normed.astype(BF16)
    wait_all(loads[1:])
    w_mine, w_other = qkv_of(w_mine_ref), qkv_of(w_other_ref)
    packed = project(rows, w_mine, w_other, mine, other).astype(BF16)
    gathered = dot(quadrant_pick(True), staged[...])
    grads[...] = gathered.astype(BF16)
    d_mixed = project(grads, proj_of(w_mine_ref), proj_of(w_other_ref), mine, other).astype(BF16)
    d_packed = []
    for s in range(2):
        part = packed[s * SPOTS : (s + 1) * SPOTS]
        query, key, value = part[:, :WIDE], part[:, WIDE : 2 * WIDE], part[:, 2 * WIDE :]
        query_wide = expand(query, mask)
        probs = softmax_down(dot(key, query_wide, NT) * SCALE + bias_p[...])
        back = attention_back(
            query, key, value, d_mixed[s * SPOTS : (s + 1) * SPOTS], probs, query_wide, mask
        )
        d_packed.append(jnp.concatenate(back, axis=1))
    d_packed = jnp.concatenate(d_packed, axis=0)
    out[...] = input_grad(gathered, normed, rstd, d_packed, w_mine, w_other, mine, other, sums)


VMEM = pl.BlockSpec(memory_space=pltpu.VMEM)
SMEM = pl.BlockSpec(memory_space=pltpu.SMEM)
HBM = pl.BlockSpec(memory_space=pltpu.HBM)


def params(size=32):
    return pltpu.CompilerParams(vmem_limit_bytes=size * 1024 * 1024)


def far(value):
    return pltpu.with_memory_space_constraint(value, pltpu.HBM)


def cost(flops, size):
    return pl.CostEstimate(flops=flops, bytes_accessed=size, transcendentals=0)


def tm_groups(bits):
    size = lax.axis_size("tm")
    step = {"core": 1, "y_hi": 2, "z": 8}[bits]
    count = {"core": 2, "y_hi": 4, "z": 8}[bits]
    groups = []
    for first in range(size):
        if (first // step) % count == 0:
            groups.append([first + step * i for i in range(count)])
    return groups


def swap(value, axis, groups=None):
    return lax.all_to_all(value, axis, 0, 0, axis_index_groups=groups)


def from_offset(value, along_tm, along_freq):
    n_tm, n_freq = lax.axis_size("tm"), lax.axis_size("freq")
    pairs = []
    for t in range(n_tm):
        for f in range(n_freq):
            source = ((t + along_tm) % n_tm) * n_freq + (f + along_freq) % n_freq
            pairs.append((source, t * n_freq + f))
    return lax.ppermute(value, ("tm", "freq"), pairs)


def other_core(value):
    return lax.ppermute(value, "tm", [(i, i ^ 1) for i in range(lax.axis_size("tm"))])


def summed(parts, count):
    return pl.pallas_call(
        sum_copies,
        out_shape=jax.ShapeDtypeStruct((count,) + parts.shape[1:], BF16),
        in_specs=[VMEM],
        out_specs=VMEM,
        compiler_params=params(),
        name="sum_copies",
    )(parts)


def shards(
    tokens, cotangent, qkv_plain, qkv_shift, proj_plain, proj_shift, table_plain, table_shift
):
    core = (lax.axis_index("tm") % 2).astype(jnp.int32).reshape(1)
    last_freq = lax.axis_index("freq") == lax.axis_size("freq") - 1
    last_time = lax.axis_index("tm") == lax.axis_size("tm") - 1
    edge = jnp.stack([last_freq, last_time]).astype(jnp.int32)
    grad_scale = 1.0 / math.sqrt(128 * lax.axis_size("tm") * lax.axis_size("freq"))
    tok = tokens.reshape(128, D)
    cot = cotangent.reshape(128, D)

    first_share, second_share = pl.pallas_call(
        prepare,
        out_shape=(
            pltpu.HBM((8, SHARE + ROWS, HALF), BF16),
            pltpu.HBM((SHARE + ROWS, HALF), BF16),
        ),
        in_specs=[SMEM] + [VMEM] * 4,
        out_specs=[HBM] * 2,
        scratch_shapes=[
            pltpu.VMEM((SHARE + ROWS, HALF), BF16),
            pltpu.VMEM((SHARE + ROWS, HALF), BF16),
            pltpu.SemaphoreType.DMA((9,)),
        ],
        compiler_params=params(60),
        name="prepare",
    )(core, qkv_plain.T, proj_plain, qkv_shift.T, proj_shift)
    second_mine = lax.all_gather(second_share, "freq")
    first_mine = swap(first_share, "freq")

    table = pltpu.HBM((SPOTS, LANES), F32)
    bias_p, bias_s = pl.pallas_call(
        biases,
        out_shape=(table, table),
        in_specs=[SMEM, VMEM, VMEM],
        out_specs=[HBM] * 2,
        scratch_shapes=[
            pltpu.VMEM((SPOTS, LANES), F32),
            pltpu.VMEM((SPOTS, LANES), F32),
            pltpu.VMEM((32, 256), F32),
            pltpu.VMEM((2 * HEADS * WIN, 128), F32),
            pltpu.SemaphoreType.DMA((2,)),
        ],
        compiler_params=params(),
        name="biases",
    )(edge, table_plain, table_shift)

    first_mine, bias_p, bias_s = lax.optimization_barrier((first_mine, bias_p, bias_s))
    first_other = other_core(first_mine)
    packet = pltpu.HBM((32, 2 * D + WIDE), BF16)
    own, to_left, to_above, to_diag = pl.pallas_call(
        plain_forward,
        out_shape=(packet,) * 4,
        in_specs=[SMEM] + [HBM] * 3 + [VMEM] * 2,
        out_specs=[HBM] * 4,
        scratch_shapes=[
            pltpu.VMEM((128, D), BF16),
            pltpu.VMEM((128, D), BF16),
            pltpu.VMEM((SPOTS, LANES), F32),
            pltpu.VMEM((128, 2 * D + WIDE), BF16),
            pltpu.VMEM((128, D), BF16),
            pltpu.VMEM((128, D), F32),
            pltpu.VMEM((LANES, WIDE), BF16),
            pltpu.SemaphoreType.DMA((7,)),
        ],
        compiler_params=params(),
        cost_estimate=cost(1_000_000, 1_000_000),
        name="plain_forward",
    )(core, far(tok), far(cot), far(bias_p), first_mine, first_other)
    right = from_offset(to_left, 1, 0)
    below = from_offset(to_above, 0, 1)
    diag = from_offset(to_diag, 1, 1)
    second_mine, right, below, diag = lax.optimization_barrier(
        (second_mine, right, below, diag)
    )
    second_other = other_core(second_mine)
    piece = pltpu.HBM((32, D), BF16)
    column = pltpu.HBM((64, D), BF16)
    local = pltpu.HBM((8, 2, ROWS, D), BF16)
    g_own, to_right, to_below, local = pl.pallas_call(
        lambda *refs: main_kernel(grad_scale, *refs),
        out_shape=(piece, column, piece, local),
        in_specs=[SMEM] + [HBM] * 3 + [VMEM] * 4,
        out_specs=[HBM] * 4,
        scratch_shapes=[
            pltpu.VMEM((8, SHARE + ROWS, HALF), BF16),
            pltpu.VMEM((SPOTS, LANES), F32),
            pltpu.VMEM((128, D), BF16),
            pltpu.VMEM((8, 2, ROWS, D), BF16),
            pltpu.VMEM((128, 2 * D + WIDE), BF16),
            pltpu.VMEM((128, D), BF16),
            pltpu.VMEM((128, D), BF16),
            pltpu.VMEM((128, D), F32),
            pltpu.VMEM((LANES, WIDE), BF16),
            pltpu.SemaphoreType.DMA((8,)),
        ],
        compiler_params=params(),
        cost_estimate=cost(1_000_000, 1_000_000),
        name="main",
    )(core, far(own), far(bias_s), far(second_mine), right, below, diag, second_other)

    local, to_right, to_below = lax.optimization_barrier((local, to_right, to_below))
    part = swap(local, "freq")
    column = from_offset(to_right, -1, 0)
    half = (2, ROWS, HALF)
    keep, send = pl.pallas_call(
        sum_split,
        out_shape=(jax.ShapeDtypeStruct(half, F32), jax.ShapeDtypeStruct(half, BF16)),
        in_specs=[SMEM, VMEM],
        out_specs=[VMEM] * 2,
        scratch_shapes=[pltpu.VMEM((2, ROWS, D), F32)],
        compiler_params=params(),
        name="sum_split",
    )(core, part)
    part = pl.pallas_call(
        pair_copies,
        out_shape=jax.ShapeDtypeStruct((8,) + half, BF16),
        in_specs=[VMEM] * 2,
        out_specs=VMEM,
        compiler_params=params(),
        name="pair_copies",
    )(keep, other_core(send))
    part, column, to_below = lax.optimization_barrier((part, column, to_below))
    part = swap(part, "tm", tm_groups("z"))
    row = from_offset(jnp.concatenate([to_below, column[32:64]], axis=0), 0, -1)
    part, row = lax.optimization_barrier((part, row))
    part = swap(summed(part, 4), "tm", tm_groups("y_hi"))
    grad_tokens = pl.pallas_call(
        plain_back,
        out_shape=jax.ShapeDtypeStruct((128, D), BF16),
        in_specs=[SMEM] + [HBM] * 5 + [VMEM] * 2,
        out_specs=VMEM,
        scratch_shapes=[
            pltpu.VMEM((128, D), BF16),
            pltpu.VMEM((SPOTS, LANES), F32),
            pltpu.VMEM((8, SHARE + ROWS, HALF), BF16),
            pltpu.VMEM((8, SHARE + ROWS, HALF), BF16),
            pltpu.VMEM((128, D), BF16),
            pltpu.VMEM((128, D), BF16),
            pltpu.VMEM((128, D), BF16),
            pltpu.VMEM((128, D), F32),
            pltpu.VMEM((LANES, WIDE), BF16),
            pltpu.SemaphoreType.DMA((5,)),
        ],
        compiler_params=params(),
        cost_estimate=cost(4_000_000_000, 4_000_000),
        name="plain_back",
    )(core, far(tok), far(g_own), far(bias_p), far(first_mine), far(first_other), column, row)
    part, grad_tokens = lax.optimization_barrier((part, grad_tokens))
    part = summed(part, 1)[0]
    part = lax.all_gather(part, "tm", axis_index_groups=tm_groups("core"))
    grad_plain, grad_shift = pl.pallas_call(
        finish,
        out_shape=(jax.ShapeDtypeStruct((ROWS, D), F32),) * 2,
        in_specs=[VMEM],
        out_specs=[VMEM] * 2,
        compiler_params=params(),
        name="finish",
    )(part)
    return (grad_tokens.reshape(tokens.shape), grad_plain, grad_shift)


def solution(mesh):
    placed = (
        P(None, "freq", "tm", None),
        P(None, "freq", "tm", None),
        P(None, "freq"),
        P(None, "freq"),
        P("freq", None),
        P("freq", None),
        P(),
        P(),
    )
    return jax.shard_map(
        shards,
        mesh=mesh,
        in_specs=placed,
        out_specs=(P(None, "freq", "tm", None), P("freq", None), P("freq", None)),
        check_vma=False,
    )
```

```python
import math

import jax
import jax.numpy as jnp
from jax import lax
from jax.experimental import pallas as pl
from jax.experimental.pallas import tpu as pltpu
from jax.sharding import PartitionSpec as P

D = 768
HEADS = 12
HEAD_DIM = 32
WIN = 8
SPOTS = 64
REL = 225
WIDE = HEADS * HEAD_DIM
LANES = HEADS * SPOTS
HALF = D // 2
SHARE = 144
ROWS = 48

NEG = -1e30
EPS = 1e-05
SCALE = HEAD_DIM ** (-0.5)

NN = (((1,), (0,)), ((), ()))
NT = (((1,), (1,)), ((), ()))
TN = (((0,), (0,)), ((), ()))

F32 = jnp.float32
BF16 = jnp.bfloat16


def offset_pick():
    column = lane((256, WIN * 128))
    entry = ((column >> 3) & 15) * 15 + (column & 7) - (column >> 7) + 7
    row = lax.broadcasted_iota(jnp.int32, (256, WIN * 128), 0)
    return jnp.where(row == entry, 1.0, 0.0).astype(BF16)


def dot(left, right, dims=NN):
    return lax.dot_general(left, right, dims, preferred_element_type=F32)


def normalize(values):
    center = values - jnp.mean(values, axis=-1, keepdims=True)
    rstd = lax.rsqrt(jnp.mean(center * center, axis=-1, keepdims=True) + EPS)
    return (center * rstd, rstd)


def lane(shape):
    return lax.broadcasted_iota(jnp.int32, shape, len(shape) - 1)


def quadrant_pick(transposed=False):
    row = lax.broadcasted_iota(jnp.int32, (128, 128), 1 if transposed else 0)
    column = lax.broadcasted_iota(jnp.int32, (128, 128), 0 if transposed else 1)
    high = (row & 64) >> 1
    low = (row & 32) >> 3
    spot = high + low + ((row & 12) << 1) + (row & 3) + ((row & 16) << 2)
    return jnp.where(spot == column, 1.0, 0.0).astype(BF16)


def head_mask():
    row = lax.broadcasted_iota(jnp.int32, (LANES, WIDE), 0)
    return jnp.where(row // SPOTS == lane((LANES, WIDE)) // HEAD_DIM, 1.0, 0.0).astype(BF16)


def expand(value, mask_ref):
    return jnp.concatenate([value] * HEADS, axis=0) * mask_ref[...]


def fold(full):
    head = lane((SPOTS, WIDE)) // HEAD_DIM
    out = jnp.zeros((SPOTS, WIDE), F32)
    for h in range(HEADS):
        out = out + jnp.where(head == h, full[h * SPOTS : (h + 1) * SPOTS], 0.0)
    return out


def softmax_down(scores):
    expo = jnp.exp(scores - jnp.max(scores, axis=0, keepdims=True))
    return expo / jnp.sum(expo, axis=0, keepdims=True)


def attention_back(query, key, value, d_mixed, probs, query_wide, mask_ref):
    weights = probs.astype(BF16)
    d_wide = expand(d_mixed, mask_ref)
    d_probs = dot(value, d_wide, NT)
    d_value = dot(weights, d_wide).astype(BF16)
    d_scores = (probs * (d_probs - jnp.sum(probs * d_probs, axis=0, keepdims=True))).astype(BF16)
    d_key = (dot(d_scores, query_wide) * SCALE).astype(BF16)
    d_query = (fold(dot(d_scores, key, TN)) * SCALE).astype(BF16)
    return (d_query, d_key, d_value)


def copy_all(pairs, sems, first=0):
    moves = [
        pltpu.make_async_copy(source, target, sems.at[first + i])
        for i, (source, target) in enumerate(pairs)
    ]
    for move in moves:
        move.start()
    return moves


def wait_all(moves):
    for move in moves:
        move.wait()


def prepare(core_ref, qkv, proj, out, block, sems):
    start = pl.multiple_of(core_ref[0] * HALF, 128)
    block[0:SHARE] = qkv[:, pl.ds(start, HALF)]
    block[SHARE : SHARE + ROWS] = proj[:, pl.ds(start, HALF)]
    wait_all(copy_all([(block, out.at[i]) for i in range(8)], sems))


def biases(edge_ref, table_p, table_s, to_p, to_s, out_p, out_s, tables, wide, sems):
    tables[...] = jnp.zeros_like(tables)
    tables[0:HEADS, 0:REL] = table_p[...]
    tables[HEADS : 2 * HEADS, 0:REL] = table_s[...]
    values = tables[...]
    high = values.astype(BF16)
    rest = values - high.astype(F32)
    middle = rest.astype(BF16)
    low = (rest - middle.astype(F32)).astype(BF16)
    ones = offset_pick()
    spread = (dot(high, ones) + dot(middle, ones)) + dot(low, ones)
    for row in range(2 * HEADS):
        for d in range(WIN):
            wide[row * WIN + d : row * WIN + d + 1] = spread[row : row + 1, d * 128 : (d + 1) * 128]
    left = lane((WIN, 128)) < SPOTS
    for c in range(WIN):
        move = (7 - c) * WIN
        for pair in range(HEADS // 2):
            for t, out in ((0, out_p), (1, out_s)):
                even = (t * HEADS + 2 * pair) * WIN
                first = pltpu.roll(wide[even : even + WIN], (128 - move) % 128, 1)
                second = pltpu.roll(wide[even + WIN : even + 2 * WIN], (SPOTS - move) % 128, 1)
                out[c * WIN : (c + 1) * WIN, pair * 128 : (pair + 1) * 128] = jnp.where(left, first, second)
    at = lane((SPOTS, LANES))
    key_at = lax.broadcasted_iota(jnp.int32, (SPOTS, LANES), 0)
    cross = at ^ key_at
    barred = (cross & 32) * edge_ref[0] + (cross & 4) * edge_ref[1]
    out_s[...] = jnp.where(barred != 0, NEG, out_s[...])
    wait_all(copy_all([(out_p, to_p), (out_s, to_s)], sems))


def project(rows_ref, w_mine, w_other, mine, other):
    return dot(rows_ref[:, pl.ds(mine, HALF)], w_mine, NT) + dot(
        rows_ref[:, pl.ds(other, HALF)], w_other, NT
    )


def sides(core_ref):
    mine = pl.multiple_of(core_ref[0] * HALF, 128)
    return (mine, pl.multiple_of(HALF - mine, 128))


def qkv_of(ref):
    return ref[:, 0:SHARE].reshape(3 * WIDE, HALF)


def proj_of(ref):
    return ref[:, SHARE : SHARE + ROWS].reshape(WIDE, HALF)


def input_grad(grad, normed, rstd, d_packed, w_mine, w_other, mine, other, sums):
    sums[:, pl.ds(mine, HALF)] = dot(d_packed, w_mine)
    sums[:, pl.ds(other, HALF)] = dot(d_packed, w_other)
    d_normed = sums[...]
    d_input = rstd * (
        d_normed
        - jnp.mean(d_normed, axis=-1, keepdims=True)
        - normed * jnp.mean(d_normed * normed, axis=-1, keepdims=True)
    )
    return (grad + d_input).astype(BF16)


def plain_forward(
    core_ref,
    tok_far,
    cot_far,
    bias_far,
    w_mine_ref,
    w_other_ref,
    out_o,
    out_r,
    out_b,
    out_d,
    tok,
    cot,
    bias_p,
    packets,
    rows,
    sums,
    mask,
    sems,
):
    mine, other = sides(core_ref)
    loads = copy_all([(tok_far, tok), (bias_far, bias_p), (cot_far, cot)], sems)
    mask[...] = head_mask()
    loads[0].wait()
    inputs = tok[...].astype(F32)
    rows[...] = normalize(inputs)[0].astype(BF16)
    w_mine, w_other = qkv_of(w_mine_ref), qkv_of(w_other_ref)
    packed = project(rows, w_mine, w_other, mine, other).astype(BF16)
    loads[1].wait()
    mixed = []
    for s in range(2):
        part = packed[s * SPOTS : (s + 1) * SPOTS]
        query, key, value = part[:, :WIDE], part[:, WIDE : 2 * WIDE], part[:, 2 * WIDE :]
        probs = softmax_down(dot(key, expand(query, mask), NT) * SCALE + bias_p[...])
        mixed.append(fold(dot(probs.astype(BF16), value, TN)).astype(BF16))
    mixed = jnp.concatenate(mixed, axis=0)
    sums[:, pl.ds(mine, HALF)] = dot(mixed, proj_of(w_mine_ref))
    sums[:, pl.ds(other, HALF)] = dot(mixed, proj_of(w_other_ref))
    block_out = (inputs + sums[...]).astype(BF16)
    pick = quadrant_pick()
    loads[2].wait()
    for whole, first in ((block_out, 0), (mixed, D), (cot[...], D + WIDE)):
        packets[:, first : first + whole.shape[1]] = dot(pick, whole).astype(BF16)
    outs = (out_d, out_b, out_r, out_o)
    wait_all(copy_all([(packets.at[i * 32 : (i + 1) * 32], out) for i, out in enumerate(outs)], sems, 3))


def main_kernel(
    grad_scale,
    core_ref,
    own_far,
    bias_far,
    right,
    below,
    diag,
    w_mine_ref,
    w_other_ref,
    to_own,
    to_column,
    to_below,
    out_keep,
    out_send,
    bias_s,
    quads,
    staged,
    rows_small,
    grads,
    sums,
    mask,
    sems,
):
    mine, other = sides(core_ref)
    loads = copy_all([(own_far, staged.at[0:32]), (bias_far, bias_s)], sems)
    mask[...] = head_mask()
    for i, part in ((1, right), (2, below), (3, diag)):
        staged[i * 32 : (i + 1) * 32] = part[...]
    wait_all(loads)
    pick = quadrant_pick(True)
    grads[...] = dot(pick, staged[:, D + WIDE :]).astype(BF16)
    block_out = dot(pick, staged[:, 0:D])
    mixed_plain = dot(pick, staged[:, D : D + WIDE]).astype(BF16)
    normed, rstd = normalize(block_out)
    rows_small[...] = normed.astype(BF16)
    w_mine, w_other = qkv_of(w_mine_ref), qkv_of(w_other_ref)
    packed = project(rows_small, w_mine, w_other, mine, other).astype(BF16)
    d_mixed = project(grads, proj_of(w_mine_ref), proj_of(w_other_ref), mine, other).astype(BF16)
    mixed, d_packed = [], []
    for s in range(2):
        part = packed[s * SPOTS : (s + 1) * SPOTS]
        query, key, value = part[:, :WIDE], part[:, WIDE : 2 * WIDE], part[:, 2 * WIDE :]
        query_wide = expand(query, mask)
        probs = softmax_down(dot(key, query_wide, NT) * SCALE + bias_s[...])
        mixed.append(fold(dot(probs.astype(BF16), value, TN)).astype(BF16))
        back = attention_back(
            query, key, value, d_mixed[s * SPOTS : (s + 1) * SPOTS], probs, query_wide, mask
        )
        d_packed.append(jnp.concatenate(back, axis=1))
    mixed_shift = jnp.concatenate(mixed, axis=0)
    d_packed = jnp.concatenate(d_packed, axis=0)
    grad = input_grad(
        grads[...].astype(F32), normed, rstd, d_packed, w_mine, w_other, mine, other, sums
    )
    quads[...] = dot(quadrant_pick(), grad).astype(BF16)
    stores = copy_all(
        [
            (quads.at[0:32], to_own),
            (quads.at[32:64], to_column.at[0:32]),
            (quads.at[96:128], to_column.at[32:64]),
            (quads.at[64:96], to_below),
        ],
        sems,
        2,
    )
    rows_small[...] = grad
    for out, start in ((out_send, other), (out_keep, mine)):
        part = dot(mixed_shift, grads[:, pl.ds(start, HALF)], TN) * grad_scale
        out[:, 1] = part.astype(BF16).reshape(8, ROWS, HALF)
        part = dot(mixed_plain, rows_small[:, pl.ds(start, HALF)], TN) * grad_scale
        out[:, 0] = part.astype(BF16).reshape(8, ROWS, HALF)
    wait_all(stores)


def sum_copies(parts, out):
    value = jnp.sum(parts[...].astype(F32), axis=0).astype(BF16)
    for i in range(out.shape[0]):
        out[i] = value


def finish(parts, out_plain, out_shift):
    for i, out in enumerate((out_plain, out_shift)):
        out[:, 0:HALF] = parts[0, i].astype(F32)
        out[:, HALF:D] = parts[1, i].astype(F32)


def plain_back(
    core_ref,
    tok_far,
    own_far,
    bias_far,
    mine_far,
    other_far,
    column,
    row,
    out,
    tok,
    bias_p,
    w_mine_ref,
    w_other_ref,
    staged,
    rows,
    grads,
    sums,
    mask,
    sems,
):
    mine, other = sides(core_ref)
    loads = copy_all(
        [
            (tok_far, tok),
            (mine_far, w_mine_ref),
            (other_far, w_other_ref),
            (own_far, staged.at[96:128]),
            (bias_far, bias_p),
        ],
        sems,
    )
    mask[...] = head_mask()
    staged[0:32] = row[32:64]
    staged[32:64] = row[0:32]
    staged[64:96] = column[0:32]
    loads[0].wait()
    normed, rstd = normalize(tok[...].astype(F32))
    rows[...] = normed.astype(BF16)
    wait_all(loads[1:])
    w_mine, w_other = qkv_of(w_mine_ref), qkv_of(w_other_ref)
    packed = project(rows, w_mine, w_other, mine, other).astype(BF16)
    gathered = dot(quadrant_pick(True), staged[...])
    grads[...] = gathered.astype(BF16)
    d_mixed = project(grads, proj_of(w_mine_ref), proj_of(w_other_ref), mine, other).astype(BF16)
    d_packed = []
    for s in range(2):
        part = packed[s * SPOTS : (s + 1) * SPOTS]
        query, key, value = part[:, :WIDE], part[:, WIDE : 2 * WIDE], part[:, 2 * WIDE :]
        query_wide = expand(query, mask)
        probs = softmax_down(dot(key, query_wide, NT) * SCALE + bias_p[...])
        back = attention_back(
            query, key, value, d_mixed[s * SPOTS : (s + 1) * SPOTS], probs, query_wide, mask
        )
        d_packed.append(jnp.concatenate(back, axis=1))
    d_packed = jnp.concatenate(d_packed, axis=0)
    out[...] = input_grad(gathered, normed, rstd, d_packed, w_mine, w_other, mine, other, sums)


VMEM = pl.BlockSpec(memory_space=pltpu.VMEM)
SMEM = pl.BlockSpec(memory_space=pltpu.SMEM)
HBM = pl.BlockSpec(memory_space=pltpu.HBM)


def params(size=32):
    return pltpu.CompilerParams(vmem_limit_bytes=size * 1024 * 1024)


def far(value):
    return pltpu.with_memory_space_constraint(value, pltpu.HBM)


def cost(flops, size):
    return pl.CostEstimate(flops=flops, bytes_accessed=size, transcendentals=0)


def tm_groups(bits):
    size = lax.axis_size("tm")
    step = {"core": 1, "y_hi": 2, "z": 8}[bits]
    count = {"core": 2, "y_hi": 4, "z": 8}[bits]
    groups = []
    for first in range(size):
        if (first // step) % count == 0:
            groups.append([first + step * i for i in range(count)])
    return groups


def swap(value, axis, groups=None):
    return lax.all_to_all(value, axis, 0, 0, axis_index_groups=groups)


def from_offset(value, along_tm, along_freq):
    n_tm, n_freq = lax.axis_size("tm"), lax.axis_size("freq")
    pairs = []
    for t in range(n_tm):
        for f in range(n_freq):
            source = ((t + along_tm) % n_tm) * n_freq + (f + along_freq) % n_freq
            pairs.append((source, t * n_freq + f))
    return lax.ppermute(value, ("tm", "freq"), pairs)


def other_core(value):
    return lax.ppermute(value, "tm", [(i, i ^ 1) for i in range(lax.axis_size("tm"))])


def summed(parts, count):
    return pl.pallas_call(
        sum_copies,
        out_shape=jax.ShapeDtypeStruct((count,) + parts.shape[1:], BF16),
        in_specs=[VMEM],
        out_specs=VMEM,
        compiler_params=params(),
        name="sum_copies",
    )(parts)


def shards(
    tokens, cotangent, qkv_plain, qkv_shift, proj_plain, proj_shift, table_plain, table_shift
):
    core = (lax.axis_index("tm") % 2).astype(jnp.int32).reshape(1)
    last_freq = lax.axis_index("freq") == lax.axis_size("freq") - 1
    last_time = lax.axis_index("tm") == lax.axis_size("tm") - 1
    edge = jnp.stack([last_freq, last_time]).astype(jnp.int32)
    grad_scale = 1.0 / math.sqrt(128 * lax.axis_size("tm") * lax.axis_size("freq"))
    tok = tokens.reshape(128, D)
    cot = cotangent.reshape(128, D)

    def share(qkv, proj):
        return pl.pallas_call(
            prepare,
            out_shape=pltpu.HBM((8, SHARE + ROWS, HALF), BF16),
            in_specs=[SMEM, VMEM, VMEM],
            out_specs=HBM,
            scratch_shapes=[
                pltpu.VMEM((SHARE + ROWS, HALF), BF16),
                pltpu.SemaphoreType.DMA((8,)),
            ],
            compiler_params=params(60),
            name="prepare",
        )(core, qkv.T, proj)

    first_mine = swap(share(qkv_plain, proj_plain), "freq")
    second_share = share(qkv_shift, proj_shift)
    table = pltpu.HBM((SPOTS, LANES), F32)
    bias_p, bias_s = pl.pallas_call(
        biases,
        out_shape=(table, table),
        in_specs=[SMEM, VMEM, VMEM],
        out_specs=[HBM] * 2,
        scratch_shapes=[
            pltpu.VMEM((SPOTS, LANES), F32),
            pltpu.VMEM((SPOTS, LANES), F32),
            pltpu.VMEM((32, 256), F32),
            pltpu.VMEM((2 * HEADS * WIN, 128), F32),
            pltpu.SemaphoreType.DMA((2,)),
        ],
        compiler_params=params(),
        name="biases",
    )(edge, table_plain, table_shift)

    first_mine, second_share, bias_p, bias_s = lax.optimization_barrier(
        (first_mine, second_share, bias_p, bias_s)
    )
    second_mine = swap(second_share, "freq")
    first_other = other_core(first_mine)
    packet = pltpu.HBM((32, 2 * D + WIDE), BF16)
    own, to_left, to_above, to_diag = pl.pallas_call(
        plain_forward,
        out_shape=(packet,) * 4,
        in_specs=[SMEM] + [HBM] * 3 + [VMEM] * 2,
        out_specs=[HBM] * 4,
        scratch_shapes=[
            pltpu.VMEM((128, D), BF16),
            pltpu.VMEM((128, D), BF16),
            pltpu.VMEM((SPOTS, LANES), F32),
            pltpu.VMEM((128, 2 * D + WIDE), BF16),
            pltpu.VMEM((128, D), BF16),
            pltpu.VMEM((128, D), F32),
            pltpu.VMEM((LANES, WIDE), BF16),
            pltpu.SemaphoreType.DMA((7,)),
        ],
        compiler_params=params(),
        cost_estimate=cost(1_000_000, 1_000_000),
        name="plain_forward",
    )(core, far(tok), far(cot), far(bias_p), first_mine, first_other)
    right = from_offset(to_left, 1, 0)
    below = from_offset(to_above, 0, 1)
    diag = from_offset(to_diag, 1, 1)
    second_mine, right, below, diag = lax.optimization_barrier(
        (second_mine, right, below, diag)
    )
    second_other = other_core(second_mine)
    piece = pltpu.HBM((32, D), BF16)
    column = pltpu.HBM((64, D), BF16)
    local = jax.ShapeDtypeStruct((8, 2, ROWS, HALF), BF16)
    g_own, to_right, to_below, keep, send = pl.pallas_call(
        lambda *refs: main_kernel(grad_scale, *refs),
        out_shape=(piece, column, piece, local, local),
        in_specs=[SMEM] + [HBM] * 2 + [VMEM] * 5,
        out_specs=[HBM] * 3 + [VMEM] * 2,
        scratch_shapes=[
            pltpu.VMEM((SPOTS, LANES), F32),
            pltpu.VMEM((128, D), BF16),
            pltpu.VMEM((128, 2 * D + WIDE), BF16),
            pltpu.VMEM((128, D), BF16),
            pltpu.VMEM((128, D), BF16),
            pltpu.VMEM((128, D), F32),
            pltpu.VMEM((LANES, WIDE), BF16),
            pltpu.SemaphoreType.DMA((6,)),
        ],
        compiler_params=params(),
        cost_estimate=cost(1_000_000, 1_000_000),
        name="main",
    )(core, far(own), far(bias_s), right, below, diag, second_mine, second_other)

    part = (keep.astype(F32) + other_core(send).astype(F32)).astype(BF16)
    part, to_right, to_below = lax.optimization_barrier((part, to_right, to_below))
    part = swap(part, "freq")
    column = from_offset(to_right, -1, 0)
    part, column, to_below = lax.optimization_barrier((part, column, to_below))
    part = swap(summed(part, 4), "tm", tm_groups("y_hi"))
    row = from_offset(jnp.concatenate([to_below, column[32:64]], axis=0), 0, -1)
    part, row = lax.optimization_barrier((part, row))
    part = swap(summed(part, 8), "tm", tm_groups("z"))
    grad_tokens = pl.pallas_call(
        plain_back,
        out_shape=jax.ShapeDtypeStruct((128, D), BF16),
        in_specs=[SMEM] + [HBM] * 5 + [VMEM] * 2,
        out_specs=VMEM,
        scratch_shapes=[
            pltpu.VMEM((128, D), BF16),
            pltpu.VMEM((SPOTS, LANES), F32),
            pltpu.VMEM((8, SHARE + ROWS, HALF), BF16),
            pltpu.VMEM((8, SHARE + ROWS, HALF), BF16),
            pltpu.VMEM((128, D), BF16),
            pltpu.VMEM((128, D), BF16),
            pltpu.VMEM((128, D), BF16),
            pltpu.VMEM((128, D), F32),
            pltpu.VMEM((LANES, WIDE), BF16),
            pltpu.SemaphoreType.DMA((5,)),
        ],
        compiler_params=params(),
        cost_estimate=cost(4_000_000_000, 4_000_000),
        name="plain_back",
    )(core, far(tok), far(g_own), far(bias_p), far(first_mine), far(first_other), column, row)
    part, grad_tokens = lax.optimization_barrier((part, grad_tokens))
    part = summed(part, 1)[0]
    part = lax.all_gather(part, "tm", axis_index_groups=tm_groups("core"))
    grad_plain, grad_shift = pl.pallas_call(
        finish,
        out_shape=(jax.ShapeDtypeStruct((ROWS, D), F32),) * 2,
        in_specs=[VMEM],
        out_specs=[VMEM] * 2,
        compiler_params=params(),
        name="finish",
    )(part)
    return (grad_tokens.reshape(tokens.shape), grad_plain, grad_shift)


def solution(mesh):
    placed = (
        P(None, "freq", "tm", None),
        P(None, "freq", "tm", None),
        P(None, "freq"),
        P(None, "freq"),
        P("freq", None),
        P("freq", None),
        P(),
        P(),
    )
    return jax.shard_map(
        shards,
        mesh=mesh,
        in_specs=placed,
        out_specs=(P(None, "freq", "tm", None), P("freq", None), P("freq", None)),
        check_vma=False,
    )
```

```python
import math

import jax
import jax.numpy as jnp
from jax import lax
from jax.experimental import pallas as pl
from jax.experimental.pallas import tpu as pltpu
from jax.sharding import PartitionSpec as P

D = 768
HEADS = 12
HEAD_DIM = 32
WIN = 8
SPOTS = 64
REL = 225
WIDE = HEADS * HEAD_DIM
LANES = HEADS * SPOTS
HALF = D // 2
SHARE = 144
ROWS = 48

NEG = -1e30
EPS = 1e-05
SCALE = HEAD_DIM ** (-0.5)

NN = (((1,), (0,)), ((), ()))
NT = (((1,), (1,)), ((), ()))
TN = (((0,), (0,)), ((), ()))

F32 = jnp.float32
BF16 = jnp.bfloat16


def offset_pick():
    column = lane((256, WIN * 128))
    entry = ((column >> 3) & 15) * 15 + (column & 7) - (column >> 7) + 7
    row = lax.broadcasted_iota(jnp.int32, (256, WIN * 128), 0)
    return jnp.where(row == entry, 1.0, 0.0).astype(BF16)


def dot(left, right, dims=NN):
    return lax.dot_general(left, right, dims, preferred_element_type=F32)


def normalize(values):
    center = values - jnp.mean(values, axis=-1, keepdims=True)
    rstd = lax.rsqrt(jnp.mean(center * center, axis=-1, keepdims=True) + EPS)
    return (center * rstd, rstd)


def lane(shape):
    return lax.broadcasted_iota(jnp.int32, shape, len(shape) - 1)


def quadrant_pick(transposed=False):
    row = lax.broadcasted_iota(jnp.int32, (128, 128), 1 if transposed else 0)
    column = lax.broadcasted_iota(jnp.int32, (128, 128), 0 if transposed else 1)
    high = (row & 64) >> 1
    low = (row & 32) >> 3
    spot = high + low + ((row & 12) << 1) + (row & 3) + ((row & 16) << 2)
    return jnp.where(spot == column, 1.0, 0.0).astype(BF16)


def head_mask():
    row = lax.broadcasted_iota(jnp.int32, (LANES, WIDE), 0)
    return jnp.where(row // SPOTS == lane((LANES, WIDE)) // HEAD_DIM, 1.0, 0.0).astype(BF16)


def expand(value, mask_ref):
    return jnp.concatenate([value] * HEADS, axis=0) * mask_ref[...]


def fold(full):
    head = lane((SPOTS, WIDE)) // HEAD_DIM
    out = jnp.zeros((SPOTS, WIDE), F32)
    for h in range(HEADS):
        out = out + jnp.where(head == h, full[h * SPOTS : (h + 1) * SPOTS], 0.0)
    return out


def softmax_down(scores):
    expo = jnp.exp(scores - jnp.max(scores, axis=0, keepdims=True))
    return expo / jnp.sum(expo, axis=0, keepdims=True)


def attention_back(query, key, value, d_mixed, probs, query_wide, mask_ref):
    weights = probs.astype(BF16)
    d_wide = expand(d_mixed, mask_ref)
    d_probs = dot(value, d_wide, NT)
    d_value = dot(weights, d_wide).astype(BF16)
    d_scores = (probs * (d_probs - jnp.sum(probs * d_probs, axis=0, keepdims=True))).astype(BF16)
    d_key = (dot(d_scores, query_wide) * SCALE).astype(BF16)
    d_query = (fold(dot(d_scores, key, TN)) * SCALE).astype(BF16)
    return (d_query, d_key, d_value)


def copy_all(pairs, sems, first=0):
    moves = [
        pltpu.make_async_copy(source, target, sems.at[first + i])
        for i, (source, target) in enumerate(pairs)
    ]
    for move in moves:
        move.start()
    return moves


def wait_all(moves):
    for move in moves:
        move.wait()


def prepare(core_ref, qkv, proj, out, block, sems):
    start = pl.multiple_of(core_ref[0] * HALF, 128)
    block[0:SHARE] = qkv[:, pl.ds(start, HALF)]
    block[SHARE : SHARE + ROWS] = proj[:, pl.ds(start, HALF)]
    wait_all(copy_all([(block, out.at[i]) for i in range(8)], sems))


def biases(edge_ref, table_p, table_s, to_p, to_s, out_p, out_s, tables, wide, sems):
    tables[...] = jnp.zeros_like(tables)
    tables[0:HEADS, 0:REL] = table_p[...]
    tables[HEADS : 2 * HEADS, 0:REL] = table_s[...]
    values = tables[...]
    high = values.astype(BF16)
    rest = values - high.astype(F32)
    middle = rest.astype(BF16)
    low = (rest - middle.astype(F32)).astype(BF16)
    ones = offset_pick()
    spread = (dot(high, ones) + dot(middle, ones)) + dot(low, ones)
    for row in range(2 * HEADS):
        for d in range(WIN):
            wide[row * WIN + d : row * WIN + d + 1] = spread[row : row + 1, d * 128 : (d + 1) * 128]
    left = lane((WIN, 128)) < SPOTS
    for c in range(WIN):
        move = (7 - c) * WIN
        for pair in range(HEADS // 2):
            for t, out in ((0, out_p), (1, out_s)):
                even = (t * HEADS + 2 * pair) * WIN
                first = pltpu.roll(wide[even : even + WIN], (128 - move) % 128, 1)
                second = pltpu.roll(wide[even + WIN : even + 2 * WIN], (SPOTS - move) % 128, 1)
                out[c * WIN : (c + 1) * WIN, pair * 128 : (pair + 1) * 128] = jnp.where(left, first, second)
    at = lane((SPOTS, LANES))
    key_at = lax.broadcasted_iota(jnp.int32, (SPOTS, LANES), 0)
    cross = at ^ key_at
    barred = (cross & 32) * edge_ref[0] + (cross & 4) * edge_ref[1]
    out_s[...] = jnp.where(barred != 0, NEG, out_s[...])
    wait_all(copy_all([(out_p, to_p), (out_s, to_s)], sems))


def project(rows_ref, w_mine, w_other, mine, other):
    return dot(rows_ref[:, pl.ds(mine, HALF)], w_mine, NT) + dot(
        rows_ref[:, pl.ds(other, HALF)], w_other, NT
    )


def sides(core_ref):
    mine = pl.multiple_of(core_ref[0] * HALF, 128)
    return (mine, pl.multiple_of(HALF - mine, 128))


def qkv_of(ref):
    return ref[:, 0:SHARE].reshape(3 * WIDE, HALF)


def proj_of(ref):
    return ref[:, SHARE : SHARE + ROWS].reshape(WIDE, HALF)


def input_grad(grad, normed, rstd, d_packed, w_mine, w_other, mine, other, sums):
    sums[:, pl.ds(mine, HALF)] = dot(d_packed, w_mine)
    sums[:, pl.ds(other, HALF)] = dot(d_packed, w_other)
    d_normed = sums[...]
    d_input = rstd * (
        d_normed
        - jnp.mean(d_normed, axis=-1, keepdims=True)
        - normed * jnp.mean(d_normed * normed, axis=-1, keepdims=True)
    )
    return (grad + d_input).astype(BF16)


def plain_forward(
    core_ref,
    tok_far,
    cot_far,
    bias_far,
    w_mine_ref,
    w_other_ref,
    out_o,
    out_r,
    out_b,
    out_d,
    tok,
    cot,
    bias_p,
    packets,
    rows,
    sums,
    mask,
    sems,
):
    mine, other = sides(core_ref)
    loads = copy_all([(tok_far, tok), (bias_far, bias_p), (cot_far, cot)], sems)
    mask[...] = head_mask()
    loads[0].wait()
    inputs = tok[...].astype(F32)
    rows[...] = normalize(inputs)[0].astype(BF16)
    w_mine, w_other = qkv_of(w_mine_ref), qkv_of(w_other_ref)
    packed = project(rows, w_mine, w_other, mine, other).astype(BF16)
    loads[1].wait()
    mixed = []
    for s in range(2):
        part = packed[s * SPOTS : (s + 1) * SPOTS]
        query, key, value = part[:, :WIDE], part[:, WIDE : 2 * WIDE], part[:, 2 * WIDE :]
        probs = softmax_down(dot(key, expand(query, mask), NT) * SCALE + bias_p[...])
        mixed.append(fold(dot(probs.astype(BF16), value, TN)).astype(BF16))
    mixed = jnp.concatenate(mixed, axis=0)
    sums[:, pl.ds(mine, HALF)] = dot(mixed, proj_of(w_mine_ref))
    sums[:, pl.ds(other, HALF)] = dot(mixed, proj_of(w_other_ref))
    block_out = (inputs + sums[...]).astype(BF16)
    pick = quadrant_pick()
    loads[2].wait()
    for whole, first in ((block_out, 0), (mixed, D), (cot[...], D + WIDE)):
        packets[:, first : first + whole.shape[1]] = dot(pick, whole).astype(BF16)
    outs = (out_d, out_b, out_r, out_o)
    wait_all(copy_all([(packets.at[i * 32 : (i + 1) * 32], out) for i, out in enumerate(outs)], sems, 3))


def main_kernel(
    grad_scale,
    core_ref,
    own_far,
    bias_far,
    right,
    below,
    diag,
    w_mine_ref,
    w_other_ref,
    to_own,
    to_column,
    to_below,
    out_keep,
    out_send,
    bias_s,
    quads,
    staged,
    rows_small,
    grads,
    sums,
    mask,
    sems,
):
    mine, other = sides(core_ref)
    loads = copy_all([(own_far, staged.at[0:32]), (bias_far, bias_s)], sems)
    mask[...] = head_mask()
    for i, part in ((1, right), (2, below), (3, diag)):
        staged[i * 32 : (i + 1) * 32] = part[...]
    wait_all(loads)
    pick = quadrant_pick(True)
    grads[...] = dot(pick, staged[:, D + WIDE :]).astype(BF16)
    block_out = dot(pick, staged[:, 0:D])
    mixed_plain = dot(pick, staged[:, D : D + WIDE]).astype(BF16)
    normed, rstd = normalize(block_out)
    rows_small[...] = normed.astype(BF16)
    w_mine, w_other = qkv_of(w_mine_ref), qkv_of(w_other_ref)
    packed = project(rows_small, w_mine, w_other, mine, other).astype(BF16)
    d_mixed = project(grads, proj_of(w_mine_ref), proj_of(w_other_ref), mine, other).astype(BF16)
    mixed, d_packed = [], []
    for s in range(2):
        part = packed[s * SPOTS : (s + 1) * SPOTS]
        query, key, value = part[:, :WIDE], part[:, WIDE : 2 * WIDE], part[:, 2 * WIDE :]
        query_wide = expand(query, mask)
        probs = softmax_down(dot(key, query_wide, NT) * SCALE + bias_s[...])
        mixed.append(fold(dot(probs.astype(BF16), value, TN)).astype(BF16))
        back = attention_back(
            query, key, value, d_mixed[s * SPOTS : (s + 1) * SPOTS], probs, query_wide, mask
        )
        d_packed.append(jnp.concatenate(back, axis=1))
    mixed_shift = jnp.concatenate(mixed, axis=0)
    d_packed = jnp.concatenate(d_packed, axis=0)
    grad = input_grad(
        grads[...].astype(F32), normed, rstd, d_packed, w_mine, w_other, mine, other, sums
    )
    quads[...] = dot(quadrant_pick(), grad).astype(BF16)
    stores = copy_all(
        [
            (quads.at[0:32], to_own),
            (quads.at[32:64], to_column.at[0:32]),
            (quads.at[96:128], to_column.at[32:64]),
            (quads.at[64:96], to_below),
        ],
        sems,
        2,
    )
    rows_small[...] = grad
    for out, start in ((out_send, other), (out_keep, mine)):
        part = dot(mixed_shift, grads[:, pl.ds(start, HALF)], TN) * grad_scale
        out[:, 1] = part.astype(BF16).reshape(8, ROWS, HALF)
        part = dot(mixed_plain, rows_small[:, pl.ds(start, HALF)], TN) * grad_scale
        out[:, 0] = part.astype(BF16).reshape(8, ROWS, HALF)
    wait_all(stores)


def sum_copies(parts, out):
    value = jnp.sum(parts[...].astype(F32), axis=0).astype(BF16)
    for i in range(out.shape[0]):
        out[i] = value


def finish(parts, out_plain, out_shift):
    for i, out in enumerate((out_plain, out_shift)):
        out[:, 0:HALF] = parts[0, i].astype(F32)
        out[:, HALF:D] = parts[1, i].astype(F32)


def plain_back(
    core_ref,
    tok_far,
    own_far,
    bias_far,
    mine_far,
    other_far,
    column,
    row,
    out,
    tok,
    bias_p,
    w_mine_ref,
    w_other_ref,
    staged,
    rows,
    grads,
    sums,
    mask,
    sems,
):
    mine, other = sides(core_ref)
    loads = copy_all(
        [
            (tok_far, tok),
            (mine_far, w_mine_ref),
            (other_far, w_other_ref),
            (own_far, staged.at[96:128]),
            (bias_far, bias_p),
        ],
        sems,
    )
    mask[...] = head_mask()
    staged[0:32] = row[32:64]
    staged[32:64] = row[0:32]
    staged[64:96] = column[0:32]
    loads[0].wait()
    normed, rstd = normalize(tok[...].astype(F32))
    rows[...] = normed.astype(BF16)
    wait_all(loads[1:])
    w_mine, w_other = qkv_of(w_mine_ref), qkv_of(w_other_ref)
    packed = project(rows, w_mine, w_other, mine, other).astype(BF16)
    gathered = dot(quadrant_pick(True), staged[...])
    grads[...] = gathered.astype(BF16)
    d_mixed = project(grads, proj_of(w_mine_ref), proj_of(w_other_ref), mine, other).astype(BF16)
    d_packed = []
    for s in range(2):
        part = packed[s * SPOTS : (s + 1) * SPOTS]
        query, key, value = part[:, :WIDE], part[:, WIDE : 2 * WIDE], part[:, 2 * WIDE :]
        query_wide = expand(query, mask)
        probs = softmax_down(dot(key, query_wide, NT) * SCALE + bias_p[...])
        back = attention_back(
            query, key, value, d_mixed[s * SPOTS : (s + 1) * SPOTS], probs, query_wide, mask
        )
        d_packed.append(jnp.concatenate(back, axis=1))
    d_packed = jnp.concatenate(d_packed, axis=0)
    out[...] = input_grad(gathered, normed, rstd, d_packed, w_mine, w_other, mine, other, sums)


VMEM = pl.BlockSpec(memory_space=pltpu.VMEM)
SMEM = pl.BlockSpec(memory_space=pltpu.SMEM)
HBM = pl.BlockSpec(memory_space=pltpu.HBM)


def params(size=32):
    return pltpu.CompilerParams(vmem_limit_bytes=size * 1024 * 1024)


def far(value):
    return pltpu.with_memory_space_constraint(value, pltpu.HBM)


def cost(flops, size):
    return pl.CostEstimate(flops=flops, bytes_accessed=size, transcendentals=0)


def tm_groups(bits):
    size = lax.axis_size("tm")
    step = {"core": 1, "y_hi": 2, "z": 8}[bits]
    count = {"core": 2, "y_hi": 4, "z": 8}[bits]
    groups = []
    for first in range(size):
        if (first // step) % count == 0:
            groups.append([first + step * i for i in range(count)])
    return groups


def swap(value, axis, groups=None):
    return lax.all_to_all(value, axis, 0, 0, axis_index_groups=groups)


def from_offset(value, along_tm, along_freq):
    n_tm, n_freq = lax.axis_size("tm"), lax.axis_size("freq")
    pairs = []
    for t in range(n_tm):
        for f in range(n_freq):
            source = ((t + along_tm) % n_tm) * n_freq + (f + along_freq) % n_freq
            pairs.append((source, t * n_freq + f))
    return lax.ppermute(value, ("tm", "freq"), pairs)


def other_core(value):
    return lax.ppermute(value, "tm", [(i, i ^ 1) for i in range(lax.axis_size("tm"))])


def summed(parts, count):
    return pl.pallas_call(
        sum_copies,
        out_shape=jax.ShapeDtypeStruct((count,) + parts.shape[1:], BF16),
        in_specs=[VMEM],
        out_specs=VMEM,
        compiler_params=params(),
        name="sum_copies",
    )(parts)


def shards(
    tokens, cotangent, qkv_plain, qkv_shift, proj_plain, proj_shift, table_plain, table_shift
):
    core = (lax.axis_index("tm") % 2).astype(jnp.int32).reshape(1)
    last_freq = lax.axis_index("freq") == lax.axis_size("freq") - 1
    last_time = lax.axis_index("tm") == lax.axis_size("tm") - 1
    edge = jnp.stack([last_freq, last_time]).astype(jnp.int32)
    grad_scale = 1.0 / math.sqrt(128 * lax.axis_size("tm") * lax.axis_size("freq"))
    tok = tokens.reshape(128, D)
    cot = cotangent.reshape(128, D)

    def share(qkv, proj):
        return pl.pallas_call(
            prepare,
            out_shape=pltpu.HBM((8, SHARE + ROWS, HALF), BF16),
            in_specs=[SMEM, VMEM, VMEM],
            out_specs=HBM,
            scratch_shapes=[
                pltpu.VMEM((SHARE + ROWS, HALF), BF16),
                pltpu.SemaphoreType.DMA((8,)),
            ],
            compiler_params=params(60),
            name="prepare",
        )(core, qkv.T, proj)

    first_mine = swap(share(qkv_plain, proj_plain), "freq")
    second_share = share(qkv_shift, proj_shift)
    table = pltpu.HBM((SPOTS, LANES), F32)
    bias_p, bias_s = pl.pallas_call(
        biases,
        out_shape=(table, table),
        in_specs=[SMEM, VMEM, VMEM],
        out_specs=[HBM] * 2,
        scratch_shapes=[
            pltpu.VMEM((SPOTS, LANES), F32),
            pltpu.VMEM((SPOTS, LANES), F32),
            pltpu.VMEM((32, 256), F32),
            pltpu.VMEM((2 * HEADS * WIN, 128), F32),
            pltpu.SemaphoreType.DMA((2,)),
        ],
        compiler_params=params(),
        name="biases",
    )(edge, table_plain, table_shift)

    first_mine, second_share, bias_p, bias_s = lax.optimization_barrier(
        (first_mine, second_share, bias_p, bias_s)
    )
    second_mine = swap(second_share, "freq")
    first_other = other_core(first_mine)
    packet = pltpu.HBM((32, 2 * D + WIDE), BF16)
    own, to_left, to_above, to_diag = pl.pallas_call(
        plain_forward,
        out_shape=(packet,) * 4,
        in_specs=[SMEM] + [HBM] * 3 + [VMEM] * 2,
        out_specs=[HBM] * 4,
        scratch_shapes=[
            pltpu.VMEM((128, D), BF16),
            pltpu.VMEM((128, D), BF16),
            pltpu.VMEM((SPOTS, LANES), F32),
            pltpu.VMEM((128, 2 * D + WIDE), BF16),
            pltpu.VMEM((128, D), BF16),
            pltpu.VMEM((128, D), F32),
            pltpu.VMEM((LANES, WIDE), BF16),
            pltpu.SemaphoreType.DMA((7,)),
        ],
        compiler_params=params(),
        cost_estimate=cost(20_000_000_000, 1_000_000),
        name="plain_forward",
    )(core, far(tok), far(cot), far(bias_p), first_mine, first_other)
    right = from_offset(to_left, 1, 0)
    below = from_offset(to_above, 0, 1)
    diag = from_offset(to_diag, 1, 1)
    second_mine, right, below, diag = lax.optimization_barrier(
        (second_mine, right, below, diag)
    )
    second_other = other_core(second_mine)
    piece = pltpu.HBM((32, D), BF16)
    column = pltpu.HBM((64, D), BF16)
    local = jax.ShapeDtypeStruct((8, 2, ROWS, HALF), BF16)
    g_own, to_right, to_below, keep, send = pl.pallas_call(
        lambda *refs: main_kernel(grad_scale, *refs),
        out_shape=(piece, column, piece, local, local),
        in_specs=[SMEM] + [HBM] * 2 + [VMEM] * 5,
        out_specs=[HBM] * 3 + [VMEM] * 2,
        scratch_shapes=[
            pltpu.VMEM((SPOTS, LANES), F32),
            pltpu.VMEM((128, D), BF16),
            pltpu.VMEM((128, 2 * D + WIDE), BF16),
            pltpu.VMEM((128, D), BF16),
            pltpu.VMEM((128, D), BF16),
            pltpu.VMEM((128, D), F32),
            pltpu.VMEM((LANES, WIDE), BF16),
            pltpu.SemaphoreType.DMA((6,)),
        ],
        compiler_params=params(),
        cost_estimate=cost(1_000_000, 1_000_000),
        name="main",
    )(core, far(own), far(bias_s), right, below, diag, second_mine, second_other)

    part = (keep.astype(F32) + other_core(send).astype(F32)).astype(BF16)
    part, to_right, to_below = lax.optimization_barrier((part, to_right, to_below))
    part = swap(part, "freq")
    column = from_offset(to_right, -1, 0)
    part, column, to_below = lax.optimization_barrier((part, column, to_below))
    part = swap(summed(part, 4), "tm", tm_groups("y_hi"))
    row = from_offset(jnp.concatenate([to_below, column[32:64]], axis=0), 0, -1)
    part, row = lax.optimization_barrier((part, row))
    part = swap(summed(part, 8), "tm", tm_groups("z"))
    grad_tokens = pl.pallas_call(
        plain_back,
        out_shape=jax.ShapeDtypeStruct((128, D), BF16),
        in_specs=[SMEM] + [HBM] * 5 + [VMEM] * 2,
        out_specs=VMEM,
        scratch_shapes=[
            pltpu.VMEM((128, D), BF16),
            pltpu.VMEM((SPOTS, LANES), F32),
            pltpu.VMEM((8, SHARE + ROWS, HALF), BF16),
            pltpu.VMEM((8, SHARE + ROWS, HALF), BF16),
            pltpu.VMEM((128, D), BF16),
            pltpu.VMEM((128, D), BF16),
            pltpu.VMEM((128, D), BF16),
            pltpu.VMEM((128, D), F32),
            pltpu.VMEM((LANES, WIDE), BF16),
            pltpu.SemaphoreType.DMA((5,)),
        ],
        compiler_params=params(),
        cost_estimate=cost(4_000_000_000, 4_000_000),
        name="plain_back",
    )(core, far(tok), far(g_own), far(bias_p), far(first_mine), far(first_other), column, row)
    part, grad_tokens = lax.optimization_barrier((part, grad_tokens))
    part = summed(part, 1)[0]
    part = lax.all_gather(part, "tm", axis_index_groups=tm_groups("core"))
    grad_plain, grad_shift = pl.pallas_call(
        finish,
        out_shape=(jax.ShapeDtypeStruct((ROWS, D), F32),) * 2,
        in_specs=[VMEM],
        out_specs=[VMEM] * 2,
        compiler_params=params(),
        name="finish",
    )(part)
    return (grad_tokens.reshape(tokens.shape), grad_plain, grad_shift)


def solution(mesh):
    placed = (
        P(None, "freq", "tm", None),
        P(None, "freq", "tm", None),
        P(None, "freq"),
        P(None, "freq"),
        P("freq", None),
        P("freq", None),
        P(),
        P(),
    )
    return jax.shard_map(
        shards,
        mesh=mesh,
        in_specs=placed,
        out_specs=(P(None, "freq", "tm", None), P("freq", None), P("freq", None)),
        check_vma=False,
    )
```

```python
import math

import jax
import jax.numpy as jnp
from jax import lax
from jax.experimental import pallas as pl
from jax.experimental.pallas import tpu as pltpu
from jax.sharding import PartitionSpec as P

D = 768
HEADS = 12
HEAD_DIM = 32
WIN = 8
SPOTS = 64
REL = 225
WIDE = HEADS * HEAD_DIM
LANES = HEADS * SPOTS
HALF = D // 2
SHARE = 144
ROWS = 48
PART = SHARE + ROWS

NEG = -1e30
EPS = 1e-05
SCALE = HEAD_DIM ** (-0.5)

NN = (((1,), (0,)), ((), ()))
NT = (((1,), (1,)), ((), ()))
TN = (((0,), (0,)), ((), ()))

F32 = jnp.float32
BF16 = jnp.bfloat16


def offset_pick():
    column = lane((256, WIN * 128))
    entry = ((column >> 3) & 15) * 15 + (column & 7) - (column >> 7) + 7
    row = lax.broadcasted_iota(jnp.int32, (256, WIN * 128), 0)
    return jnp.where(row == entry, 1.0, 0.0).astype(BF16)


def dot(left, right, dims=NN):
    return lax.dot_general(left, right, dims, preferred_element_type=F32)


def normalize(values):
    center = values - jnp.mean(values, axis=-1, keepdims=True)
    rstd = lax.rsqrt(jnp.mean(center * center, axis=-1, keepdims=True) + EPS)
    return (center * rstd, rstd)


def lane(shape):
    return lax.broadcasted_iota(jnp.int32, shape, len(shape) - 1)


def quadrant_pick(transposed=False):
    row = lax.broadcasted_iota(jnp.int32, (128, 128), 1 if transposed else 0)
    column = lax.broadcasted_iota(jnp.int32, (128, 128), 0 if transposed else 1)
    high = (row & 64) >> 1
    low = (row & 32) >> 3
    spot = high + low + ((row & 12) << 1) + (row & 3) + ((row & 16) << 2)
    return jnp.where(spot == column, 1.0, 0.0).astype(BF16)


def head_mask():
    row = lax.broadcasted_iota(jnp.int32, (LANES, WIDE), 0)
    return jnp.where(row // SPOTS == lane((LANES, WIDE)) // HEAD_DIM, 1.0, 0.0).astype(BF16)


def expand(value, mask_ref):
    return jnp.concatenate([value] * HEADS, axis=0) * mask_ref[...]


def fold(full):
    head = lane((SPOTS, WIDE)) // HEAD_DIM
    out = jnp.zeros((SPOTS, WIDE), F32)
    for h in range(HEADS):
        out = out + jnp.where(head == h, full[h * SPOTS : (h + 1) * SPOTS], 0.0)
    return out


def softmax_down(scores):
    expo = jnp.exp(scores - jnp.max(scores, axis=0, keepdims=True))
    return expo / jnp.sum(expo, axis=0, keepdims=True)


def attention_back(query, key, value, d_mixed, probs, query_wide, mask_ref):
    weights = probs.astype(BF16)
    d_wide = expand(d_mixed, mask_ref)
    d_probs = dot(value, d_wide, NT)
    d_value = dot(weights, d_wide).astype(BF16)
    d_scores = (probs * (d_probs - jnp.sum(probs * d_probs, axis=0, keepdims=True))).astype(BF16)
    d_key = (dot(d_scores, query_wide) * SCALE).astype(BF16)
    d_query = (fold(dot(d_scores, key, TN)) * SCALE).astype(BF16)
    return (d_query, d_key, d_value)


def copy_all(pairs, sems, first=0):
    moves = [
        pltpu.make_async_copy(source, target, sems.at[first + i])
        for i, (source, target) in enumerate(pairs)
    ]
    for move in moves:
        move.start()
    return moves


def wait_all(moves):
    for move in moves:
        move.wait()


def prepare(core_ref, qkv_p, proj_p, qkv_s, proj_s, out, block, sems):
    start = pl.multiple_of(core_ref[0] * HALF, 128)
    for first, qkv, proj in ((0, qkv_p, proj_p), (PART, qkv_s, proj_s)):
        block[first : first + SHARE] = qkv[:, pl.ds(start, HALF)]
        block[first + SHARE : first + PART] = proj[:, pl.ds(start, HALF)]
    wait_all(copy_all([(block, out.at[i]) for i in range(8)], sems))


def biases(edge_ref, table_p, table_s, to_p, to_s, out_p, out_s, tables, wide, sems):
    tables[...] = jnp.zeros_like(tables)
    tables[0:HEADS, 0:REL] = table_p[...]
    tables[HEADS : 2 * HEADS, 0:REL] = table_s[...]
    values = tables[...]
    high = values.astype(BF16)
    rest = values - high.astype(F32)
    middle = rest.astype(BF16)
    low = (rest - middle.astype(F32)).astype(BF16)
    ones = offset_pick()
    spread = (dot(high, ones) + dot(middle, ones)) + dot(low, ones)
    for row in range(2 * HEADS):
        for d in range(WIN):
            wide[row * WIN + d : row * WIN + d + 1] = spread[row : row + 1, d * 128 : (d + 1) * 128]
    left = lane((WIN, 128)) < SPOTS
    for c in range(WIN):
        move = (7 - c) * WIN
        for pair in range(HEADS // 2):
            for t, out in ((0, out_p), (1, out_s)):
                even = (t * HEADS + 2 * pair) * WIN
                first = pltpu.roll(wide[even : even + WIN], (128 - move) % 128, 1)
                second = pltpu.roll(wide[even + WIN : even + 2 * WIN], (SPOTS - move) % 128, 1)
                out[c * WIN : (c + 1) * WIN, pair * 128 : (pair + 1) * 128] = jnp.where(left, first, second)
    at = lane((SPOTS, LANES))
    key_at = lax.broadcasted_iota(jnp.int32, (SPOTS, LANES), 0)
    cross = at ^ key_at
    barred = (cross & 32) * edge_ref[0] + (cross & 4) * edge_ref[1]
    out_s[...] = jnp.where(barred != 0, NEG, out_s[...])
    wait_all(copy_all([(out_p, to_p), (out_s, to_s)], sems))


def project(rows_ref, w_mine, w_other, mine, other):
    return dot(rows_ref[:, pl.ds(mine, HALF)], w_mine, NT) + dot(
        rows_ref[:, pl.ds(other, HALF)], w_other, NT
    )


def sides(core_ref):
    mine = pl.multiple_of(core_ref[0] * HALF, 128)
    return (mine, pl.multiple_of(HALF - mine, 128))


def qkv_of(ref, first=0):
    return ref[:, first : first + SHARE].reshape(3 * WIDE, HALF)


def proj_of(ref, first=0):
    return ref[:, first + SHARE : first + PART].reshape(WIDE, HALF)


def input_grad(grad, normed, rstd, d_packed, w_mine, w_other, mine, other, sums):
    sums[:, pl.ds(mine, HALF)] = dot(d_packed, w_mine)
    sums[:, pl.ds(other, HALF)] = dot(d_packed, w_other)
    d_normed = sums[...]
    d_input = rstd * (
        d_normed
        - jnp.mean(d_normed, axis=-1, keepdims=True)
        - normed * jnp.mean(d_normed * normed, axis=-1, keepdims=True)
    )
    return (grad + d_input).astype(BF16)


def plain_begin(
    core_ref,
    tok_far,
    cot_far,
    bias_p_far,
    bias_s_far,
    w_mine_ref,
    out_tok,
    out_cot,
    out_rows,
    out_part,
    out_bias_p,
    out_bias_s,
    cot,
    sems,
):
    mine, _ = sides(core_ref)
    loads = copy_all(
        [(tok_far, out_tok), (cot_far, cot), (bias_p_far, out_bias_p), (bias_s_far, out_bias_s)],
        sems,
    )
    loads[0].wait()
    out_rows[...] = normalize(out_tok[...].astype(F32))[0].astype(BF16)
    out_part[...] = dot(out_rows[:, pl.ds(mine, HALF)], qkv_of(w_mine_ref), NT)
    loads[1].wait()
    out_cot[...] = dot(quadrant_pick(), cot[...]).astype(BF16)
    wait_all(loads[2:])


def plain_forward(
    core_ref,
    tok,
    cot_quads,
    rows,
    part,
    bias_p,
    w_mine_ref,
    w_other_ref,
    out_o,
    out_r,
    out_b,
    out_d,
    sums,
    mask,
):
    mine, other = sides(core_ref)
    mask[...] = head_mask()
    packed = part[...] + dot(rows[:, pl.ds(other, HALF)], qkv_of(w_other_ref), NT)
    packed = packed.astype(BF16)
    mixed = []
    for s in range(2):
        block = packed[s * SPOTS : (s + 1) * SPOTS]
        query, key, value = block[:, :WIDE], block[:, WIDE : 2 * WIDE], block[:, 2 * WIDE :]
        probs = softmax_down(dot(key, expand(query, mask), NT) * SCALE + bias_p[...])
        mixed.append(fold(dot(probs.astype(BF16), value, TN)).astype(BF16))
    mixed = jnp.concatenate(mixed, axis=0)
    sums[:, pl.ds(mine, HALF)] = dot(mixed, proj_of(w_mine_ref))
    sums[:, pl.ds(other, HALF)] = dot(mixed, proj_of(w_other_ref))
    block_out = (tok[...].astype(F32) + sums[...]).astype(BF16)
    pick = quadrant_pick()
    outs = (out_d, out_b, out_r, out_o)
    for whole, first in ((block_out, 0), (mixed, D)):
        quads = dot(pick, whole).astype(BF16)
        for i, out in enumerate(outs):
            out[:, first : first + whole.shape[1]] = quads[i * 32 : (i + 1) * 32]
    for i, out in enumerate(outs):
        out[:, D + WIDE :] = cot_quads[i * 32 : (i + 1) * 32]


def main_kernel(
    grad_scale,
    core_ref,
    own,
    right,
    below,
    diag,
    w_mine_ref,
    w_other_ref,
    bias_s,
    to_own,
    to_column,
    to_below,
    out_keep,
    out_send,
    quads,
    staged,
    rows_small,
    grads,
    sums,
    mask,
    sems,
):
    mine, other = sides(core_ref)
    mask[...] = head_mask()
    for i, part in enumerate((own, right, below, diag)):
        staged[i * 32 : (i + 1) * 32] = part[...]
    pick = quadrant_pick(True)
    grads[...] = dot(pick, staged[:, D + WIDE :]).astype(BF16)
    block_out = dot(pick, staged[:, 0:D])
    mixed_plain = dot(pick, staged[:, D : D + WIDE]).astype(BF16)
    normed, rstd = normalize(block_out)
    rows_small[...] = normed.astype(BF16)
    w_mine, w_other = qkv_of(w_mine_ref, PART), qkv_of(w_other_ref, PART)
    packed = project(rows_small, w_mine, w_other, mine, other).astype(BF16)
    d_mixed = project(grads, proj_of(w_mine_ref, PART), proj_of(w_other_ref, PART), mine, other).astype(BF16)
    mixed, d_packed = [], []
    for s in range(2):
        part = packed[s * SPOTS : (s + 1) * SPOTS]
        query, key, value = part[:, :WIDE], part[:, WIDE : 2 * WIDE], part[:, 2 * WIDE :]
        query_wide = expand(query, mask)
        probs = softmax_down(dot(key, query_wide, NT) * SCALE + bias_s[...])
        mixed.append(fold(dot(probs.astype(BF16), value, TN)).astype(BF16))
        back = attention_back(
            query, key, value, d_mixed[s * SPOTS : (s + 1) * SPOTS], probs, query_wide, mask
        )
        d_packed.append(jnp.concatenate(back, axis=1))
    mixed_shift = jnp.concatenate(mixed, axis=0)
    d_packed = jnp.concatenate(d_packed, axis=0)
    grad = input_grad(
        grads[...].astype(F32), normed, rstd, d_packed, w_mine, w_other, mine, other, sums
    )
    quads[...] = dot(quadrant_pick(), grad).astype(BF16)
    stores = copy_all(
        [
            (quads.at[0:32], to_own),
            (quads.at[32:64], to_column.at[0:32]),
            (quads.at[96:128], to_column.at[32:64]),
            (quads.at[64:96], to_below),
        ],
        sems,
    )
    rows_small[...] = grad
    for out, start in ((out_send, other), (out_keep, mine)):
        part = dot(mixed_shift, grads[:, pl.ds(start, HALF)], TN) * grad_scale
        out[:, 1] = part.astype(BF16).reshape(8, ROWS, HALF)
        part = dot(mixed_plain, rows_small[:, pl.ds(start, HALF)], TN) * grad_scale
        out[:, 0] = part.astype(BF16).reshape(8, ROWS, HALF)
    wait_all(stores)


def sum_copies(parts, out):
    value = jnp.sum(parts[...].astype(F32), axis=0).astype(BF16)
    for i in range(out.shape[0]):
        out[i] = value


def finish(parts, out_plain, out_shift):
    for i, out in enumerate((out_plain, out_shift)):
        out[:, 0:HALF] = parts[0, i].astype(F32)
        out[:, HALF:D] = parts[1, i].astype(F32)


def plain_back(
    core_ref,
    tok_far,
    own_far,
    bias_far,
    mine_far,
    other_far,
    column,
    row,
    out,
    tok,
    bias_p,
    w_mine_ref,
    w_other_ref,
    staged,
    rows,
    grads,
    sums,
    mask,
    sems,
):
    mine, other = sides(core_ref)
    loads = copy_all(
        [
            (tok_far, tok),
            (mine_far.at[:, 0:PART], w_mine_ref),
            (other_far.at[:, 0:PART], w_other_ref),
            (own_far, staged.at[96:128]),
            (bias_far, bias_p),
        ],
        sems,
    )
    mask[...] = head_mask()
    staged[0:32] = row[32:64]
    staged[32:64] = row[0:32]
    staged[64:96] = column[0:32]
    loads[0].wait()
    normed, rstd = normalize(tok[...].astype(F32))
    rows[...] = normed.astype(BF16)
    wait_all(loads[1:])
    w_mine, w_other = qkv_of(w_mine_ref), qkv_of(w_other_ref)
    packed = project(rows, w_mine, w_other, mine, other).astype(BF16)
    gathered = dot(quadrant_pick(True), staged[...])
    grads[...] = gathered.astype(BF16)
    d_mixed = project(grads, proj_of(w_mine_ref), proj_of(w_other_ref), mine, other).astype(BF16)
    d_packed = []
    for s in range(2):
        part = packed[s * SPOTS : (s + 1) * SPOTS]
        query, key, value = part[:, :WIDE], part[:, WIDE : 2 * WIDE], part[:, 2 * WIDE :]
        query_wide = expand(query, mask)
        probs = softmax_down(dot(key, query_wide, NT) * SCALE + bias_p[...])
        back = attention_back(
            query, key, value, d_mixed[s * SPOTS : (s + 1) * SPOTS], probs, query_wide, mask
        )
        d_packed.append(jnp.concatenate(back, axis=1))
    d_packed = jnp.concatenate(d_packed, axis=0)
    out[...] = input_grad(gathered, normed, rstd, d_packed, w_mine, w_other, mine, other, sums)


VMEM = pl.BlockSpec(memory_space=pltpu.VMEM)
SMEM = pl.BlockSpec(memory_space=pltpu.SMEM)
HBM = pl.BlockSpec(memory_space=pltpu.HBM)


def params(size=32):
    return pltpu.CompilerParams(vmem_limit_bytes=size * 1024 * 1024)


def far(value):
    return pltpu.with_memory_space_constraint(value, pltpu.HBM)


def cost(flops, size):
    return pl.CostEstimate(flops=flops, bytes_accessed=size, transcendentals=0)


def tm_groups(bits):
    size = lax.axis_size("tm")
    step = {"core": 1, "y_hi": 2, "z": 8}[bits]
    count = {"core": 2, "y_hi": 4, "z": 8}[bits]
    groups = []
    for first in range(size):
        if (first // step) % count == 0:
            groups.append([first + step * i for i in range(count)])
    return groups


def swap(value, axis, groups=None):
    return lax.all_to_all(value, axis, 0, 0, axis_index_groups=groups)


def from_offset(value, along_tm, along_freq):
    n_tm, n_freq = lax.axis_size("tm"), lax.axis_size("freq")
    pairs = []
    for t in range(n_tm):
        for f in range(n_freq):
            source = ((t + along_tm) % n_tm) * n_freq + (f + along_freq) % n_freq
            pairs.append((source, t * n_freq + f))
    return lax.ppermute(value, ("tm", "freq"), pairs)


def other_core(value):
    return lax.ppermute(value, "tm", [(i, i ^ 1) for i in range(lax.axis_size("tm"))])


def summed(parts, count):
    return pl.pallas_call(
        sum_copies,
        out_shape=jax.ShapeDtypeStruct((count,) + parts.shape[1:], BF16),
        in_specs=[VMEM],
        out_specs=VMEM,
        compiler_params=params(),
        name="sum_copies",
    )(parts)


def shards(
    tokens, cotangent, qkv_plain, qkv_shift, proj_plain, proj_shift, table_plain, table_shift
):
    core = (lax.axis_index("tm") % 2).astype(jnp.int32).reshape(1)
    last_freq = lax.axis_index("freq") == lax.axis_size("freq") - 1
    last_time = lax.axis_index("tm") == lax.axis_size("tm") - 1
    edge = jnp.stack([last_freq, last_time]).astype(jnp.int32)
    grad_scale = 1.0 / math.sqrt(128 * lax.axis_size("tm") * lax.axis_size("freq"))
    tok = tokens.reshape(128, D)
    cot = cotangent.reshape(128, D)

    shares = pl.pallas_call(
        prepare,
        out_shape=pltpu.HBM((8, 2 * PART, HALF), BF16),
        in_specs=[SMEM] + [VMEM] * 4,
        out_specs=HBM,
        scratch_shapes=[pltpu.VMEM((2 * PART, HALF), BF16), pltpu.SemaphoreType.DMA((8,))],
        compiler_params=params(60),
        name="prepare",
    )(core, qkv_plain.T, proj_plain, qkv_shift.T, proj_shift)
    w_mine = swap(shares, "freq")

    table = pltpu.HBM((SPOTS, LANES), F32)
    bias_p, bias_s = pl.pallas_call(
        biases,
        out_shape=(table, table),
        in_specs=[SMEM, VMEM, VMEM],
        out_specs=[HBM] * 2,
        scratch_shapes=[
            pltpu.VMEM((SPOTS, LANES), F32),
            pltpu.VMEM((SPOTS, LANES), F32),
            pltpu.VMEM((32, 256), F32),
            pltpu.VMEM((2 * HEADS * WIN, 128), F32),
            pltpu.SemaphoreType.DMA((2,)),
        ],
        compiler_params=params(),
        name="biases",
    )(edge, table_plain, table_shift)

    w_mine, bias_p, bias_s = lax.optimization_barrier((w_mine, bias_p, bias_s))
    w_other = other_core(w_mine)
    tile = jax.ShapeDtypeStruct((128, D), BF16)
    near_table = jax.ShapeDtypeStruct((SPOTS, LANES), F32)
    near_tok, near_cot, rows, part, near_p, near_s = pl.pallas_call(
        plain_begin,
        out_shape=(
            tile,
            tile,
            tile,
            jax.ShapeDtypeStruct((128, 3 * WIDE), F32),
            near_table,
            near_table,
        ),
        in_specs=[SMEM] + [HBM] * 4 + [VMEM],
        out_specs=[VMEM] * 6,
        scratch_shapes=[pltpu.VMEM((128, D), BF16), pltpu.SemaphoreType.DMA((4,))],
        compiler_params=params(),
        cost_estimate=cost(5_000_000_000, 1_000_000),
        name="plain_begin",
    )(core, far(tok), far(cot), far(bias_p), far(bias_s), w_mine)
    packet = jax.ShapeDtypeStruct((32, 2 * D + WIDE), BF16)
    own, to_left, to_above, to_diag = pl.pallas_call(
        plain_forward,
        out_shape=(packet,) * 4,
        in_specs=[SMEM] + [VMEM] * 7,
        out_specs=[VMEM] * 4,
        scratch_shapes=[pltpu.VMEM((128, D), F32), pltpu.VMEM((LANES, WIDE), BF16)],
        compiler_params=params(),
        cost_estimate=cost(1_000_000, 1_000_000),
        name="plain_forward",
    )(core, near_tok, near_cot, rows, part, near_p, w_mine, w_other)
    right = from_offset(to_left, 1, 0)
    below = from_offset(to_above, 0, 1)
    diag = from_offset(to_diag, 1, 1)
    piece = pltpu.HBM((32, D), BF16)
    column = pltpu.HBM((64, D), BF16)
    local = jax.ShapeDtypeStruct((8, 2, ROWS, HALF), BF16)
    g_own, to_right, to_below, keep, send = pl.pallas_call(
        lambda *refs: main_kernel(grad_scale, *refs),
        out_shape=(piece, column, piece, local, local),
        in_specs=[SMEM] + [VMEM] * 7,
        out_specs=[HBM] * 3 + [VMEM] * 2,
        scratch_shapes=[
            pltpu.VMEM((128, D), BF16),
            pltpu.VMEM((128, 2 * D + WIDE), BF16),
            pltpu.VMEM((128, D), BF16),
            pltpu.VMEM((128, D), BF16),
            pltpu.VMEM((128, D), F32),
            pltpu.VMEM((LANES, WIDE), BF16),
            pltpu.SemaphoreType.DMA((4,)),
        ],
        compiler_params=params(),
        cost_estimate=cost(1_000_000, 1_000_000),
        name="main",
    )(core, own, right, below, diag, w_mine, w_other, near_s)

    part = (keep.astype(F32) + other_core(send).astype(F32)).astype(BF16)
    part, to_right, to_below = lax.optimization_barrier((part, to_right, to_below))
    part = swap(part, "freq")
    column = from_offset(to_right, -1, 0)
    part, column, to_below = lax.optimization_barrier((part, column, to_below))
    part = swap(summed(part, 4), "tm", tm_groups("y_hi"))
    row = from_offset(jnp.concatenate([to_below, column[32:64]], axis=0), 0, -1)
    part, row = lax.optimization_barrier((part, row))
    part = swap(summed(part, 8), "tm", tm_groups("z"))
    grad_tokens = pl.pallas_call(
        plain_back,
        out_shape=jax.ShapeDtypeStruct((128, D), BF16),
        in_specs=[SMEM] + [HBM] * 5 + [VMEM] * 2,
        out_specs=VMEM,
        scratch_shapes=[
            pltpu.VMEM((128, D), BF16),
            pltpu.VMEM((SPOTS, LANES), F32),
            pltpu.VMEM((8, SHARE + ROWS, HALF), BF16),
            pltpu.VMEM((8, SHARE + ROWS, HALF), BF16),
            pltpu.VMEM((128, D), BF16),
            pltpu.VMEM((128, D), BF16),
            pltpu.VMEM((128, D), BF16),
            pltpu.VMEM((128, D), F32),
            pltpu.VMEM((LANES, WIDE), BF16),
            pltpu.SemaphoreType.DMA((5,)),
        ],
        compiler_params=params(),
        cost_estimate=cost(4_000_000_000, 4_000_000),
        name="plain_back",
    )(core, far(tok), far(g_own), far(bias_p), far(w_mine), far(w_other), column, row)
    part, grad_tokens = lax.optimization_barrier((part, grad_tokens))
    part = summed(part, 1)[0]
    part = lax.all_gather(part, "tm", axis_index_groups=tm_groups("core"))
    grad_plain, grad_shift = pl.pallas_call(
        finish,
        out_shape=(jax.ShapeDtypeStruct((ROWS, D), F32),) * 2,
        in_specs=[VMEM],
        out_specs=[VMEM] * 2,
        compiler_params=params(),
        name="finish",
    )(part)
    return (grad_tokens.reshape(tokens.shape), grad_plain, grad_shift)


def solution(mesh):
    placed = (
        P(None, "freq", "tm", None),
        P(None, "freq", "tm", None),
        P(None, "freq"),
        P(None, "freq"),
        P("freq", None),
        P("freq", None),
        P(),
        P(),
    )
    return jax.shard_map(
        shards,
        mesh=mesh,
        in_specs=placed,
        out_specs=(P(None, "freq", "tm", None), P("freq", None), P("freq", None)),
        check_vma=False,
    )
```

```python
import math

import jax
import jax.numpy as jnp
from jax import lax
from jax.experimental import pallas as pl
from jax.experimental.pallas import tpu as pltpu
from jax.sharding import PartitionSpec as P

D = 768
HEADS = 12
HEAD_DIM = 32
WIN = 8
SPOTS = 64
REL = 225
WIDE = HEADS * HEAD_DIM
LANES = HEADS * SPOTS
HALF = D // 2
SHARE = 144
ROWS = 48

NEG = -1e30
EPS = 1e-05
SCALE = HEAD_DIM ** (-0.5)

NN = (((1,), (0,)), ((), ()))
NT = (((1,), (1,)), ((), ()))
TN = (((0,), (0,)), ((), ()))

F32 = jnp.float32
BF16 = jnp.bfloat16


def offset_pick():
    column = lane((256, WIN * 128))
    entry = ((column >> 3) & 15) * 15 + (column & 7) - (column >> 7) + 7
    row = lax.broadcasted_iota(jnp.int32, (256, WIN * 128), 0)
    return jnp.where(row == entry, 1.0, 0.0).astype(BF16)


def dot(left, right, dims=NN):
    return lax.dot_general(left, right, dims, preferred_element_type=F32)


def normalize(values):
    center = values - jnp.mean(values, axis=-1, keepdims=True)
    rstd = lax.rsqrt(jnp.mean(center * center, axis=-1, keepdims=True) + EPS)
    return (center * rstd, rstd)


def lane(shape):
    return lax.broadcasted_iota(jnp.int32, shape, len(shape) - 1)


def quadrant_pick(transposed=False):
    row = lax.broadcasted_iota(jnp.int32, (128, 128), 1 if transposed else 0)
    column = lax.broadcasted_iota(jnp.int32, (128, 128), 0 if transposed else 1)
    high = (row & 64) >> 1
    low = (row & 32) >> 3
    spot = high + low + ((row & 12) << 1) + (row & 3) + ((row & 16) << 2)
    return jnp.where(spot == column, 1.0, 0.0).astype(BF16)


def head_mask():
    row = lax.broadcasted_iota(jnp.int32, (LANES, WIDE), 0)
    return jnp.where(row // SPOTS == lane((LANES, WIDE)) // HEAD_DIM, 1.0, 0.0).astype(BF16)


def expand(value, mask_ref):
    return jnp.concatenate([value] * HEADS, axis=0) * mask_ref[...]


def fold(full):
    head = lane((SPOTS, WIDE)) // HEAD_DIM
    out = jnp.zeros((SPOTS, WIDE), F32)
    for h in range(HEADS):
        out = out + jnp.where(head == h, full[h * SPOTS : (h + 1) * SPOTS], 0.0)
    return out


def softmax_down(scores):
    expo = jnp.exp(scores - jnp.max(scores, axis=0, keepdims=True))
    return expo / jnp.sum(expo, axis=0, keepdims=True)


def attention_back(query, key, value, d_mixed, probs, query_wide, mask_ref):
    weights = probs.astype(BF16)
    d_wide = expand(d_mixed, mask_ref)
    d_probs = dot(value, d_wide, NT)
    d_value = dot(weights, d_wide).astype(BF16)
    d_scores = (probs * (d_probs - jnp.sum(probs * d_probs, axis=0, keepdims=True))).astype(BF16)
    d_key = (dot(d_scores, query_wide) * SCALE).astype(BF16)
    d_query = (fold(dot(d_scores, key, TN)) * SCALE).astype(BF16)
    return (d_query, d_key, d_value)


def copy_all(pairs, sems, first=0):
    moves = [
        pltpu.make_async_copy(source, target, sems.at[first + i])
        for i, (source, target) in enumerate(pairs)
    ]
    for move in moves:
        move.start()
    return moves


def wait_all(moves):
    for move in moves:
        move.wait()


def prepare(core_ref, qkv, proj, out, block, sems):
    start = pl.multiple_of(core_ref[0] * HALF, 128)
    block[0:SHARE] = qkv[:, pl.ds(start, HALF)]
    block[SHARE : SHARE + ROWS] = proj[:, pl.ds(start, HALF)]
    wait_all(copy_all([(block, out.at[i]) for i in range(8)], sems))


def biases(edge_ref, table_p, table_s, to_p, to_s, out_p, out_s, tables, wide, sems):
    tables[...] = jnp.zeros_like(tables)
    tables[0:HEADS, 0:REL] = table_p[...]
    tables[HEADS : 2 * HEADS, 0:REL] = table_s[...]
    values = tables[...]
    high = values.astype(BF16)
    rest = values - high.astype(F32)
    middle = rest.astype(BF16)
    low = (rest - middle.astype(F32)).astype(BF16)
    ones = offset_pick()
    spread = (dot(high, ones) + dot(middle, ones)) + dot(low, ones)
    for row in range(2 * HEADS):
        for d in range(WIN):
            wide[row * WIN + d : row * WIN + d + 1] = spread[row : row + 1, d * 128 : (d + 1) * 128]
    left = lane((WIN, 128)) < SPOTS
    for c in range(WIN):
        move = (7 - c) * WIN
        for pair in range(HEADS // 2):
            for t, out in ((0, out_p), (1, out_s)):
                even = (t * HEADS + 2 * pair) * WIN
                first = pltpu.roll(wide[even : even + WIN], (128 - move) % 128, 1)
                second = pltpu.roll(wide[even + WIN : even + 2 * WIN], (SPOTS - move) % 128, 1)
                out[c * WIN : (c + 1) * WIN, pair * 128 : (pair + 1) * 128] = jnp.where(left, first, second)
    at = lane((SPOTS, LANES))
    key_at = lax.broadcasted_iota(jnp.int32, (SPOTS, LANES), 0)
    cross = at ^ key_at
    barred = (cross & 32) * edge_ref[0] + (cross & 4) * edge_ref[1]
    out_s[...] = jnp.where(barred != 0, NEG, out_s[...])
    wait_all(copy_all([(out_p, to_p), (out_s, to_s)], sems))


def project(rows_ref, w_mine, w_other, mine, other):
    return dot(rows_ref[:, pl.ds(mine, HALF)], w_mine, NT) + dot(
        rows_ref[:, pl.ds(other, HALF)], w_other, NT
    )


def sides(core_ref):
    mine = pl.multiple_of(core_ref[0] * HALF, 128)
    return (mine, pl.multiple_of(HALF - mine, 128))


def qkv_of(ref):
    return ref[:, 0:SHARE].reshape(3 * WIDE, HALF)


def proj_of(ref):
    return ref[:, SHARE : SHARE + ROWS].reshape(WIDE, HALF)


def input_grad(grad, normed, rstd, d_packed, w_mine, w_other, mine, other, sums):
    sums[:, pl.ds(mine, HALF)] = dot(d_packed, w_mine)
    sums[:, pl.ds(other, HALF)] = dot(d_packed, w_other)
    d_normed = sums[...]
    d_input = rstd * (
        d_normed
        - jnp.mean(d_normed, axis=-1, keepdims=True)
        - normed * jnp.mean(d_normed * normed, axis=-1, keepdims=True)
    )
    return (grad + d_input).astype(BF16)


def plain_forward(
    core_ref,
    tok_far,
    cot_far,
    bias_far,
    w_mine_ref,
    w_other_ref,
    out_own,
    out_top,
    out_column,
    tok,
    cot,
    bias_p,
    packets,
    rows,
    sums,
    mask,
    sems,
):
    mine, other = sides(core_ref)
    loads = copy_all([(tok_far, tok), (bias_far, bias_p), (cot_far, cot)], sems)
    mask[...] = head_mask()
    loads[0].wait()
    inputs = tok[...].astype(F32)
    rows[...] = normalize(inputs)[0].astype(BF16)
    w_mine, w_other = qkv_of(w_mine_ref), qkv_of(w_other_ref)
    packed = project(rows, w_mine, w_other, mine, other).astype(BF16)
    loads[1].wait()
    mixed = []
    for s in range(2):
        part = packed[s * SPOTS : (s + 1) * SPOTS]
        query, key, value = part[:, :WIDE], part[:, WIDE : 2 * WIDE], part[:, 2 * WIDE :]
        probs = softmax_down(dot(key, expand(query, mask), NT) * SCALE + bias_p[...])
        mixed.append(fold(dot(probs.astype(BF16), value, TN)).astype(BF16))
    mixed = jnp.concatenate(mixed, axis=0)
    sums[:, pl.ds(mine, HALF)] = dot(mixed, proj_of(w_mine_ref))
    sums[:, pl.ds(other, HALF)] = dot(mixed, proj_of(w_other_ref))
    block_out = (inputs + sums[...]).astype(BF16)
    pick = quadrant_pick()
    loads[2].wait()
    for whole, first in ((block_out, 0), (mixed, D), (cot[...], D + WIDE)):
        packets[:, first : first + whole.shape[1]] = dot(pick, whole).astype(BF16)
    stores = [
        (packets.at[0:32], out_column.at[0:32]),
        (packets.at[64:96], out_column.at[32:64]),
        (packets.at[32:64], out_top),
        (packets.at[96:128], out_own),
    ]
    wait_all(copy_all(stores, sems, 3))


def main_kernel(
    grad_scale,
    core_ref,
    own_far,
    bias_far,
    right,
    below,
    w_mine_ref,
    w_other_ref,
    to_own,
    to_column,
    to_below,
    out_keep,
    out_send,
    bias_s,
    quads,
    staged,
    rows_small,
    grads,
    sums,
    mask,
    sems,
):
    mine, other = sides(core_ref)
    loads = copy_all([(own_far, staged.at[0:32]), (bias_far, bias_s)], sems)
    mask[...] = head_mask()
    staged[32:64] = right[32:64]
    staged[64:128] = below[...]
    wait_all(loads)
    pick = quadrant_pick(True)
    grads[...] = dot(pick, staged[:, D + WIDE :]).astype(BF16)
    block_out = dot(pick, staged[:, 0:D])
    mixed_plain = dot(pick, staged[:, D : D + WIDE]).astype(BF16)
    normed, rstd = normalize(block_out)
    rows_small[...] = normed.astype(BF16)
    w_mine, w_other = qkv_of(w_mine_ref), qkv_of(w_other_ref)
    packed = project(rows_small, w_mine, w_other, mine, other).astype(BF16)
    d_mixed = project(grads, proj_of(w_mine_ref), proj_of(w_other_ref), mine, other).astype(BF16)
    mixed, d_packed = [], []
    for s in range(2):
        part = packed[s * SPOTS : (s + 1) * SPOTS]
        query, key, value = part[:, :WIDE], part[:, WIDE : 2 * WIDE], part[:, 2 * WIDE :]
        query_wide = expand(query, mask)
        probs = softmax_down(dot(key, query_wide, NT) * SCALE + bias_s[...])
        mixed.append(fold(dot(probs.astype(BF16), value, TN)).astype(BF16))
        back = attention_back(
            query, key, value, d_mixed[s * SPOTS : (s + 1) * SPOTS], probs, query_wide, mask
        )
        d_packed.append(jnp.concatenate(back, axis=1))
    mixed_shift = jnp.concatenate(mixed, axis=0)
    d_packed = jnp.concatenate(d_packed, axis=0)
    grad = input_grad(
        grads[...].astype(F32), normed, rstd, d_packed, w_mine, w_other, mine, other, sums
    )
    quads[...] = dot(quadrant_pick(), grad).astype(BF16)
    stores = copy_all(
        [
            (quads.at[0:32], to_own),
            (quads.at[32:64], to_column.at[0:32]),
            (quads.at[96:128], to_column.at[32:64]),
            (quads.at[64:96], to_below),
        ],
        sems,
        2,
    )
    rows_small[...] = grad
    for out, start in ((out_send, other), (out_keep, mine)):
        part = dot(mixed_shift, grads[:, pl.ds(start, HALF)], TN) * grad_scale
        out[:, 1] = part.astype(BF16).reshape(8, ROWS, HALF)
        part = dot(mixed_plain, rows_small[:, pl.ds(start, HALF)], TN) * grad_scale
        out[:, 0] = part.astype(BF16).reshape(8, ROWS, HALF)
    wait_all(stores)


def sum_copies(parts, out):
    value = jnp.sum(parts[...].astype(F32), axis=0).astype(BF16)
    for i in range(out.shape[0]):
        out[i] = value


def finish(parts, out_plain, out_shift):
    for i, out in enumerate((out_plain, out_shift)):
        out[:, 0:HALF] = parts[0, i].astype(F32)
        out[:, HALF:D] = parts[1, i].astype(F32)


def plain_back(
    core_ref,
    tok_far,
    own_far,
    bias_far,
    mine_far,
    other_far,
    column,
    row,
    out,
    tok,
    bias_p,
    w_mine_ref,
    w_other_ref,
    staged,
    rows,
    grads,
    sums,
    mask,
    sems,
):
    mine, other = sides(core_ref)
    loads = copy_all(
        [
            (tok_far, tok),
            (mine_far, w_mine_ref),
            (other_far, w_other_ref),
            (own_far, staged.at[96:128]),
            (bias_far, bias_p),
        ],
        sems,
    )
    mask[...] = head_mask()
    staged[0:32] = row[32:64]
    staged[32:64] = row[0:32]
    staged[64:96] = column[0:32]
    loads[0].wait()
    normed, rstd = normalize(tok[...].astype(F32))
    rows[...] = normed.astype(BF16)
    wait_all(loads[1:])
    w_mine, w_other = qkv_of(w_mine_ref), qkv_of(w_other_ref)
    packed = project(rows, w_mine, w_other, mine, other).astype(BF16)
    gathered = dot(quadrant_pick(True), staged[...])
    grads[...] = gathered.astype(BF16)
    d_mixed = project(grads, proj_of(w_mine_ref), proj_of(w_other_ref), mine, other).astype(BF16)
    d_packed = []
    for s in range(2):
        part = packed[s * SPOTS : (s + 1) * SPOTS]
        query, key, value = part[:, :WIDE], part[:, WIDE : 2 * WIDE], part[:, 2 * WIDE :]
        query_wide = expand(query, mask)
        probs = softmax_down(dot(key, query_wide, NT) * SCALE + bias_p[...])
        back = attention_back(
            query, key, value, d_mixed[s * SPOTS : (s + 1) * SPOTS], probs, query_wide, mask
        )
        d_packed.append(jnp.concatenate(back, axis=1))
    d_packed = jnp.concatenate(d_packed, axis=0)
    out[...] = input_grad(gathered, normed, rstd, d_packed, w_mine, w_other, mine, other, sums)


VMEM = pl.BlockSpec(memory_space=pltpu.VMEM)
SMEM = pl.BlockSpec(memory_space=pltpu.SMEM)
HBM = pl.BlockSpec(memory_space=pltpu.HBM)


def params(size=32):
    return pltpu.CompilerParams(vmem_limit_bytes=size * 1024 * 1024)


def far(value):
    return pltpu.with_memory_space_constraint(value, pltpu.HBM)


def cost(flops, size):
    return pl.CostEstimate(flops=flops, bytes_accessed=size, transcendentals=0)


def tm_groups(bits):
    size = lax.axis_size("tm")
    step = {"core": 1, "y_hi": 2, "z": 8}[bits]
    count = {"core": 2, "y_hi": 4, "z": 8}[bits]
    groups = []
    for first in range(size):
        if (first // step) % count == 0:
            groups.append([first + step * i for i in range(count)])
    return groups


def swap(value, axis, groups=None):
    return lax.all_to_all(value, axis, 0, 0, axis_index_groups=groups)


def from_offset(value, along_tm, along_freq):
    n_tm, n_freq = lax.axis_size("tm"), lax.axis_size("freq")
    pairs = []
    for t in range(n_tm):
        for f in range(n_freq):
            source = ((t + along_tm) % n_tm) * n_freq + (f + along_freq) % n_freq
            pairs.append((source, t * n_freq + f))
    return lax.ppermute(value, ("tm", "freq"), pairs)


def other_core(value):
    return lax.ppermute(value, "tm", [(i, i ^ 1) for i in range(lax.axis_size("tm"))])


def summed(parts, count):
    return pl.pallas_call(
        sum_copies,
        out_shape=jax.ShapeDtypeStruct((count,) + parts.shape[1:], BF16),
        in_specs=[VMEM],
        out_specs=VMEM,
        compiler_params=params(),
        name="sum_copies",
    )(parts)


def shards(
    tokens, cotangent, qkv_plain, qkv_shift, proj_plain, proj_shift, table_plain, table_shift
):
    core = (lax.axis_index("tm") % 2).astype(jnp.int32).reshape(1)
    last_freq = lax.axis_index("freq") == lax.axis_size("freq") - 1
    last_time = lax.axis_index("tm") == lax.axis_size("tm") - 1
    edge = jnp.stack([last_freq, last_time]).astype(jnp.int32)
    grad_scale = 1.0 / math.sqrt(128 * lax.axis_size("tm") * lax.axis_size("freq"))
    tok = tokens.reshape(128, D)
    cot = cotangent.reshape(128, D)

    def share(qkv, proj):
        return pl.pallas_call(
            prepare,
            out_shape=pltpu.HBM((8, SHARE + ROWS, HALF), BF16),
            in_specs=[SMEM, VMEM, VMEM],
            out_specs=HBM,
            scratch_shapes=[
                pltpu.VMEM((SHARE + ROWS, HALF), BF16),
                pltpu.SemaphoreType.DMA((8,)),
            ],
            compiler_params=params(60),
            name="prepare",
        )(core, qkv.T, proj)

    first_mine = swap(share(qkv_plain, proj_plain), "freq")
    second_share = share(qkv_shift, proj_shift)
    table = pltpu.HBM((SPOTS, LANES), F32)
    bias_p, bias_s = pl.pallas_call(
        biases,
        out_shape=(table, table),
        in_specs=[SMEM, VMEM, VMEM],
        out_specs=[HBM] * 2,
        scratch_shapes=[
            pltpu.VMEM((SPOTS, LANES), F32),
            pltpu.VMEM((SPOTS, LANES), F32),
            pltpu.VMEM((32, 256), F32),
            pltpu.VMEM((2 * HEADS * WIN, 128), F32),
            pltpu.SemaphoreType.DMA((2,)),
        ],
        compiler_params=params(),
        name="biases",
    )(edge, table_plain, table_shift)

    first_mine, second_share, bias_p, bias_s = lax.optimization_barrier(
        (first_mine, second_share, bias_p, bias_s)
    )
    second_mine = swap(second_share, "freq")
    first_other = other_core(first_mine)
    packet = pltpu.HBM((32, 2 * D + WIDE), BF16)
    wide = pltpu.HBM((64, 2 * D + WIDE), BF16)
    own, to_above, to_left = pl.pallas_call(
        plain_forward,
        out_shape=(packet, packet, wide),
        in_specs=[SMEM] + [HBM] * 3 + [VMEM] * 2,
        out_specs=[HBM] * 3,
        scratch_shapes=[
            pltpu.VMEM((128, D), BF16),
            pltpu.VMEM((128, D), BF16),
            pltpu.VMEM((SPOTS, LANES), F32),
            pltpu.VMEM((128, 2 * D + WIDE), BF16),
            pltpu.VMEM((128, D), BF16),
            pltpu.VMEM((128, D), F32),
            pltpu.VMEM((LANES, WIDE), BF16),
            pltpu.SemaphoreType.DMA((7,)),
        ],
        compiler_params=params(),
        cost_estimate=cost(20_000_000_000, 1_000_000),
        name="plain_forward",
    )(core, far(tok), far(cot), far(bias_p), first_mine, first_other)
    right = from_offset(to_left, 1, 0)
    second_mine, right = lax.optimization_barrier((second_mine, right))
    below = from_offset(jnp.concatenate([to_above, right[0:32]], axis=0), 0, 1)
    second_other = other_core(second_mine)
    piece = pltpu.HBM((32, D), BF16)
    column = pltpu.HBM((64, D), BF16)
    local = jax.ShapeDtypeStruct((8, 2, ROWS, HALF), BF16)
    g_own, to_right, to_below, keep, send = pl.pallas_call(
        lambda *refs: main_kernel(grad_scale, *refs),
        out_shape=(piece, column, piece, local, local),
        in_specs=[SMEM] + [HBM] * 2 + [VMEM] * 4,
        out_specs=[HBM] * 3 + [VMEM] * 2,
        scratch_shapes=[
            pltpu.VMEM((SPOTS, LANES), F32),
            pltpu.VMEM((128, D), BF16),
            pltpu.VMEM((128, 2 * D + WIDE), BF16),
            pltpu.VMEM((128, D), BF16),
            pltpu.VMEM((128, D), BF16),
            pltpu.VMEM((128, D), F32),
            pltpu.VMEM((LANES, WIDE), BF16),
            pltpu.SemaphoreType.DMA((6,)),
        ],
        compiler_params=params(),
        cost_estimate=cost(1_000_000, 1_000_000),
        name="main",
    )(core, far(own), far(bias_s), right, below, second_mine, second_other)

    part = (keep.astype(F32) + other_core(send).astype(F32)).astype(BF16)
    part, to_right, to_below = lax.optimization_barrier((part, to_right, to_below))
    part = swap(part, "freq")
    column = from_offset(to_right, -1, 0)
    part, column, to_below = lax.optimization_barrier((part, column, to_below))
    part = swap(summed(part, 4), "tm", tm_groups("y_hi"))
    row = from_offset(jnp.concatenate([to_below, column[32:64]], axis=0), 0, -1)
    part, row = lax.optimization_barrier((part, row))
    part = swap(summed(part, 8), "tm", tm_groups("z"))
    grad_tokens = pl.pallas_call(
        plain_back,
        out_shape=jax.ShapeDtypeStruct((128, D), BF16),
        in_specs=[SMEM] + [HBM] * 5 + [VMEM] * 2,
        out_specs=VMEM,
        scratch_shapes=[
            pltpu.VMEM((128, D), BF16),
            pltpu.VMEM((SPOTS, LANES), F32),
            pltpu.VMEM((8, SHARE + ROWS, HALF), BF16),
            pltpu.VMEM((8, SHARE + ROWS, HALF), BF16),
            pltpu.VMEM((128, D), BF16),
            pltpu.VMEM((128, D), BF16),
            pltpu.VMEM((128, D), BF16),
            pltpu.VMEM((128, D), F32),
            pltpu.VMEM((LANES, WIDE), BF16),
            pltpu.SemaphoreType.DMA((5,)),
        ],
        compiler_params=params(),
        cost_estimate=cost(4_000_000_000, 4_000_000),
        name="plain_back",
    )(core, far(tok), far(g_own), far(bias_p), far(first_mine), far(first_other), column, row)
    part, grad_tokens = lax.optimization_barrier((part, grad_tokens))
    part = summed(part, 1)[0]
    part = lax.all_gather(part, "tm", axis_index_groups=tm_groups("core"))
    grad_plain, grad_shift = pl.pallas_call(
        finish,
        out_shape=(jax.ShapeDtypeStruct((ROWS, D), F32),) * 2,
        in_specs=[VMEM],
        out_specs=[VMEM] * 2,
        compiler_params=params(),
        name="finish",
    )(part)
    return (grad_tokens.reshape(tokens.shape), grad_plain, grad_shift)


def solution(mesh):
    placed = (
        P(None, "freq", "tm", None),
        P(None, "freq", "tm", None),
        P(None, "freq"),
        P(None, "freq"),
        P("freq", None),
        P("freq", None),
        P(),
        P(),
    )
    return jax.shard_map(
        shards,
        mesh=mesh,
        in_specs=placed,
        out_specs=(P(None, "freq", "tm", None), P("freq", None), P("freq", None)),
        check_vma=False,
    )
```

```python
import math

import jax
import jax.numpy as jnp
from jax import lax
from jax.experimental import pallas as pl
from jax.experimental.pallas import tpu as pltpu
from jax.sharding import PartitionSpec as P

D = 768
HEADS = 12
HEAD_DIM = 32
WIN = 8
SPOTS = 64
REL = 225
WIDE = HEADS * HEAD_DIM
LANES = HEADS * SPOTS
HALF = D // 2
SHARE = 144
ROWS = 48

NEG = -1e30
EPS = 1e-05
SCALE = HEAD_DIM ** (-0.5)

NN = (((1,), (0,)), ((), ()))
NT = (((1,), (1,)), ((), ()))
TN = (((0,), (0,)), ((), ()))

F32 = jnp.float32
BF16 = jnp.bfloat16


def offset_pick():
    column = lane((256, WIN * 128))
    entry = ((column >> 3) & 15) * 15 + (column & 7) - (column >> 7) + 7
    row = lax.broadcasted_iota(jnp.int32, (256, WIN * 128), 0)
    return jnp.where(row == entry, 1.0, 0.0).astype(BF16)


def dot(left, right, dims=NN):
    return lax.dot_general(left, right, dims, preferred_element_type=F32)


def normalize(values):
    center = values - jnp.mean(values, axis=-1, keepdims=True)
    rstd = lax.rsqrt(jnp.mean(center * center, axis=-1, keepdims=True) + EPS)
    return (center * rstd, rstd)


def lane(shape):
    return lax.broadcasted_iota(jnp.int32, shape, len(shape) - 1)


def quadrant_pick(transposed=False):
    row = lax.broadcasted_iota(jnp.int32, (128, 128), 1 if transposed else 0)
    column = lax.broadcasted_iota(jnp.int32, (128, 128), 0 if transposed else 1)
    high = (row & 64) >> 1
    low = (row & 32) >> 3
    spot = high + low + ((row & 12) << 1) + (row & 3) + ((row & 16) << 2)
    return jnp.where(spot == column, 1.0, 0.0).astype(BF16)


def head_mask():
    row = lax.broadcasted_iota(jnp.int32, (LANES, WIDE), 0)
    return jnp.where(row // SPOTS == lane((LANES, WIDE)) // HEAD_DIM, 1.0, 0.0).astype(BF16)


def expand(value, mask_ref):
    return jnp.concatenate([value] * HEADS, axis=0) * mask_ref[...]


def fold(full):
    head = lane((SPOTS, WIDE)) // HEAD_DIM
    out = jnp.zeros((SPOTS, WIDE), F32)
    for h in range(HEADS):
        out = out + jnp.where(head == h, full[h * SPOTS : (h + 1) * SPOTS], 0.0)
    return out


def softmax_down(scores):
    expo = jnp.exp(scores - jnp.max(scores, axis=0, keepdims=True))
    return expo / jnp.sum(expo, axis=0, keepdims=True)


def attention_back(query, key, value, d_mixed, probs, query_wide, mask_ref):
    weights = probs.astype(BF16)
    d_wide = expand(d_mixed, mask_ref)
    d_probs = dot(value, d_wide, NT)
    d_value = dot(weights, d_wide).astype(BF16)
    d_scores = (probs * (d_probs - jnp.sum(probs * d_probs, axis=0, keepdims=True))).astype(BF16)
    d_key = (dot(d_scores, query_wide) * SCALE).astype(BF16)
    d_query = (fold(dot(d_scores, key, TN)) * SCALE).astype(BF16)
    return (d_query, d_key, d_value)


def copy_all(pairs, sems, first=0):
    moves = [
        pltpu.make_async_copy(source, target, sems.at[first + i])
        for i, (source, target) in enumerate(pairs)
    ]
    for move in moves:
        move.start()
    return moves


def wait_all(moves):
    for move in moves:
        move.wait()


def biases(edge_ref, table_p, table_s, to_p, to_s, out_p, out_s, tables, wide, sems):
    tables[...] = jnp.zeros_like(tables)
    tables[0:HEADS, 0:REL] = table_p[...]
    tables[HEADS : 2 * HEADS, 0:REL] = table_s[...]
    values = tables[...]
    high = values.astype(BF16)
    rest = values - high.astype(F32)
    middle = rest.astype(BF16)
    low = (rest - middle.astype(F32)).astype(BF16)
    ones = offset_pick()
    spread = (dot(high, ones) + dot(middle, ones)) + dot(low, ones)
    for row in range(2 * HEADS):
        for d in range(WIN):
            wide[row * WIN + d : row * WIN + d + 1] = spread[row : row + 1, d * 128 : (d + 1) * 128]
    left = lane((WIN, 128)) < SPOTS
    for c in range(WIN):
        move = (7 - c) * WIN
        for pair in range(HEADS // 2):
            for t, out in ((0, out_p), (1, out_s)):
                even = (t * HEADS + 2 * pair) * WIN
                first = pltpu.roll(wide[even : even + WIN], (128 - move) % 128, 1)
                second = pltpu.roll(wide[even + WIN : even + 2 * WIN], (SPOTS - move) % 128, 1)
                out[c * WIN : (c + 1) * WIN, pair * 128 : (pair + 1) * 128] = jnp.where(left, first, second)
    at = lane((SPOTS, LANES))
    key_at = lax.broadcasted_iota(jnp.int32, (SPOTS, LANES), 0)
    cross = at ^ key_at
    barred = (cross & 32) * edge_ref[0] + (cross & 4) * edge_ref[1]
    out_s[...] = jnp.where(barred != 0, NEG, out_s[...])
    wait_all(copy_all([(out_p, to_p), (out_s, to_s)], sems))


def project(rows_ref, w_mine, w_other, mine, other):
    return dot(rows_ref[:, pl.ds(mine, HALF)], w_mine, NT) + dot(
        rows_ref[:, pl.ds(other, HALF)], w_other, NT
    )


def sides(core_ref):
    mine = pl.multiple_of(core_ref[0] * HALF, 128)
    return (mine, pl.multiple_of(HALF - mine, 128))


def qkv_of(ref):
    return ref[:, 0:SHARE].reshape(3 * WIDE, HALF)


def proj_of(ref):
    return ref[:, SHARE : SHARE + ROWS].reshape(WIDE, HALF)


def input_grad(grad, normed, rstd, d_packed, w_mine, w_other, mine, other, sums):
    sums[:, pl.ds(mine, HALF)] = dot(d_packed, w_mine)
    sums[:, pl.ds(other, HALF)] = dot(d_packed, w_other)
    d_normed = sums[...]
    d_input = rstd * (
        d_normed
        - jnp.mean(d_normed, axis=-1, keepdims=True)
        - normed * jnp.mean(d_normed * normed, axis=-1, keepdims=True)
    )
    return (grad + d_input).astype(BF16)


def plain_forward(
    core_ref,
    tok_far,
    cot_far,
    bias_far,
    w_mine_ref,
    w_other_ref,
    out_o,
    out_r,
    out_b,
    out_d,
    tok,
    cot,
    bias_p,
    packets,
    rows,
    sums,
    mask,
    sems,
):
    mine, other = sides(core_ref)
    loads = copy_all([(tok_far, tok), (bias_far, bias_p), (cot_far, cot)], sems)
    mask[...] = head_mask()
    loads[0].wait()
    inputs = tok[...].astype(F32)
    rows[...] = normalize(inputs)[0].astype(BF16)
    w_mine, w_other = qkv_of(w_mine_ref), qkv_of(w_other_ref)
    packed = project(rows, w_mine, w_other, mine, other).astype(BF16)
    loads[1].wait()
    mixed = []
    for s in range(2):
        part = packed[s * SPOTS : (s + 1) * SPOTS]
        query, key, value = part[:, :WIDE], part[:, WIDE : 2 * WIDE], part[:, 2 * WIDE :]
        probs = softmax_down(dot(key, expand(query, mask), NT) * SCALE + bias_p[...])
        mixed.append(fold(dot(probs.astype(BF16), value, TN)).astype(BF16))
    mixed = jnp.concatenate(mixed, axis=0)
    sums[:, pl.ds(mine, HALF)] = dot(mixed, proj_of(w_mine_ref))
    sums[:, pl.ds(other, HALF)] = dot(mixed, proj_of(w_other_ref))
    block_out = (inputs + sums[...]).astype(BF16)
    pick = quadrant_pick()
    loads[2].wait()
    for whole, first in ((block_out, 0), (mixed, D), (cot[...], D + WIDE)):
        packets[:, first : first + whole.shape[1]] = dot(pick, whole).astype(BF16)
    outs = (out_d, out_b, out_r, out_o)
    wait_all(copy_all([(packets.at[i * 32 : (i + 1) * 32], out) for i, out in enumerate(outs)], sems, 3))


def main_kernel(
    grad_scale,
    core_ref,
    own_far,
    bias_far,
    right,
    below,
    diag,
    w_mine_ref,
    w_other_ref,
    to_own,
    to_column,
    to_below,
    out_keep,
    out_send,
    bias_s,
    quads,
    staged,
    rows_small,
    grads,
    sums,
    mask,
    sems,
):
    mine, other = sides(core_ref)
    loads = copy_all([(own_far, staged.at[0:32]), (bias_far, bias_s)], sems)
    mask[...] = head_mask()
    for i, part in ((1, right), (2, below), (3, diag)):
        staged[i * 32 : (i + 1) * 32] = part[...]
    wait_all(loads)
    pick = quadrant_pick(True)
    grads[...] = dot(pick, staged[:, D + WIDE :]).astype(BF16)
    block_out = dot(pick, staged[:, 0:D])
    mixed_plain = dot(pick, staged[:, D : D + WIDE]).astype(BF16)
    normed, rstd = normalize(block_out)
    rows_small[...] = normed.astype(BF16)
    w_mine, w_other = qkv_of(w_mine_ref), qkv_of(w_other_ref)
    packed = project(rows_small, w_mine, w_other, mine, other).astype(BF16)
    d_mixed = project(grads, proj_of(w_mine_ref), proj_of(w_other_ref), mine, other).astype(BF16)
    mixed, d_packed = [], []
    for s in range(2):
        part = packed[s * SPOTS : (s + 1) * SPOTS]
        query, key, value = part[:, :WIDE], part[:, WIDE : 2 * WIDE], part[:, 2 * WIDE :]
        query_wide = expand(query, mask)
        probs = softmax_down(dot(key, query_wide, NT) * SCALE + bias_s[...])
        mixed.append(fold(dot(probs.astype(BF16), value, TN)).astype(BF16))
        back = attention_back(
            query, key, value, d_mixed[s * SPOTS : (s + 1) * SPOTS], probs, query_wide, mask
        )
        d_packed.append(jnp.concatenate(back, axis=1))
    mixed_shift = jnp.concatenate(mixed, axis=0)
    d_packed = jnp.concatenate(d_packed, axis=0)
    grad = input_grad(
        grads[...].astype(F32), normed, rstd, d_packed, w_mine, w_other, mine, other, sums
    )
    quads[...] = dot(quadrant_pick(), grad).astype(BF16)
    stores = copy_all(
        [
            (quads.at[0:32], to_own),
            (quads.at[32:64], to_column.at[0:32]),
            (quads.at[96:128], to_column.at[32:64]),
            (quads.at[64:96], to_below),
        ],
        sems,
        2,
    )
    rows_small[...] = grad
    for out, start in ((out_send, other), (out_keep, mine)):
        part = dot(mixed_shift, grads[:, pl.ds(start, HALF)], TN) * grad_scale
        out[:, 1] = part.astype(BF16).reshape(8, ROWS, HALF)
        part = dot(mixed_plain, rows_small[:, pl.ds(start, HALF)], TN) * grad_scale
        out[:, 0] = part.astype(BF16).reshape(8, ROWS, HALF)
    wait_all(stores)


def sum_copies(parts, out):
    value = jnp.sum(parts[...].astype(F32), axis=0).astype(BF16)
    for i in range(out.shape[0]):
        out[i] = value


def finish(parts, out_plain, out_shift):
    for i, out in enumerate((out_plain, out_shift)):
        out[:, 0:HALF] = parts[0, i].astype(F32)
        out[:, HALF:D] = parts[1, i].astype(F32)


def plain_back(
    core_ref,
    tok_far,
    own_far,
    bias_far,
    mine_far,
    other_far,
    column,
    row,
    out,
    tok,
    bias_p,
    w_mine_ref,
    w_other_ref,
    staged,
    rows,
    grads,
    sums,
    mask,
    sems,
):
    mine, other = sides(core_ref)
    loads = copy_all(
        [
            (tok_far, tok),
            (mine_far, w_mine_ref),
            (other_far, w_other_ref),
            (own_far, staged.at[96:128]),
            (bias_far, bias_p),
        ],
        sems,
    )
    mask[...] = head_mask()
    staged[0:32] = row[32:64]
    staged[32:64] = row[0:32]
    staged[64:96] = column[0:32]
    loads[0].wait()
    normed, rstd = normalize(tok[...].astype(F32))
    rows[...] = normed.astype(BF16)
    wait_all(loads[1:])
    w_mine, w_other = qkv_of(w_mine_ref), qkv_of(w_other_ref)
    packed = project(rows, w_mine, w_other, mine, other).astype(BF16)
    gathered = dot(quadrant_pick(True), staged[...])
    grads[...] = gathered.astype(BF16)
    d_mixed = project(grads, proj_of(w_mine_ref), proj_of(w_other_ref), mine, other).astype(BF16)
    d_packed = []
    for s in range(2):
        part = packed[s * SPOTS : (s + 1) * SPOTS]
        query, key, value = part[:, :WIDE], part[:, WIDE : 2 * WIDE], part[:, 2 * WIDE :]
        query_wide = expand(query, mask)
        probs = softmax_down(dot(key, query_wide, NT) * SCALE + bias_p[...])
        back = attention_back(
            query, key, value, d_mixed[s * SPOTS : (s + 1) * SPOTS], probs, query_wide, mask
        )
        d_packed.append(jnp.concatenate(back, axis=1))
    d_packed = jnp.concatenate(d_packed, axis=0)
    out[...] = input_grad(gathered, normed, rstd, d_packed, w_mine, w_other, mine, other, sums)


VMEM = pl.BlockSpec(memory_space=pltpu.VMEM)
SMEM = pl.BlockSpec(memory_space=pltpu.SMEM)
HBM = pl.BlockSpec(memory_space=pltpu.HBM)


def params(size=32):
    return pltpu.CompilerParams(vmem_limit_bytes=size * 1024 * 1024)


def far(value):
    return pltpu.with_memory_space_constraint(value, pltpu.HBM)


def cost(flops, size):
    return pl.CostEstimate(flops=flops, bytes_accessed=size, transcendentals=0)


def tm_groups(bits):
    size = lax.axis_size("tm")
    step = {"core": 1, "y_hi": 2, "z": 8}[bits]
    count = {"core": 2, "y_hi": 4, "z": 8}[bits]
    groups = []
    for first in range(size):
        if (first // step) % count == 0:
            groups.append([first + step * i for i in range(count)])
    return groups


def swap(value, axis, groups=None):
    return lax.all_to_all(value, axis, 0, 0, axis_index_groups=groups)


def from_offset(value, along_tm, along_freq):
    n_tm, n_freq = lax.axis_size("tm"), lax.axis_size("freq")
    pairs = []
    for t in range(n_tm):
        for f in range(n_freq):
            source = ((t + along_tm) % n_tm) * n_freq + (f + along_freq) % n_freq
            pairs.append((source, t * n_freq + f))
    return lax.ppermute(value, ("tm", "freq"), pairs)


def other_core(value):
    return lax.ppermute(value, "tm", [(i, i ^ 1) for i in range(lax.axis_size("tm"))])


def summed(parts, count):
    return pl.pallas_call(
        sum_copies,
        out_shape=jax.ShapeDtypeStruct((count,) + parts.shape[1:], BF16),
        in_specs=[VMEM],
        out_specs=VMEM,
        compiler_params=params(),
        name="sum_copies",
    )(parts)


def shards(
    tokens, cotangent, qkv_plain, qkv_shift, proj_plain, proj_shift, table_plain, table_shift
):
    core = (lax.axis_index("tm") % 2).astype(jnp.int32).reshape(1)
    last_freq = lax.axis_index("freq") == lax.axis_size("freq") - 1
    last_time = lax.axis_index("tm") == lax.axis_size("tm") - 1
    edge = jnp.stack([last_freq, last_time]).astype(jnp.int32)
    grad_scale = 1.0 / math.sqrt(128 * lax.axis_size("tm") * lax.axis_size("freq"))
    tok = tokens.reshape(128, D)
    cot = cotangent.reshape(128, D)

    def share(qkv, proj):
        rows = jnp.concatenate([qkv.T, proj], axis=0)
        half = lax.dynamic_slice_in_dim(rows, core[0] * HALF, HALF, axis=1)
        return jnp.broadcast_to(half[None], (8, SHARE + ROWS, HALF))

    first_mine = swap(share(qkv_plain, proj_plain), "freq")
    second_share = share(qkv_shift, proj_shift)
    table = pltpu.HBM((SPOTS, LANES), F32)
    bias_p, bias_s = pl.pallas_call(
        biases,
        out_shape=(table, table),
        in_specs=[SMEM, VMEM, VMEM],
        out_specs=[HBM] * 2,
        scratch_shapes=[
            pltpu.VMEM((SPOTS, LANES), F32),
            pltpu.VMEM((SPOTS, LANES), F32),
            pltpu.VMEM((32, 256), F32),
            pltpu.VMEM((2 * HEADS * WIN, 128), F32),
            pltpu.SemaphoreType.DMA((2,)),
        ],
        compiler_params=params(),
        name="biases",
    )(edge, table_plain, table_shift)

    first_mine, second_share, bias_p, bias_s = lax.optimization_barrier(
        (first_mine, second_share, bias_p, bias_s)
    )
    second_mine = swap(second_share, "freq")
    first_other = other_core(first_mine)
    packet = pltpu.HBM((32, 2 * D + WIDE), BF16)
    own, to_left, to_above, to_diag = pl.pallas_call(
        plain_forward,
        out_shape=(packet,) * 4,
        in_specs=[SMEM] + [HBM] * 3 + [VMEM] * 2,
        out_specs=[HBM] * 4,
        scratch_shapes=[
            pltpu.VMEM((128, D), BF16),
            pltpu.VMEM((128, D), BF16),
            pltpu.VMEM((SPOTS, LANES), F32),
            pltpu.VMEM((128, 2 * D + WIDE), BF16),
            pltpu.VMEM((128, D), BF16),
            pltpu.VMEM((128, D), F32),
            pltpu.VMEM((LANES, WIDE), BF16),
            pltpu.SemaphoreType.DMA((7,)),
        ],
        compiler_params=params(),
        cost_estimate=cost(20_000_000_000, 1_000_000),
        name="plain_forward",
    )(core, far(tok), far(cot), far(bias_p), first_mine, first_other)
    right = from_offset(to_left, 1, 0)
    below = from_offset(to_above, 0, 1)
    diag = from_offset(to_diag, 1, 1)
    second_mine, right, below, diag = lax.optimization_barrier(
        (second_mine, right, below, diag)
    )
    second_other = other_core(second_mine)
    piece = pltpu.HBM((32, D), BF16)
    column = pltpu.HBM((64, D), BF16)
    local = jax.ShapeDtypeStruct((8, 2, ROWS, HALF), BF16)
    g_own, to_right, to_below, keep, send = pl.pallas_call(
        lambda *refs: main_kernel(grad_scale, *refs),
        out_shape=(piece, column, piece, local, local),
        in_specs=[SMEM] + [HBM] * 2 + [VMEM] * 5,
        out_specs=[HBM] * 3 + [VMEM] * 2,
        scratch_shapes=[
            pltpu.VMEM((SPOTS, LANES), F32),
            pltpu.VMEM((128, D), BF16),
            pltpu.VMEM((128, 2 * D + WIDE), BF16),
            pltpu.VMEM((128, D), BF16),
            pltpu.VMEM((128, D), BF16),
            pltpu.VMEM((128, D), F32),
            pltpu.VMEM((LANES, WIDE), BF16),
            pltpu.SemaphoreType.DMA((6,)),
        ],
        compiler_params=params(),
        cost_estimate=cost(1_000_000, 1_000_000),
        name="main",
    )(core, far(own), far(bias_s), right, below, diag, second_mine, second_other)

    part = (keep.astype(F32) + other_core(send).astype(F32)).astype(BF16)
    part, to_right, to_below = lax.optimization_barrier((part, to_right, to_below))
    part = swap(part, "freq")
    column = from_offset(to_right, -1, 0)
    part, column, to_below = lax.optimization_barrier((part, column, to_below))
    part = swap(summed(part, 4), "tm", tm_groups("y_hi"))
    row = from_offset(jnp.concatenate([to_below, column[32:64]], axis=0), 0, -1)
    part, row = lax.optimization_barrier((part, row))
    part = swap(summed(part, 8), "tm", tm_groups("z"))
    grad_tokens = pl.pallas_call(
        plain_back,
        out_shape=jax.ShapeDtypeStruct((128, D), BF16),
        in_specs=[SMEM] + [HBM] * 5 + [VMEM] * 2,
        out_specs=VMEM,
        scratch_shapes=[
            pltpu.VMEM((128, D), BF16),
            pltpu.VMEM((SPOTS, LANES), F32),
            pltpu.VMEM((8, SHARE + ROWS, HALF), BF16),
            pltpu.VMEM((8, SHARE + ROWS, HALF), BF16),
            pltpu.VMEM((128, D), BF16),
            pltpu.VMEM((128, D), BF16),
            pltpu.VMEM((128, D), BF16),
            pltpu.VMEM((128, D), F32),
            pltpu.VMEM((LANES, WIDE), BF16),
            pltpu.SemaphoreType.DMA((5,)),
        ],
        compiler_params=params(),
        cost_estimate=cost(4_000_000_000, 4_000_000),
        name="plain_back",
    )(core, far(tok), far(g_own), far(bias_p), far(first_mine), far(first_other), column, row)
    part, grad_tokens = lax.optimization_barrier((part, grad_tokens))
    part = summed(part, 1)[0]
    part = lax.all_gather(part, "tm", axis_index_groups=tm_groups("core"))
    grad_plain, grad_shift = pl.pallas_call(
        finish,
        out_shape=(jax.ShapeDtypeStruct((ROWS, D), F32),) * 2,
        in_specs=[VMEM],
        out_specs=[VMEM] * 2,
        compiler_params=params(),
        name="finish",
    )(part)
    return (grad_tokens.reshape(tokens.shape), grad_plain, grad_shift)


def solution(mesh):
    placed = (
        P(None, "freq", "tm", None),
        P(None, "freq", "tm", None),
        P(None, "freq"),
        P(None, "freq"),
        P("freq", None),
        P("freq", None),
        P(),
        P(),
    )
    return jax.shard_map(
        shards,
        mesh=mesh,
        in_specs=placed,
        out_specs=(P(None, "freq", "tm", None), P("freq", None), P("freq", None)),
        check_vma=False,
    )
```

```python
import math

import jax
import jax.numpy as jnp
from jax import lax
from jax.experimental import pallas as pl
from jax.experimental.pallas import tpu as pltpu
from jax.sharding import PartitionSpec as P

D = 768
HEADS = 12
HEAD_DIM = 32
WIN = 8
SPOTS = 64
REL = 225
WIDE = HEADS * HEAD_DIM
LANES = HEADS * SPOTS
HALF = D // 2
SHARE = 144
ROWS = 48

NEG = -1e30
EPS = 1e-05
SCALE = HEAD_DIM ** (-0.5)

NN = (((1,), (0,)), ((), ()))
NT = (((1,), (1,)), ((), ()))
TN = (((0,), (0,)), ((), ()))

F32 = jnp.float32
BF16 = jnp.bfloat16


def offset_pick():
    column = lane((256, WIN * 128))
    entry = ((column >> 3) & 15) * 15 + (column & 7) - (column >> 7) + 7
    row = lax.broadcasted_iota(jnp.int32, (256, WIN * 128), 0)
    return jnp.where(row == entry, 1.0, 0.0).astype(BF16)


def dot(left, right, dims=NN):
    return lax.dot_general(left, right, dims, preferred_element_type=F32)


def normalize(values):
    center = values - jnp.mean(values, axis=-1, keepdims=True)
    rstd = lax.rsqrt(jnp.mean(center * center, axis=-1, keepdims=True) + EPS)
    return (center * rstd, rstd)


def lane(shape):
    return lax.broadcasted_iota(jnp.int32, shape, len(shape) - 1)


def quadrant_pick(transposed=False):
    row = lax.broadcasted_iota(jnp.int32, (128, 128), 1 if transposed else 0)
    column = lax.broadcasted_iota(jnp.int32, (128, 128), 0 if transposed else 1)
    high = (row & 64) >> 1
    low = (row & 32) >> 3
    spot = high + low + ((row & 12) << 1) + (row & 3) + ((row & 16) << 2)
    return jnp.where(spot == column, 1.0, 0.0).astype(BF16)


def head_mask():
    row = lax.broadcasted_iota(jnp.int32, (LANES, WIDE), 0)
    return jnp.where(row // SPOTS == lane((LANES, WIDE)) // HEAD_DIM, 1.0, 0.0).astype(BF16)


def expand(value, mask_ref):
    return jnp.concatenate([value] * HEADS, axis=0) * mask_ref[...]


def fold(full):
    head = lane((SPOTS, WIDE)) // HEAD_DIM
    out = jnp.zeros((SPOTS, WIDE), F32)
    for h in range(HEADS):
        out = out + jnp.where(head == h, full[h * SPOTS : (h + 1) * SPOTS], 0.0)
    return out


def softmax_down(scores):
    expo = jnp.exp(scores - jnp.max(scores, axis=0, keepdims=True))
    return expo / jnp.sum(expo, axis=0, keepdims=True)


def attention_back(query, key, value, d_mixed, probs, query_wide, mask_ref):
    weights = probs.astype(BF16)
    d_wide = expand(d_mixed, mask_ref)
    d_probs = dot(value, d_wide, NT)
    d_value = dot(weights, d_wide).astype(BF16)
    d_scores = (probs * (d_probs - jnp.sum(probs * d_probs, axis=0, keepdims=True))).astype(BF16)
    d_key = (dot(d_scores, query_wide) * SCALE).astype(BF16)
    d_query = (fold(dot(d_scores, key, TN)) * SCALE).astype(BF16)
    return (d_query, d_key, d_value)


def copy_all(pairs, sems, first=0):
    moves = [
        pltpu.make_async_copy(source, target, sems.at[first + i])
        for i, (source, target) in enumerate(pairs)
    ]
    for move in moves:
        move.start()
    return moves


def wait_all(moves):
    for move in moves:
        move.wait()


def prepare(core_ref, qkv, proj, out, block, sems):
    start = pl.multiple_of(core_ref[0] * HALF, 128)
    block[0:SHARE] = qkv[:, pl.ds(start, HALF)]
    block[SHARE : SHARE + ROWS] = proj[:, pl.ds(start, HALF)]
    wait_all(copy_all([(block, out.at[i]) for i in range(8)], sems))


def biases(
    edge_ref,
    table_p,
    table_s,
    cot,
    to_p,
    to_s,
    to_diag,
    to_above,
    to_left,
    to_own,
    out_p,
    out_s,
    tables,
    wide,
    quads,
    sems,
):
    quads[...] = dot(quadrant_pick(), cot[...]).astype(BF16)
    stores = copy_all(
        [
            (quads.at[i * 32 : (i + 1) * 32], out)
            for i, out in enumerate((to_diag, to_above, to_left, to_own))
        ],
        sems,
    )
    tables[...] = jnp.zeros_like(tables)
    tables[0:HEADS, 0:REL] = table_p[...]
    tables[HEADS : 2 * HEADS, 0:REL] = table_s[...]
    values = tables[...]
    high = values.astype(BF16)
    rest = values - high.astype(F32)
    middle = rest.astype(BF16)
    low = (rest - middle.astype(F32)).astype(BF16)
    ones = offset_pick()
    spread = (dot(high, ones) + dot(middle, ones)) + dot(low, ones)
    for row in range(2 * HEADS):
        for d in range(WIN):
            wide[row * WIN + d : row * WIN + d + 1] = spread[row : row + 1, d * 128 : (d + 1) * 128]
    left = lane((WIN, 128)) < SPOTS
    for c in range(WIN):
        move = (7 - c) * WIN
        for pair in range(HEADS // 2):
            for t, out in ((0, out_p), (1, out_s)):
                even = (t * HEADS + 2 * pair) * WIN
                first = pltpu.roll(wide[even : even + WIN], (128 - move) % 128, 1)
                second = pltpu.roll(wide[even + WIN : even + 2 * WIN], (SPOTS - move) % 128, 1)
                out[c * WIN : (c + 1) * WIN, pair * 128 : (pair + 1) * 128] = jnp.where(left, first, second)
    at = lane((SPOTS, LANES))
    key_at = lax.broadcasted_iota(jnp.int32, (SPOTS, LANES), 0)
    cross = at ^ key_at
    barred = (cross & 32) * edge_ref[0] + (cross & 4) * edge_ref[1]
    out_s[...] = jnp.where(barred != 0, NEG, out_s[...])
    wait_all(stores + copy_all([(out_p, to_p), (out_s, to_s)], sems, 4))


def project(rows_ref, w_mine, w_other, mine, other):
    return dot(rows_ref[:, pl.ds(mine, HALF)], w_mine, NT) + dot(
        rows_ref[:, pl.ds(other, HALF)], w_other, NT
    )


def sides(core_ref):
    mine = pl.multiple_of(core_ref[0] * HALF, 128)
    return (mine, pl.multiple_of(HALF - mine, 128))


def qkv_of(ref):
    return ref[:, 0:SHARE].reshape(3 * WIDE, HALF)


def proj_of(ref):
    return ref[:, SHARE : SHARE + ROWS].reshape(WIDE, HALF)


def input_grad(grad, normed, rstd, d_packed, w_mine, w_other, mine, other, sums):
    sums[:, pl.ds(mine, HALF)] = dot(d_packed, w_mine)
    sums[:, pl.ds(other, HALF)] = dot(d_packed, w_other)
    d_normed = sums[...]
    d_input = rstd * (
        d_normed
        - jnp.mean(d_normed, axis=-1, keepdims=True)
        - normed * jnp.mean(d_normed * normed, axis=-1, keepdims=True)
    )
    return (grad + d_input).astype(BF16)


def plain_forward(
    core_ref,
    tok_far,
    bias_far,
    w_mine_ref,
    w_other_ref,
    out_o,
    out_r,
    out_b,
    out_d,
    tok,
    bias_p,
    packets,
    rows,
    sums,
    mask,
    sems,
):
    mine, other = sides(core_ref)
    loads = copy_all([(tok_far, tok), (bias_far, bias_p)], sems)
    mask[...] = head_mask()
    loads[0].wait()
    inputs = tok[...].astype(F32)
    rows[...] = normalize(inputs)[0].astype(BF16)
    w_mine, w_other = qkv_of(w_mine_ref), qkv_of(w_other_ref)
    packed = project(rows, w_mine, w_other, mine, other).astype(BF16)
    loads[1].wait()
    mixed = []
    for s in range(2):
        part = packed[s * SPOTS : (s + 1) * SPOTS]
        query, key, value = part[:, :WIDE], part[:, WIDE : 2 * WIDE], part[:, 2 * WIDE :]
        probs = softmax_down(dot(key, expand(query, mask), NT) * SCALE + bias_p[...])
        mixed.append(fold(dot(probs.astype(BF16), value, TN)).astype(BF16))
    mixed = jnp.concatenate(mixed, axis=0)
    sums[:, pl.ds(mine, HALF)] = dot(mixed, proj_of(w_mine_ref))
    sums[:, pl.ds(other, HALF)] = dot(mixed, proj_of(w_other_ref))
    block_out = (inputs + sums[...]).astype(BF16)
    pick = quadrant_pick()
    for whole, first in ((block_out, 0), (mixed, D)):
        packets[:, first : first + whole.shape[1]] = dot(pick, whole).astype(BF16)
    outs = (out_d, out_b, out_r, out_o)
    wait_all(copy_all([(packets.at[i * 32 : (i + 1) * 32], out) for i, out in enumerate(outs)], sems, 2))


def main_kernel(
    grad_scale,
    core_ref,
    own_far,
    bias_far,
    cot_own,
    cot_right,
    cot_below,
    cot_diag,
    right,
    below,
    diag,
    w_mine_ref,
    w_other_ref,
    to_own,
    to_column,
    to_below,
    out_keep,
    out_send,
    bias_s,
    quads,
    staged,
    staged_cot,
    rows_small,
    grads,
    sums,
    mask,
    sems,
):
    mine, other = sides(core_ref)
    loads = copy_all([(own_far, staged.at[0:32]), (bias_far, bias_s)], sems)
    cots = (cot_own, cot_right, cot_below, cot_diag)
    loads += copy_all([(c, staged_cot.at[i * 32 : (i + 1) * 32]) for i, c in enumerate(cots)], sems, 2)
    mask[...] = head_mask()
    for i, part in ((1, right), (2, below), (3, diag)):
        staged[i * 32 : (i + 1) * 32] = part[...]
    loads[0].wait()
    pick = quadrant_pick(True)
    block_out = dot(pick, staged[:, 0:D])
    mixed_plain = dot(pick, staged[:, D : D + WIDE]).astype(BF16)
    normed, rstd = normalize(block_out)
    wait_all(loads[1:])
    grads[...] = dot(pick, staged_cot[...]).astype(BF16)
    rows_small[...] = normed.astype(BF16)
    w_mine, w_other = qkv_of(w_mine_ref), qkv_of(w_other_ref)
    packed = project(rows_small, w_mine, w_other, mine, other).astype(BF16)
    d_mixed = project(grads, proj_of(w_mine_ref), proj_of(w_other_ref), mine, other).astype(BF16)
    mixed, d_packed = [], []
    for s in range(2):
        part = packed[s * SPOTS : (s + 1) * SPOTS]
        query, key, value = part[:, :WIDE], part[:, WIDE : 2 * WIDE], part[:, 2 * WIDE :]
        query_wide = expand(query, mask)
        probs = softmax_down(dot(key, query_wide, NT) * SCALE + bias_s[...])
        mixed.append(fold(dot(probs.astype(BF16), value, TN)).astype(BF16))
        back = attention_back(
            query, key, value, d_mixed[s * SPOTS : (s + 1) * SPOTS], probs, query_wide, mask
        )
        d_packed.append(jnp.concatenate(back, axis=1))
    mixed_shift = jnp.concatenate(mixed, axis=0)
    d_packed = jnp.concatenate(d_packed, axis=0)
    grad = input_grad(
        grads[...].astype(F32), normed, rstd, d_packed, w_mine, w_other, mine, other, sums
    )
    quads[...] = dot(quadrant_pick(), grad).astype(BF16)
    stores = copy_all(
        [
            (quads.at[0:32], to_own),
            (quads.at[32:64], to_column.at[0:32]),
            (quads.at[96:128], to_column.at[32:64]),
            (quads.at[64:96], to_below),
        ],
        sems,
        6,
    )
    rows_small[...] = grad
    for out, start in ((out_send, other), (out_keep, mine)):
        part = dot(mixed_shift, grads[:, pl.ds(start, HALF)], TN) * grad_scale
        out[:, 1] = part.astype(BF16).reshape(8, ROWS, HALF)
        part = dot(mixed_plain, rows_small[:, pl.ds(start, HALF)], TN) * grad_scale
        out[:, 0] = part.astype(BF16).reshape(8, ROWS, HALF)
    wait_all(stores)


def sum_copies(parts, out):
    value = jnp.sum(parts[...].astype(F32), axis=0).astype(BF16)
    for i in range(out.shape[0]):
        out[i] = value


def finish(parts, out_plain, out_shift):
    for i, out in enumerate((out_plain, out_shift)):
        out[:, 0:HALF] = parts[0, i].astype(F32)
        out[:, HALF:D] = parts[1, i].astype(F32)


def plain_back(
    core_ref,
    tok_far,
    own_far,
    bias_far,
    mine_far,
    other_far,
    column,
    row,
    out,
    tok,
    bias_p,
    w_mine_ref,
    w_other_ref,
    staged,
    rows,
    grads,
    sums,
    mask,
    sems,
):
    mine, other = sides(core_ref)
    loads = copy_all(
        [
            (tok_far, tok),
            (mine_far, w_mine_ref),
            (other_far, w_other_ref),
            (own_far, staged.at[96:128]),
            (bias_far, bias_p),
        ],
        sems,
    )
    mask[...] = head_mask()
    staged[0:32] = row[32:64]
    staged[32:64] = row[0:32]
    staged[64:96] = column[0:32]
    loads[0].wait()
    normed, rstd = normalize(tok[...].astype(F32))
    rows[...] = normed.astype(BF16)
    wait_all(loads[1:])
    w_mine, w_other = qkv_of(w_mine_ref), qkv_of(w_other_ref)
    packed = project(rows, w_mine, w_other, mine, other).astype(BF16)
    gathered = dot(quadrant_pick(True), staged[...])
    grads[...] = gathered.astype(BF16)
    d_mixed = project(grads, proj_of(w_mine_ref), proj_of(w_other_ref), mine, other).astype(BF16)
    d_packed = []
    for s in range(2):
        part = packed[s * SPOTS : (s + 1) * SPOTS]
        query, key, value = part[:, :WIDE], part[:, WIDE : 2 * WIDE], part[:, 2 * WIDE :]
        query_wide = expand(query, mask)
        probs = softmax_down(dot(key, query_wide, NT) * SCALE + bias_p[...])
        back = attention_back(
            query, key, value, d_mixed[s * SPOTS : (s + 1) * SPOTS], probs, query_wide, mask
        )
        d_packed.append(jnp.concatenate(back, axis=1))
    d_packed = jnp.concatenate(d_packed, axis=0)
    out[...] = input_grad(gathered, normed, rstd, d_packed, w_mine, w_other, mine, other, sums)


VMEM = pl.BlockSpec(memory_space=pltpu.VMEM)
SMEM = pl.BlockSpec(memory_space=pltpu.SMEM)
HBM = pl.BlockSpec(memory_space=pltpu.HBM)


def params(size=32):
    return pltpu.CompilerParams(vmem_limit_bytes=size * 1024 * 1024)


def far(value):
    return pltpu.with_memory_space_constraint(value, pltpu.HBM)


def cost(flops, size):
    return pl.CostEstimate(flops=flops, bytes_accessed=size, transcendentals=0)


def tm_groups(bits):
    size = lax.axis_size("tm")
    step = {"core": 1, "y_hi": 2, "z": 8}[bits]
    count = {"core": 2, "y_hi": 4, "z": 8}[bits]
    groups = []
    for first in range(size):
        if (first // step) % count == 0:
            groups.append([first + step * i for i in range(count)])
    return groups


def swap(value, axis, groups=None):
    return lax.all_to_all(value, axis, 0, 0, axis_index_groups=groups)


def from_offset(value, along_tm, along_freq):
    n_tm, n_freq = lax.axis_size("tm"), lax.axis_size("freq")
    pairs = []
    for t in range(n_tm):
        for f in range(n_freq):
            source = ((t + along_tm) % n_tm) * n_freq + (f + along_freq) % n_freq
            pairs.append((source, t * n_freq + f))
    return lax.ppermute(value, ("tm", "freq"), pairs)


def other_core(value):
    return lax.ppermute(value, "tm", [(i, i ^ 1) for i in range(lax.axis_size("tm"))])


def summed(parts, count):
    return pl.pallas_call(
        sum_copies,
        out_shape=jax.ShapeDtypeStruct((count,) + parts.shape[1:], BF16),
        in_specs=[VMEM],
        out_specs=VMEM,
        compiler_params=params(),
        name="sum_copies",
    )(parts)


def shards(
    tokens, cotangent, qkv_plain, qkv_shift, proj_plain, proj_shift, table_plain, table_shift
):
    core = (lax.axis_index("tm") % 2).astype(jnp.int32).reshape(1)
    last_freq = lax.axis_index("freq") == lax.axis_size("freq") - 1
    last_time = lax.axis_index("tm") == lax.axis_size("tm") - 1
    edge = jnp.stack([last_freq, last_time]).astype(jnp.int32)
    grad_scale = 1.0 / math.sqrt(128 * lax.axis_size("tm") * lax.axis_size("freq"))
    tok = tokens.reshape(128, D)
    cot = cotangent.reshape(128, D)

    def share(qkv, proj):
        return pl.pallas_call(
            prepare,
            out_shape=pltpu.HBM((8, SHARE + ROWS, HALF), BF16),
            in_specs=[SMEM, VMEM, VMEM],
            out_specs=HBM,
            scratch_shapes=[
                pltpu.VMEM((SHARE + ROWS, HALF), BF16),
                pltpu.SemaphoreType.DMA((8,)),
            ],
            compiler_params=params(60),
            name="prepare",
        )(core, qkv.T, proj)

    first_mine = swap(share(qkv_plain, proj_plain), "freq")
    second_share = share(qkv_shift, proj_shift)
    table = pltpu.HBM((SPOTS, LANES), F32)
    piece = pltpu.HBM((32, D), BF16)
    bias_p, bias_s, cot_diag, cot_above, cot_left, cot_own = pl.pallas_call(
        biases,
        out_shape=(table, table) + (piece,) * 4,
        in_specs=[SMEM] + [VMEM] * 3,
        out_specs=[HBM] * 6,
        scratch_shapes=[
            pltpu.VMEM((SPOTS, LANES), F32),
            pltpu.VMEM((SPOTS, LANES), F32),
            pltpu.VMEM((32, 256), F32),
            pltpu.VMEM((2 * HEADS * WIN, 128), F32),
            pltpu.VMEM((128, D), BF16),
            pltpu.SemaphoreType.DMA((6,)),
        ],
        compiler_params=params(),
        name="biases",
    )(edge, table_plain, table_shift, cot)
    cot_right = from_offset(cot_left, 1, 0)
    cot_below = from_offset(cot_above, 0, 1)
    cot_diag = from_offset(cot_diag, 1, 1)

    first_mine, second_share, bias_p, bias_s, cot_right, cot_below, cot_diag = lax.optimization_barrier(
        (first_mine, second_share, bias_p, bias_s, cot_right, cot_below, cot_diag)
    )
    second_mine = swap(second_share, "freq")
    first_other = other_core(first_mine)
    packet = pltpu.HBM((32, D + WIDE), BF16)
    own, to_left, to_above, to_diag = pl.pallas_call(
        plain_forward,
        out_shape=(packet,) * 4,
        in_specs=[SMEM] + [HBM] * 2 + [VMEM] * 2,
        out_specs=[HBM] * 4,
        scratch_shapes=[
            pltpu.VMEM((128, D), BF16),
            pltpu.VMEM((SPOTS, LANES), F32),
            pltpu.VMEM((128, D + WIDE), BF16),
            pltpu.VMEM((128, D), BF16),
            pltpu.VMEM((128, D), F32),
            pltpu.VMEM((LANES, WIDE), BF16),
            pltpu.SemaphoreType.DMA((6,)),
        ],
        compiler_params=params(),
        cost_estimate=cost(20_000_000_000, 1_000_000),
        name="plain_forward",
    )(core, far(tok), far(bias_p), first_mine, first_other)
    right = from_offset(to_left, 1, 0)
    below = from_offset(to_above, 0, 1)
    diag = from_offset(to_diag, 1, 1)
    second_mine, right, below, diag = lax.optimization_barrier(
        (second_mine, right, below, diag)
    )
    second_other = other_core(second_mine)
    column = pltpu.HBM((64, D), BF16)
    local = jax.ShapeDtypeStruct((8, 2, ROWS, HALF), BF16)
    g_own, to_right, to_below, keep, send = pl.pallas_call(
        lambda *refs: main_kernel(grad_scale, *refs),
        out_shape=(piece, column, piece, local, local),
        in_specs=[SMEM] + [HBM] * 6 + [VMEM] * 5,
        out_specs=[HBM] * 3 + [VMEM] * 2,
        scratch_shapes=[
            pltpu.VMEM((SPOTS, LANES), F32),
            pltpu.VMEM((128, D), BF16),
            pltpu.VMEM((128, D + WIDE), BF16),
            pltpu.VMEM((128, D), BF16),
            pltpu.VMEM((128, D), BF16),
            pltpu.VMEM((128, D), BF16),
            pltpu.VMEM((128, D), F32),
            pltpu.VMEM((LANES, WIDE), BF16),
            pltpu.SemaphoreType.DMA((10,)),
        ],
        compiler_params=params(),
        cost_estimate=cost(1_000_000, 1_000_000),
        name="main",
    )(
        core, far(own), far(bias_s), far(cot_own), far(cot_right), far(cot_below), far(cot_diag),
        right, below, diag, second_mine, second_other,
    )

    part = (keep.astype(F32) + other_core(send).astype(F32)).astype(BF16)
    part, to_right, to_below = lax.optimization_barrier((part, to_right, to_below))
    part = swap(part, "freq")
    column = from_offset(to_right, -1, 0)
    part, column, to_below = lax.optimization_barrier((part, column, to_below))
    part = swap(summed(part, 4), "tm", tm_groups("y_hi"))
    row = from_offset(jnp.concatenate([to_below, column[32:64]], axis=0), 0, -1)
    part, row = lax.optimization_barrier((part, row))
    part = swap(summed(part, 8), "tm", tm_groups("z"))
    grad_tokens = pl.pallas_call(
        plain_back,
        out_shape=jax.ShapeDtypeStruct((128, D), BF16),
        in_specs=[SMEM] + [HBM] * 5 + [VMEM] * 2,
        out_specs=VMEM,
        scratch_shapes=[
            pltpu.VMEM((128, D), BF16),
            pltpu.VMEM((SPOTS, LANES), F32),
            pltpu.VMEM((8, SHARE + ROWS, HALF), BF16),
            pltpu.VMEM((8, SHARE + ROWS, HALF), BF16),
            pltpu.VMEM((128, D), BF16),
            pltpu.VMEM((128, D), BF16),
            pltpu.VMEM((128, D), BF16),
            pltpu.VMEM((128, D), F32),
            pltpu.VMEM((LANES, WIDE), BF16),
            pltpu.SemaphoreType.DMA((5,)),
        ],
        compiler_params=params(),
        cost_estimate=cost(4_000_000_000, 4_000_000),
        name="plain_back",
    )(core, far(tok), far(g_own), far(bias_p), far(first_mine), far(first_other), column, row)
    part, grad_tokens = lax.optimization_barrier((part, grad_tokens))
    part = summed(part, 1)[0]
    part = lax.all_gather(part, "tm", axis_index_groups=tm_groups("core"))
    grad_plain, grad_shift = pl.pallas_call(
        finish,
        out_shape=(jax.ShapeDtypeStruct((ROWS, D), F32),) * 2,
        in_specs=[VMEM],
        out_specs=[VMEM] * 2,
        compiler_params=params(),
        name="finish",
    )(part)
    return (grad_tokens.reshape(tokens.shape), grad_plain, grad_shift)


def solution(mesh):
    placed = (
        P(None, "freq", "tm", None),
        P(None, "freq", "tm", None),
        P(None, "freq"),
        P(None, "freq"),
        P("freq", None),
        P("freq", None),
        P(),
        P(),
    )
    return jax.shard_map(
        shards,
        mesh=mesh,
        in_specs=placed,
        out_specs=(P(None, "freq", "tm", None), P("freq", None), P("freq", None)),
        check_vma=False,
    )
```

```python
import math

import jax
import jax.numpy as jnp
from jax import lax
from jax.experimental import pallas as pl
from jax.experimental.pallas import tpu as pltpu
from jax.sharding import PartitionSpec as P

D = 768
HEADS = 12
HEAD_DIM = 32
WIN = 8
SPOTS = 64
REL = 225
WIDE = HEADS * HEAD_DIM
LANES = HEADS * SPOTS
HALF = D // 2
SHARE = 144
ROWS = 48

NEG = -1e30
EPS = 1e-05
SCALE = HEAD_DIM ** (-0.5)

NN = (((1,), (0,)), ((), ()))
NT = (((1,), (1,)), ((), ()))
TN = (((0,), (0,)), ((), ()))

F32 = jnp.float32
BF16 = jnp.bfloat16


def offset_pick():
    column = lane((256, WIN * 128))
    entry = ((column >> 3) & 15) * 15 + (column & 7) - (column >> 7) + 7
    row = lax.broadcasted_iota(jnp.int32, (256, WIN * 128), 0)
    return jnp.where(row == entry, 1.0, 0.0).astype(BF16)


def dot(left, right, dims=NN):
    return lax.dot_general(left, right, dims, preferred_element_type=F32)


def normalize(values):
    center = values - jnp.mean(values, axis=-1, keepdims=True)
    rstd = lax.rsqrt(jnp.mean(center * center, axis=-1, keepdims=True) + EPS)
    return (center * rstd, rstd)


def lane(shape):
    return lax.broadcasted_iota(jnp.int32, shape, len(shape) - 1)


def quadrant_pick(transposed=False):
    row = lax.broadcasted_iota(jnp.int32, (128, 128), 1 if transposed else 0)
    column = lax.broadcasted_iota(jnp.int32, (128, 128), 0 if transposed else 1)
    high = (row & 64) >> 1
    low = (row & 32) >> 3
    spot = high + low + ((row & 12) << 1) + (row & 3) + ((row & 16) << 2)
    return jnp.where(spot == column, 1.0, 0.0).astype(BF16)


def head_mask():
    row = lax.broadcasted_iota(jnp.int32, (LANES, WIDE), 0)
    return jnp.where(row // SPOTS == lane((LANES, WIDE)) // HEAD_DIM, 1.0, 0.0).astype(BF16)


def expand(value, mask_ref):
    return jnp.concatenate([value] * HEADS, axis=0) * mask_ref[...]


def fold(full):
    head = lane((SPOTS, WIDE)) // HEAD_DIM
    out = jnp.zeros((SPOTS, WIDE), F32)
    for h in range(HEADS):
        out = out + jnp.where(head == h, full[h * SPOTS : (h + 1) * SPOTS], 0.0)
    return out


def softmax_down(scores):
    expo = jnp.exp(scores - jnp.max(scores, axis=0, keepdims=True))
    return expo / jnp.sum(expo, axis=0, keepdims=True)


def attention_back(query, key, value, d_mixed, probs, query_wide, mask_ref):
    weights = probs.astype(BF16)
    d_wide = expand(d_mixed, mask_ref)
    d_probs = dot(value, d_wide, NT)
    d_value = dot(weights, d_wide).astype(BF16)
    d_scores = (probs * (d_probs - jnp.sum(probs * d_probs, axis=0, keepdims=True))).astype(BF16)
    d_key = (dot(d_scores, query_wide) * SCALE).astype(BF16)
    d_query = (fold(dot(d_scores, key, TN)) * SCALE).astype(BF16)
    return (d_query, d_key, d_value)


def copy_all(pairs, sems, first=0):
    moves = [
        pltpu.make_async_copy(source, target, sems.at[first + i])
        for i, (source, target) in enumerate(pairs)
    ]
    for move in moves:
        move.start()
    return moves


def wait_all(moves):
    for move in moves:
        move.wait()


def prepare(core_ref, qkv, proj, out, block, sems):
    start = pl.multiple_of(core_ref[0] * HALF, 128)
    block[0:SHARE] = qkv[:, pl.ds(start, HALF)]
    block[SHARE : SHARE + ROWS] = proj[:, pl.ds(start, HALF)]
    wait_all(copy_all([(block, out.at[i]) for i in range(8)], sems))


def biases(edge_ref, table_p, table_s, to_p, to_s, out_p, out_s, tables, wide, sems):
    tables[...] = jnp.zeros_like(tables)
    tables[0:HEADS, 0:REL] = table_p[...]
    tables[HEADS : 2 * HEADS, 0:REL] = table_s[...]
    values = tables[...]
    high = values.astype(BF16)
    rest = values - high.astype(F32)
    middle = rest.astype(BF16)
    low = (rest - middle.astype(F32)).astype(BF16)
    ones = offset_pick()
    spread = (dot(high, ones) + dot(middle, ones)) + dot(low, ones)
    for row in range(2 * HEADS):
        for d in range(WIN):
            wide[row * WIN + d : row * WIN + d + 1] = spread[row : row + 1, d * 128 : (d + 1) * 128]
    left = lane((WIN, 128)) < SPOTS
    for c in range(WIN):
        move = (7 - c) * WIN
        for pair in range(HEADS // 2):
            for t, out in ((0, out_p), (1, out_s)):
                even = (t * HEADS + 2 * pair) * WIN
                first = pltpu.roll(wide[even : even + WIN], (128 - move) % 128, 1)
                second = pltpu.roll(wide[even + WIN : even + 2 * WIN], (SPOTS - move) % 128, 1)
                out[c * WIN : (c + 1) * WIN, pair * 128 : (pair + 1) * 128] = jnp.where(left, first, second)
    at = lane((SPOTS, LANES))
    key_at = lax.broadcasted_iota(jnp.int32, (SPOTS, LANES), 0)
    cross = at ^ key_at
    barred = (cross & 32) * edge_ref[0] + (cross & 4) * edge_ref[1]
    out_s[...] = jnp.where(barred != 0, NEG, out_s[...])
    wait_all(copy_all([(out_p, to_p), (out_s, to_s)], sems))


def project(rows_ref, w_mine, w_other, mine, other):
    return dot(rows_ref[:, pl.ds(mine, HALF)], w_mine, NT) + dot(
        rows_ref[:, pl.ds(other, HALF)], w_other, NT
    )


def sides(core_ref):
    mine = pl.multiple_of(core_ref[0] * HALF, 128)
    return (mine, pl.multiple_of(HALF - mine, 128))


def qkv_of(ref):
    return ref[:, 0:SHARE].reshape(3 * WIDE, HALF)


def proj_of(ref):
    return ref[:, SHARE : SHARE + ROWS].reshape(WIDE, HALF)


def input_grad(grad, normed, rstd, d_packed, w_mine, w_other, mine, other, sums):
    sums[:, pl.ds(mine, HALF)] = dot(d_packed, w_mine)
    sums[:, pl.ds(other, HALF)] = dot(d_packed, w_other)
    d_normed = sums[...]
    d_input = rstd * (
        d_normed
        - jnp.mean(d_normed, axis=-1, keepdims=True)
        - normed * jnp.mean(d_normed * normed, axis=-1, keepdims=True)
    )
    return (grad + d_input).astype(BF16)


def plain_forward(
    core_ref,
    tok_far,
    cot_far,
    bias_far,
    w_mine_ref,
    w_other_ref,
    out_o,
    out_r,
    out_b,
    out_d,
    tok,
    cot,
    bias_p,
    packets,
    rows,
    sums,
    mask,
    sems,
):
    mine, other = sides(core_ref)
    loads = copy_all([(tok_far, tok), (bias_far, bias_p), (cot_far, cot)], sems)
    mask[...] = head_mask()
    loads[0].wait()
    inputs = tok[...].astype(F32)
    rows[...] = normalize(inputs)[0].astype(BF16)
    w_mine, w_other = qkv_of(w_mine_ref), qkv_of(w_other_ref)
    packed = project(rows, w_mine, w_other, mine, other).astype(BF16)
    loads[1].wait()
    mixed = []
    for s in range(2):
        part = packed[s * SPOTS : (s + 1) * SPOTS]
        query, key, value = part[:, :WIDE], part[:, WIDE : 2 * WIDE], part[:, 2 * WIDE :]
        probs = softmax_down(dot(key, expand(query, mask), NT) * SCALE + bias_p[...])
        mixed.append(fold(dot(probs.astype(BF16), value, TN)).astype(BF16))
    mixed = jnp.concatenate(mixed, axis=0)
    sums[:, pl.ds(mine, HALF)] = dot(mixed, proj_of(w_mine_ref))
    sums[:, pl.ds(other, HALF)] = dot(mixed, proj_of(w_other_ref))
    block_out = (inputs + sums[...]).astype(BF16)
    pick = quadrant_pick()
    loads[2].wait()
    for whole, first in ((block_out, 0), (mixed, D), (cot[...], D + WIDE)):
        packets[:, first : first + whole.shape[1]] = dot(pick, whole).astype(BF16)
    outs = (out_d, out_b, out_r, out_o)
    wait_all(copy_all([(packets.at[i * 32 : (i + 1) * 32], out) for i, out in enumerate(outs)], sems, 3))


def main_kernel(
    grad_scale,
    core_ref,
    own_far,
    bias_far,
    right,
    below,
    diag,
    w_mine_ref,
    w_other_ref,
    to_own,
    to_right,
    to_below,
    to_diag,
    out_keep,
    out_send,
    bias_s,
    quads,
    staged,
    rows_small,
    grads,
    sums,
    mask,
    sems,
):
    mine, other = sides(core_ref)
    loads = copy_all([(own_far, staged.at[0:32]), (bias_far, bias_s)], sems)
    mask[...] = head_mask()
    for i, part in ((1, right), (2, below), (3, diag)):
        staged[i * 32 : (i + 1) * 32] = part[...]
    wait_all(loads)
    pick = quadrant_pick(True)
    grads[...] = dot(pick, staged[:, D + WIDE :]).astype(BF16)
    block_out = dot(pick, staged[:, 0:D])
    mixed_plain = dot(pick, staged[:, D : D + WIDE]).astype(BF16)
    normed, rstd = normalize(block_out)
    rows_small[...] = normed.astype(BF16)
    w_mine, w_other = qkv_of(w_mine_ref), qkv_of(w_other_ref)
    packed = project(rows_small, w_mine, w_other, mine, other).astype(BF16)
    d_mixed = project(grads, proj_of(w_mine_ref), proj_of(w_other_ref), mine, other).astype(BF16)
    mixed, d_packed = [], []
    for s in range(2):
        part = packed[s * SPOTS : (s + 1) * SPOTS]
        query, key, value = part[:, :WIDE], part[:, WIDE : 2 * WIDE], part[:, 2 * WIDE :]
        query_wide = expand(query, mask)
        probs = softmax_down(dot(key, query_wide, NT) * SCALE + bias_s[...])
        mixed.append(fold(dot(probs.astype(BF16), value, TN)).astype(BF16))
        back = attention_back(
            query, key, value, d_mixed[s * SPOTS : (s + 1) * SPOTS], probs, query_wide, mask
        )
        d_packed.append(jnp.concatenate(back, axis=1))
    mixed_shift = jnp.concatenate(mixed, axis=0)
    d_packed = jnp.concatenate(d_packed, axis=0)
    grad = input_grad(
        grads[...].astype(F32), normed, rstd, d_packed, w_mine, w_other, mine, other, sums
    )
    quads[...] = dot(quadrant_pick(), grad).astype(BF16)
    stores = copy_all(
        [
            (quads.at[0:32], to_own),
            (quads.at[32:64], to_right),
            (quads.at[64:96], to_below),
            (quads.at[96:128], to_diag),
        ],
        sems,
        2,
    )
    rows_small[...] = grad
    for out, start in ((out_send, other), (out_keep, mine)):
        part = dot(mixed_shift, grads[:, pl.ds(start, HALF)], TN) * grad_scale
        out[:, 1] = part.astype(BF16).reshape(8, ROWS, HALF)
        part = dot(mixed_plain, rows_small[:, pl.ds(start, HALF)], TN) * grad_scale
        out[:, 0] = part.astype(BF16).reshape(8, ROWS, HALF)
    wait_all(stores)


def sum_copies(parts, out):
    value = jnp.sum(parts[...].astype(F32), axis=0).astype(BF16)
    for i in range(out.shape[0]):
        out[i] = value


def finish(parts, out_plain, out_shift):
    for i, out in enumerate((out_plain, out_shift)):
        out[:, 0:HALF] = parts[0, i].astype(F32)
        out[:, HALF:D] = parts[1, i].astype(F32)


def plain_back(
    core_ref,
    tok_far,
    own_far,
    bias_far,
    mine_far,
    other_far,
    g_left,
    g_above,
    g_diag,
    out,
    tok,
    bias_p,
    w_mine_ref,
    w_other_ref,
    staged,
    rows,
    grads,
    sums,
    mask,
    sems,
):
    mine, other = sides(core_ref)
    loads = copy_all(
        [
            (tok_far, tok),
            (mine_far, w_mine_ref),
            (other_far, w_other_ref),
            (own_far, staged.at[96:128]),
            (bias_far, bias_p),
        ],
        sems,
    )
    mask[...] = head_mask()
    for i, part in enumerate((g_diag, g_above, g_left)):
        staged[i * 32 : (i + 1) * 32] = part[...]
    loads[0].wait()
    normed, rstd = normalize(tok[...].astype(F32))
    rows[...] = normed.astype(BF16)
    wait_all(loads[1:])
    w_mine, w_other = qkv_of(w_mine_ref), qkv_of(w_other_ref)
    packed = project(rows, w_mine, w_other, mine, other).astype(BF16)
    gathered = dot(quadrant_pick(True), staged[...])
    grads[...] = gathered.astype(BF16)
    d_mixed = project(grads, proj_of(w_mine_ref), proj_of(w_other_ref), mine, other).astype(BF16)
    d_packed = []
    for s in range(2):
        part = packed[s * SPOTS : (s + 1) * SPOTS]
        query, key, value = part[:, :WIDE], part[:, WIDE : 2 * WIDE], part[:, 2 * WIDE :]
        query_wide = expand(query, mask)
        probs = softmax_down(dot(key, query_wide, NT) * SCALE + bias_p[...])
        back = attention_back(
            query, key, value, d_mixed[s * SPOTS : (s + 1) * SPOTS], probs, query_wide, mask
        )
        d_packed.append(jnp.concatenate(back, axis=1))
    d_packed = jnp.concatenate(d_packed, axis=0)
    out[...] = input_grad(gathered, normed, rstd, d_packed, w_mine, w_other, mine, other, sums)


VMEM = pl.BlockSpec(memory_space=pltpu.VMEM)
SMEM = pl.BlockSpec(memory_space=pltpu.SMEM)
HBM = pl.BlockSpec(memory_space=pltpu.HBM)


def params(size=32):
    return pltpu.CompilerParams(vmem_limit_bytes=size * 1024 * 1024)


def far(value):
    return pltpu.with_memory_space_constraint(value, pltpu.HBM)


def cost(flops, size):
    return pl.CostEstimate(flops=flops, bytes_accessed=size, transcendentals=0)


def tm_groups(bits):
    size = lax.axis_size("tm")
    step = {"core": 1, "y_hi": 2, "z": 8}[bits]
    count = {"core": 2, "y_hi": 4, "z": 8}[bits]
    groups = []
    for first in range(size):
        if (first // step) % count == 0:
            groups.append([first + step * i for i in range(count)])
    return groups


def swap(value, axis, groups=None):
    return lax.all_to_all(value, axis, 0, 0, axis_index_groups=groups)


def from_offset(value, along_tm, along_freq):
    n_tm, n_freq = lax.axis_size("tm"), lax.axis_size("freq")
    pairs = []
    for t in range(n_tm):
        for f in range(n_freq):
            source = ((t + along_tm) % n_tm) * n_freq + (f + along_freq) % n_freq
            pairs.append((source, t * n_freq + f))
    return lax.ppermute(value, ("tm", "freq"), pairs)


def other_core(value):
    return lax.ppermute(value, "tm", [(i, i ^ 1) for i in range(lax.axis_size("tm"))])


def summed(parts, count):
    return pl.pallas_call(
        sum_copies,
        out_shape=jax.ShapeDtypeStruct((count,) + parts.shape[1:], BF16),
        in_specs=[VMEM],
        out_specs=VMEM,
        compiler_params=params(),
        name="sum_copies",
    )(parts)


def shards(
    tokens, cotangent, qkv_plain, qkv_shift, proj_plain, proj_shift, table_plain, table_shift
):
    core = (lax.axis_index("tm") % 2).astype(jnp.int32).reshape(1)
    last_freq = lax.axis_index("freq") == lax.axis_size("freq") - 1
    last_time = lax.axis_index("tm") == lax.axis_size("tm") - 1
    edge = jnp.stack([last_freq, last_time]).astype(jnp.int32)
    grad_scale = 1.0 / math.sqrt(128 * lax.axis_size("tm") * lax.axis_size("freq"))
    tok = tokens.reshape(128, D)
    cot = cotangent.reshape(128, D)

    def share(qkv, proj):
        return pl.pallas_call(
            prepare,
            out_shape=pltpu.HBM((8, SHARE + ROWS, HALF), BF16),
            in_specs=[SMEM, VMEM, VMEM],
            out_specs=HBM,
            scratch_shapes=[
                pltpu.VMEM((SHARE + ROWS, HALF), BF16),
                pltpu.SemaphoreType.DMA((8,)),
            ],
            compiler_params=params(60),
            name="prepare",
        )(core, qkv.T, proj)

    first_mine = swap(share(qkv_plain, proj_plain), "freq")
    second_share = share(qkv_shift, proj_shift)
    table = pltpu.HBM((SPOTS, LANES), F32)
    bias_p, bias_s = pl.pallas_call(
        biases,
        out_shape=(table, table),
        in_specs=[SMEM, VMEM, VMEM],
        out_specs=[HBM] * 2,
        scratch_shapes=[
            pltpu.VMEM((SPOTS, LANES), F32),
            pltpu.VMEM((SPOTS, LANES), F32),
            pltpu.VMEM((32, 256), F32),
            pltpu.VMEM((2 * HEADS * WIN, 128), F32),
            pltpu.SemaphoreType.DMA((2,)),
        ],
        compiler_params=params(),
        name="biases",
    )(edge, table_plain, table_shift)

    first_mine, second_share, bias_p, bias_s = lax.optimization_barrier(
        (first_mine, second_share, bias_p, bias_s)
    )
    second_mine = swap(second_share, "freq")
    first_other = other_core(first_mine)
    packet = pltpu.HBM((32, 2 * D + WIDE), BF16)
    own, to_left, to_above, to_diag = pl.pallas_call(
        plain_forward,
        out_shape=(packet,) * 4,
        in_specs=[SMEM] + [HBM] * 3 + [VMEM] * 2,
        out_specs=[HBM] * 4,
        scratch_shapes=[
            pltpu.VMEM((128, D), BF16),
            pltpu.VMEM((128, D), BF16),
            pltpu.VMEM((SPOTS, LANES), F32),
            pltpu.VMEM((128, 2 * D + WIDE), BF16),
            pltpu.VMEM((128, D), BF16),
            pltpu.VMEM((128, D), F32),
            pltpu.VMEM((LANES, WIDE), BF16),
            pltpu.SemaphoreType.DMA((7,)),
        ],
        compiler_params=params(),
        cost_estimate=cost(20_000_000_000, 1_000_000),
        name="plain_forward",
    )(core, far(tok), far(cot), far(bias_p), first_mine, first_other)
    right = from_offset(to_left, 1, 0)
    below = from_offset(to_above, 0, 1)
    diag = from_offset(to_diag, 1, 1)
    second_mine, right, below, diag = lax.optimization_barrier(
        (second_mine, right, below, diag)
    )
    second_other = other_core(second_mine)
    piece = pltpu.HBM((32, D), BF16)
    local = jax.ShapeDtypeStruct((8, 2, ROWS, HALF), BF16)
    g_own, to_right, to_below, to_diag, keep, send = pl.pallas_call(
        lambda *refs: main_kernel(grad_scale, *refs),
        out_shape=(piece,) * 4 + (local, local),
        in_specs=[SMEM] + [HBM] * 2 + [VMEM] * 5,
        out_specs=[HBM] * 4 + [VMEM] * 2,
        scratch_shapes=[
            pltpu.VMEM((SPOTS, LANES), F32),
            pltpu.VMEM((128, D), BF16),
            pltpu.VMEM((128, 2 * D + WIDE), BF16),
            pltpu.VMEM((128, D), BF16),
            pltpu.VMEM((128, D), BF16),
            pltpu.VMEM((128, D), F32),
            pltpu.VMEM((LANES, WIDE), BF16),
            pltpu.SemaphoreType.DMA((6,)),
        ],
        compiler_params=params(),
        cost_estimate=cost(1_000_000, 1_000_000),
        name="main",
    )(core, far(own), far(bias_s), right, below, diag, second_mine, second_other)

    part = (keep.astype(F32) + other_core(send).astype(F32)).astype(BF16)
    part, to_right, to_below, to_diag = lax.optimization_barrier(
        (part, to_right, to_below, to_diag)
    )
    part = swap(part, "freq")
    left = from_offset(to_right, -1, 0)
    above = from_offset(to_below, 0, -1)
    corner = from_offset(to_diag, -1, -1)
    part, left, above, corner = lax.optimization_barrier((part, left, above, corner))
    part = swap(summed(part, 4), "tm", tm_groups("y_hi"))
    part = swap(summed(part, 8), "tm", tm_groups("z"))
    grad_tokens = pl.pallas_call(
        plain_back,
        out_shape=jax.ShapeDtypeStruct((128, D), BF16),
        in_specs=[SMEM] + [HBM] * 5 + [VMEM] * 3,
        out_specs=VMEM,
        scratch_shapes=[
            pltpu.VMEM((128, D), BF16),
            pltpu.VMEM((SPOTS, LANES), F32),
            pltpu.VMEM((8, SHARE + ROWS, HALF), BF16),
            pltpu.VMEM((8, SHARE + ROWS, HALF), BF16),
            pltpu.VMEM((128, D), BF16),
            pltpu.VMEM((128, D), BF16),
            pltpu.VMEM((128, D), BF16),
            pltpu.VMEM((128, D), F32),
            pltpu.VMEM((LANES, WIDE), BF16),
            pltpu.SemaphoreType.DMA((5,)),
        ],
        compiler_params=params(),
        cost_estimate=cost(4_000_000_000, 4_000_000),
        name="plain_back",
    )(core, far(tok), far(g_own), far(bias_p), far(first_mine), far(first_other), left, above, corner)
    part, grad_tokens = lax.optimization_barrier((part, grad_tokens))
    part = summed(part, 1)[0]
    part = lax.all_gather(part, "tm", axis_index_groups=tm_groups("core"))
    grad_plain, grad_shift = pl.pallas_call(
        finish,
        out_shape=(jax.ShapeDtypeStruct((ROWS, D), F32),) * 2,
        in_specs=[VMEM],
        out_specs=[VMEM] * 2,
        compiler_params=params(),
        name="finish",
    )(part)
    return (grad_tokens.reshape(tokens.shape), grad_plain, grad_shift)


def solution(mesh):
    placed = (
        P(None, "freq", "tm", None),
        P(None, "freq", "tm", None),
        P(None, "freq"),
        P(None, "freq"),
        P("freq", None),
        P("freq", None),
        P(),
        P(),
    )
    return jax.shard_map(
        shards,
        mesh=mesh,
        in_specs=placed,
        out_specs=(P(None, "freq", "tm", None), P("freq", None), P("freq", None)),
        check_vma=False,
    )
```

```python
import math

import jax
import jax.numpy as jnp
from jax import lax
from jax.experimental import pallas as pl
from jax.experimental.pallas import tpu as pltpu
from jax.sharding import PartitionSpec as P

D = 768
HEADS = 12
HEAD_DIM = 32
WIN = 8
SPOTS = 64
REL = 225
WIDE = HEADS * HEAD_DIM
LANES = HEADS * SPOTS
HALF = D // 2
SHARE = 144
ROWS = 48

NEG = -1e30
EPS = 1e-05
SCALE = HEAD_DIM ** (-0.5)

NN = (((1,), (0,)), ((), ()))
NT = (((1,), (1,)), ((), ()))
TN = (((0,), (0,)), ((), ()))

F32 = jnp.float32
BF16 = jnp.bfloat16


def offset_pick():
    column = lane((256, WIN * 128))
    entry = ((column >> 3) & 15) * 15 + (column & 7) - (column >> 7) + 7
    row = lax.broadcasted_iota(jnp.int32, (256, WIN * 128), 0)
    return jnp.where(row == entry, 1.0, 0.0).astype(BF16)


def dot(left, right, dims=NN):
    return lax.dot_general(left, right, dims, preferred_element_type=F32)


def normalize(values):
    center = values - jnp.mean(values, axis=-1, keepdims=True)
    rstd = lax.rsqrt(jnp.mean(center * center, axis=-1, keepdims=True) + EPS)
    return (center * rstd, rstd)


def lane(shape):
    return lax.broadcasted_iota(jnp.int32, shape, len(shape) - 1)


def quadrant_pick(transposed=False):
    row = lax.broadcasted_iota(jnp.int32, (128, 128), 1 if transposed else 0)
    column = lax.broadcasted_iota(jnp.int32, (128, 128), 0 if transposed else 1)
    high = (row & 64) >> 1
    low = (row & 32) >> 3
    spot = high + low + ((row & 12) << 1) + (row & 3) + ((row & 16) << 2)
    return jnp.where(spot == column, 1.0, 0.0).astype(BF16)


def head_mask():
    row = lax.broadcasted_iota(jnp.int32, (LANES, WIDE), 0)
    return jnp.where(row // SPOTS == lane((LANES, WIDE)) // HEAD_DIM, 1.0, 0.0).astype(BF16)


def expand(value, mask_ref):
    return jnp.concatenate([value] * HEADS, axis=0) * mask_ref[...]


def fold(full):
    head = lane((SPOTS, WIDE)) // HEAD_DIM
    out = jnp.zeros((SPOTS, WIDE), F32)
    for h in range(HEADS):
        out = out + jnp.where(head == h, full[h * SPOTS : (h + 1) * SPOTS], 0.0)
    return out


def softmax_down(scores):
    expo = jnp.exp(scores - jnp.max(scores, axis=0, keepdims=True))
    return expo / jnp.sum(expo, axis=0, keepdims=True)


def attention_back(query, key, value, d_mixed, probs, query_wide, mask_ref):
    weights = probs.astype(BF16)
    d_wide = expand(d_mixed, mask_ref)
    d_probs = dot(value, d_wide, NT)
    d_value = dot(weights, d_wide).astype(BF16)
    d_scores = (probs * (d_probs - jnp.sum(probs * d_probs, axis=0, keepdims=True))).astype(BF16)
    d_key = (dot(d_scores, query_wide) * SCALE).astype(BF16)
    d_query = (fold(dot(d_scores, key, TN)) * SCALE).astype(BF16)
    return (d_query, d_key, d_value)


def copy_all(pairs, sems, first=0):
    moves = [
        pltpu.make_async_copy(source, target, sems.at[first + i])
        for i, (source, target) in enumerate(pairs)
    ]
    for move in moves:
        move.start()
    return moves


def wait_all(moves):
    for move in moves:
        move.wait()


def prepare(core_ref, qkv, proj, out, block, sems):
    start = pl.multiple_of(core_ref[0] * HALF, 128)
    block[0:SHARE] = qkv[:, pl.ds(start, HALF)]
    block[SHARE : SHARE + ROWS] = proj[:, pl.ds(start, HALF)]
    wait_all(copy_all([(block, out.at[i]) for i in range(8)], sems))


def biases(edge_ref, table_p, table_s, to_p, to_s, out_p, out_s, tables, wide, sems):
    tables[...] = jnp.zeros_like(tables)
    tables[0:HEADS, 0:REL] = table_p[...]
    tables[HEADS : 2 * HEADS, 0:REL] = table_s[...]
    values = tables[...]
    high = values.astype(BF16)
    rest = values - high.astype(F32)
    middle = rest.astype(BF16)
    low = (rest - middle.astype(F32)).astype(BF16)
    ones = offset_pick()
    spread = (dot(high, ones) + dot(middle, ones)) + dot(low, ones)
    for row in range(2 * HEADS):
        for d in range(WIN):
            wide[row * WIN + d : row * WIN + d + 1] = spread[row : row + 1, d * 128 : (d + 1) * 128]
    left = lane((WIN, 128)) < SPOTS
    for c in range(WIN):
        move = (7 - c) * WIN
        for pair in range(HEADS // 2):
            for t, out in ((0, out_p), (1, out_s)):
                even = (t * HEADS + 2 * pair) * WIN
                first = pltpu.roll(wide[even : even + WIN], (128 - move) % 128, 1)
                second = pltpu.roll(wide[even + WIN : even + 2 * WIN], (SPOTS - move) % 128, 1)
                out[c * WIN : (c + 1) * WIN, pair * 128 : (pair + 1) * 128] = jnp.where(left, first, second)
    at = lane((SPOTS, LANES))
    key_at = lax.broadcasted_iota(jnp.int32, (SPOTS, LANES), 0)
    cross = at ^ key_at
    barred = (cross & 32) * edge_ref[0] + (cross & 4) * edge_ref[1]
    out_s[...] = jnp.where(barred != 0, NEG, out_s[...])
    wait_all(copy_all([(out_p, to_p), (out_s, to_s)], sems))


def project(rows_ref, w_mine, w_other, mine, other):
    return dot(rows_ref[:, pl.ds(mine, HALF)], w_mine, NT) + dot(
        rows_ref[:, pl.ds(other, HALF)], w_other, NT
    )


def sides(core_ref):
    mine = pl.multiple_of(core_ref[0] * HALF, 128)
    return (mine, pl.multiple_of(HALF - mine, 128))


def qkv_of(ref):
    return ref[:, 0:SHARE].reshape(3 * WIDE, HALF)


def proj_of(ref):
    return ref[:, SHARE : SHARE + ROWS].reshape(WIDE, HALF)


def input_grad(grad, normed, rstd, d_packed, w_mine, w_other, mine, other, sums):
    sums[:, pl.ds(mine, HALF)] = dot(d_packed, w_mine)
    sums[:, pl.ds(other, HALF)] = dot(d_packed, w_other)
    d_normed = sums[...]
    d_input = rstd * (
        d_normed
        - jnp.mean(d_normed, axis=-1, keepdims=True)
        - normed * jnp.mean(d_normed * normed, axis=-1, keepdims=True)
    )
    return (grad + d_input).astype(BF16)


def plain_forward(
    core_ref,
    tok_far,
    cot_far,
    bias_far,
    w_mine_ref,
    w_other_ref,
    out_o,
    out_r,
    out_b,
    out_d,
    tok,
    cot,
    bias_p,
    packets,
    rows,
    sums,
    mask,
    sems,
):
    mine, other = sides(core_ref)
    loads = copy_all([(tok_far, tok), (bias_far, bias_p), (cot_far, cot)], sems)
    mask[...] = head_mask()
    loads[0].wait()
    inputs = tok[...].astype(F32)
    rows[...] = normalize(inputs)[0].astype(BF16)
    w_mine, w_other = qkv_of(w_mine_ref), qkv_of(w_other_ref)
    packed = project(rows, w_mine, w_other, mine, other).astype(BF16)
    loads[1].wait()
    mixed = []
    for s in range(2):
        part = packed[s * SPOTS : (s + 1) * SPOTS]
        query, key, value = part[:, :WIDE], part[:, WIDE : 2 * WIDE], part[:, 2 * WIDE :]
        probs = softmax_down(dot(key, expand(query, mask), NT) * SCALE + bias_p[...])
        mixed.append(fold(dot(probs.astype(BF16), value, TN)).astype(BF16))
    mixed = jnp.concatenate(mixed, axis=0)
    sums[:, pl.ds(mine, HALF)] = dot(mixed, proj_of(w_mine_ref))
    sums[:, pl.ds(other, HALF)] = dot(mixed, proj_of(w_other_ref))
    block_out = (inputs + sums[...]).astype(BF16)
    pick = quadrant_pick()
    loads[2].wait()
    for whole, first in ((block_out, 0), (mixed, D), (cot[...], D + WIDE)):
        packets[:, first : first + whole.shape[1]] = dot(pick, whole).astype(BF16)
    outs = (out_d, out_b, out_r, out_o)
    wait_all(copy_all([(packets.at[i * 32 : (i + 1) * 32], out) for i, out in enumerate(outs)], sems, 3))


def main_begin(
    core_ref,
    own_far,
    bias_far,
    right,
    below,
    diag,
    w_mine_ref,
    out_grads,
    out_normed,
    out_rows,
    out_rstd,
    out_mixed,
    out_packed,
    out_d_mixed,
    out_bias,
    staged,
    sems,
):
    mine, _ = sides(core_ref)
    loads = copy_all([(own_far, staged.at[0:32]), (bias_far, out_bias)], sems)
    for i, part in ((1, right), (2, below), (3, diag)):
        staged[i * 32 : (i + 1) * 32] = part[...]
    pick = quadrant_pick(True)
    loads[0].wait()
    out_grads[...] = dot(pick, staged[:, D + WIDE :]).astype(BF16)
    block_out = dot(pick, staged[:, 0:D])
    out_mixed[...] = dot(pick, staged[:, D : D + WIDE]).astype(BF16)
    normed, rstd = normalize(block_out)
    out_normed[...] = normed
    out_rstd[...] = jnp.broadcast_to(rstd, (128, 128))
    out_rows[...] = normed.astype(BF16)
    out_packed[...] = dot(out_rows[:, pl.ds(mine, HALF)], qkv_of(w_mine_ref), NT)
    out_d_mixed[...] = dot(out_grads[:, pl.ds(mine, HALF)], proj_of(w_mine_ref), NT)
    loads[1].wait()


def main_kernel(
    grad_scale,
    core_ref,
    grads,
    normed_ref,
    rows,
    rstd_ref,
    mixed_ref,
    packed_ref,
    d_mixed_ref,
    bias_s,
    w_mine_ref,
    w_other_ref,
    to_own,
    to_column,
    to_below,
    out_keep,
    out_send,
    quads,
    rows_small,
    sums,
    mask,
    sems,
):
    mine, other = sides(core_ref)
    mask[...] = head_mask()
    normed, rstd = normed_ref[...], rstd_ref[:, 0:1]
    mixed_plain = mixed_ref[...]
    w_mine, w_other = qkv_of(w_mine_ref), qkv_of(w_other_ref)
    packed = packed_ref[...] + dot(rows[:, pl.ds(other, HALF)], w_other, NT)
    packed = packed.astype(BF16)
    d_mixed = d_mixed_ref[...] + dot(grads[:, pl.ds(other, HALF)], proj_of(w_other_ref), NT)
    d_mixed = d_mixed.astype(BF16)
    mixed, d_packed = [], []
    for s in range(2):
        part = packed[s * SPOTS : (s + 1) * SPOTS]
        query, key, value = part[:, :WIDE], part[:, WIDE : 2 * WIDE], part[:, 2 * WIDE :]
        query_wide = expand(query, mask)
        probs = softmax_down(dot(key, query_wide, NT) * SCALE + bias_s[...])
        mixed.append(fold(dot(probs.astype(BF16), value, TN)).astype(BF16))
        back = attention_back(
            query, key, value, d_mixed[s * SPOTS : (s + 1) * SPOTS], probs, query_wide, mask
        )
        d_packed.append(jnp.concatenate(back, axis=1))
    mixed_shift = jnp.concatenate(mixed, axis=0)
    d_packed = jnp.concatenate(d_packed, axis=0)
    grad = input_grad(
        grads[...].astype(F32), normed, rstd, d_packed, w_mine, w_other, mine, other, sums
    )
    quads[...] = dot(quadrant_pick(), grad).astype(BF16)
    stores = copy_all(
        [
            (quads.at[0:32], to_own),
            (quads.at[32:64], to_column.at[0:32]),
            (quads.at[96:128], to_column.at[32:64]),
            (quads.at[64:96], to_below),
        ],
        sems,
    )
    rows_small[...] = grad
    for out, start in ((out_send, other), (out_keep, mine)):
        part = dot(mixed_shift, grads[:, pl.ds(start, HALF)], TN) * grad_scale
        out[:, 1] = part.astype(BF16).reshape(8, ROWS, HALF)
        part = dot(mixed_plain, rows_small[:, pl.ds(start, HALF)], TN) * grad_scale
        out[:, 0] = part.astype(BF16).reshape(8, ROWS, HALF)
    wait_all(stores)


def sum_copies(parts, out):
    value = jnp.sum(parts[...].astype(F32), axis=0).astype(BF16)
    for i in range(out.shape[0]):
        out[i] = value


def finish(parts, out_plain, out_shift):
    for i, out in enumerate((out_plain, out_shift)):
        out[:, 0:HALF] = parts[0, i].astype(F32)
        out[:, HALF:D] = parts[1, i].astype(F32)


def plain_back(
    core_ref,
    tok_far,
    own_far,
    bias_far,
    mine_far,
    other_far,
    column,
    row,
    out,
    tok,
    bias_p,
    w_mine_ref,
    w_other_ref,
    staged,
    rows,
    grads,
    sums,
    mask,
    sems,
):
    mine, other = sides(core_ref)
    loads = copy_all(
        [
            (tok_far, tok),
            (mine_far, w_mine_ref),
            (other_far, w_other_ref),
            (own_far, staged.at[96:128]),
            (bias_far, bias_p),
        ],
        sems,
    )
    mask[...] = head_mask()
    staged[0:32] = row[32:64]
    staged[32:64] = row[0:32]
    staged[64:96] = column[0:32]
    loads[0].wait()
    normed, rstd = normalize(tok[...].astype(F32))
    rows[...] = normed.astype(BF16)
    wait_all(loads[1:])
    w_mine, w_other = qkv_of(w_mine_ref), qkv_of(w_other_ref)
    packed = project(rows, w_mine, w_other, mine, other).astype(BF16)
    gathered = dot(quadrant_pick(True), staged[...])
    grads[...] = gathered.astype(BF16)
    d_mixed = project(grads, proj_of(w_mine_ref), proj_of(w_other_ref), mine, other).astype(BF16)
    d_packed = []
    for s in range(2):
        part = packed[s * SPOTS : (s + 1) * SPOTS]
        query, key, value = part[:, :WIDE], part[:, WIDE : 2 * WIDE], part[:, 2 * WIDE :]
        query_wide = expand(query, mask)
        probs = softmax_down(dot(key, query_wide, NT) * SCALE + bias_p[...])
        back = attention_back(
            query, key, value, d_mixed[s * SPOTS : (s + 1) * SPOTS], probs, query_wide, mask
        )
        d_packed.append(jnp.concatenate(back, axis=1))
    d_packed = jnp.concatenate(d_packed, axis=0)
    out[...] = input_grad(gathered, normed, rstd, d_packed, w_mine, w_other, mine, other, sums)


VMEM = pl.BlockSpec(memory_space=pltpu.VMEM)
SMEM = pl.BlockSpec(memory_space=pltpu.SMEM)
HBM = pl.BlockSpec(memory_space=pltpu.HBM)


def params(size=32):
    return pltpu.CompilerParams(vmem_limit_bytes=size * 1024 * 1024)


def far(value):
    return pltpu.with_memory_space_constraint(value, pltpu.HBM)


def cost(flops, size):
    return pl.CostEstimate(flops=flops, bytes_accessed=size, transcendentals=0)


def tm_groups(bits):
    size = lax.axis_size("tm")
    step = {"core": 1, "y_hi": 2, "z": 8}[bits]
    count = {"core": 2, "y_hi": 4, "z": 8}[bits]
    groups = []
    for first in range(size):
        if (first // step) % count == 0:
            groups.append([first + step * i for i in range(count)])
    return groups


def swap(value, axis, groups=None):
    return lax.all_to_all(value, axis, 0, 0, axis_index_groups=groups)


def from_offset(value, along_tm, along_freq):
    n_tm, n_freq = lax.axis_size("tm"), lax.axis_size("freq")
    pairs = []
    for t in range(n_tm):
        for f in range(n_freq):
            source = ((t + along_tm) % n_tm) * n_freq + (f + along_freq) % n_freq
            pairs.append((source, t * n_freq + f))
    return lax.ppermute(value, ("tm", "freq"), pairs)


def other_core(value):
    return lax.ppermute(value, "tm", [(i, i ^ 1) for i in range(lax.axis_size("tm"))])


def summed(parts, count):
    return pl.pallas_call(
        sum_copies,
        out_shape=jax.ShapeDtypeStruct((count,) + parts.shape[1:], BF16),
        in_specs=[VMEM],
        out_specs=VMEM,
        compiler_params=params(),
        name="sum_copies",
    )(parts)


def shards(
    tokens, cotangent, qkv_plain, qkv_shift, proj_plain, proj_shift, table_plain, table_shift
):
    core = (lax.axis_index("tm") % 2).astype(jnp.int32).reshape(1)
    last_freq = lax.axis_index("freq") == lax.axis_size("freq") - 1
    last_time = lax.axis_index("tm") == lax.axis_size("tm") - 1
    edge = jnp.stack([last_freq, last_time]).astype(jnp.int32)
    grad_scale = 1.0 / math.sqrt(128 * lax.axis_size("tm") * lax.axis_size("freq"))
    tok = tokens.reshape(128, D)
    cot = cotangent.reshape(128, D)

    def share(qkv, proj):
        return pl.pallas_call(
            prepare,
            out_shape=pltpu.HBM((8, SHARE + ROWS, HALF), BF16),
            in_specs=[SMEM, VMEM, VMEM],
            out_specs=HBM,
            scratch_shapes=[
                pltpu.VMEM((SHARE + ROWS, HALF), BF16),
                pltpu.SemaphoreType.DMA((8,)),
            ],
            compiler_params=params(60),
            name="prepare",
        )(core, qkv.T, proj)

    first_mine = swap(share(qkv_plain, proj_plain), "freq")
    second_share = share(qkv_shift, proj_shift)
    table = pltpu.HBM((SPOTS, LANES), F32)
    bias_p, bias_s = pl.pallas_call(
        biases,
        out_shape=(table, table),
        in_specs=[SMEM, VMEM, VMEM],
        out_specs=[HBM] * 2,
        scratch_shapes=[
            pltpu.VMEM((SPOTS, LANES), F32),
            pltpu.VMEM((SPOTS, LANES), F32),
            pltpu.VMEM((32, 256), F32),
            pltpu.VMEM((2 * HEADS * WIN, 128), F32),
            pltpu.SemaphoreType.DMA((2,)),
        ],
        compiler_params=params(),
        name="biases",
    )(edge, table_plain, table_shift)

    first_mine, second_share, bias_p, bias_s = lax.optimization_barrier(
        (first_mine, second_share, bias_p, bias_s)
    )
    second_mine = swap(second_share, "freq")
    first_other = other_core(first_mine)
    packet = pltpu.HBM((32, 2 * D + WIDE), BF16)
    own, to_left, to_above, to_diag = pl.pallas_call(
        plain_forward,
        out_shape=(packet,) * 4,
        in_specs=[SMEM] + [HBM] * 3 + [VMEM] * 2,
        out_specs=[HBM] * 4,
        scratch_shapes=[
            pltpu.VMEM((128, D), BF16),
            pltpu.VMEM((128, D), BF16),
            pltpu.VMEM((SPOTS, LANES), F32),
            pltpu.VMEM((128, 2 * D + WIDE), BF16),
            pltpu.VMEM((128, D), BF16),
            pltpu.VMEM((128, D), F32),
            pltpu.VMEM((LANES, WIDE), BF16),
            pltpu.SemaphoreType.DMA((7,)),
        ],
        compiler_params=params(),
        cost_estimate=cost(20_000_000_000, 1_000_000),
        name="plain_forward",
    )(core, far(tok), far(cot), far(bias_p), first_mine, first_other)
    right = from_offset(to_left, 1, 0)
    below = from_offset(to_above, 0, 1)
    diag = from_offset(to_diag, 1, 1)
    second_mine, right, below, diag = lax.optimization_barrier(
        (second_mine, right, below, diag)
    )
    second_other = other_core(second_mine)
    piece = pltpu.HBM((32, D), BF16)
    column = pltpu.HBM((64, D), BF16)
    local = jax.ShapeDtypeStruct((8, 2, ROWS, HALF), BF16)
    def near(shape, dtype):
        return jax.ShapeDtypeStruct(shape, dtype)

    begun = pl.pallas_call(
        main_begin,
        out_shape=(
            near((128, D), BF16),
            near((128, D), F32),
            near((128, D), BF16),
            near((128, 128), F32),
            near((128, WIDE), BF16),
            near((128, 3 * WIDE), F32),
            near((128, WIDE), F32),
            near((SPOTS, LANES), F32),
        ),
        in_specs=[SMEM] + [HBM] * 2 + [VMEM] * 4,
        out_specs=[VMEM] * 8,
        scratch_shapes=[
            pltpu.VMEM((128, 2 * D + WIDE), BF16),
            pltpu.SemaphoreType.DMA((2,)),
        ],
        compiler_params=params(),
        cost_estimate=cost(5_000_000_000, 1_000_000),
        name="main_begin",
    )(core, far(own), far(bias_s), right, below, diag, second_mine)
    g_own, to_right, to_below, keep, send = pl.pallas_call(
        lambda *refs: main_kernel(grad_scale, *refs),
        out_shape=(piece, column, piece, local, local),
        in_specs=[SMEM] + [VMEM] * 10,
        out_specs=[HBM] * 3 + [VMEM] * 2,
        scratch_shapes=[
            pltpu.VMEM((128, D), BF16),
            pltpu.VMEM((128, D), BF16),
            pltpu.VMEM((128, D), F32),
            pltpu.VMEM((LANES, WIDE), BF16),
            pltpu.SemaphoreType.DMA((4,)),
        ],
        compiler_params=params(),
        cost_estimate=cost(1_000_000, 1_000_000),
        name="main",
    )(core, *begun, second_mine, second_other)

    part = (keep.astype(F32) + other_core(send).astype(F32)).astype(BF16)
    part, to_right, to_below = lax.optimization_barrier((part, to_right, to_below))
    part = swap(part, "freq")
    column = from_offset(to_right, -1, 0)
    part, column, to_below = lax.optimization_barrier((part, column, to_below))
    part = swap(summed(part, 4), "tm", tm_groups("y_hi"))
    row = from_offset(jnp.concatenate([to_below, column[32:64]], axis=0), 0, -1)
    part, row = lax.optimization_barrier((part, row))
    part = swap(summed(part, 8), "tm", tm_groups("z"))
    grad_tokens = pl.pallas_call(
        plain_back,
        out_shape=jax.ShapeDtypeStruct((128, D), BF16),
        in_specs=[SMEM] + [HBM] * 5 + [VMEM] * 2,
        out_specs=VMEM,
        scratch_shapes=[
            pltpu.VMEM((128, D), BF16),
            pltpu.VMEM((SPOTS, LANES), F32),
            pltpu.VMEM((8, SHARE + ROWS, HALF), BF16),
            pltpu.VMEM((8, SHARE + ROWS, HALF), BF16),
            pltpu.VMEM((128, D), BF16),
            pltpu.VMEM((128, D), BF16),
            pltpu.VMEM((128, D), BF16),
            pltpu.VMEM((128, D), F32),
            pltpu.VMEM((LANES, WIDE), BF16),
            pltpu.SemaphoreType.DMA((5,)),
        ],
        compiler_params=params(),
        cost_estimate=cost(4_000_000_000, 4_000_000),
        name="plain_back",
    )(core, far(tok), far(g_own), far(bias_p), far(first_mine), far(first_other), column, row)
    part, grad_tokens = lax.optimization_barrier((part, grad_tokens))
    part = summed(part, 1)[0]
    part = lax.all_gather(part, "tm", axis_index_groups=tm_groups("core"))
    grad_plain, grad_shift = pl.pallas_call(
        finish,
        out_shape=(jax.ShapeDtypeStruct((ROWS, D), F32),) * 2,
        in_specs=[VMEM],
        out_specs=[VMEM] * 2,
        compiler_params=params(),
        name="finish",
    )(part)
    return (grad_tokens.reshape(tokens.shape), grad_plain, grad_shift)


def solution(mesh):
    placed = (
        P(None, "freq", "tm", None),
        P(None, "freq", "tm", None),
        P(None, "freq"),
        P(None, "freq"),
        P("freq", None),
        P("freq", None),
        P(),
        P(),
    )
    return jax.shard_map(
        shards,
        mesh=mesh,
        in_specs=placed,
        out_specs=(P(None, "freq", "tm", None), P("freq", None), P("freq", None)),
        check_vma=False,
    )
```

```python
import math

import jax
import jax.numpy as jnp
from jax import lax
from jax.experimental import pallas as pl
from jax.experimental.pallas import tpu as pltpu
from jax.sharding import PartitionSpec as P

D = 768
HEADS = 12
HEAD_DIM = 32
WIN = 8
SPOTS = 64
REL = 225
WIDE = HEADS * HEAD_DIM
LANES = HEADS * SPOTS
HALF = D // 2
SHARE = 144
ROWS = 48

NEG = -1e30
EPS = 1e-05
SCALE = HEAD_DIM ** (-0.5)

NN = (((1,), (0,)), ((), ()))
NT = (((1,), (1,)), ((), ()))
TN = (((0,), (0,)), ((), ()))

F32 = jnp.float32
BF16 = jnp.bfloat16


def offset_pick():
    column = lane((256, WIN * 128))
    entry = ((column >> 3) & 15) * 15 + (column & 7) - (column >> 7) + 7
    row = lax.broadcasted_iota(jnp.int32, (256, WIN * 128), 0)
    return jnp.where(row == entry, 1.0, 0.0).astype(BF16)


def dot(left, right, dims=NN):
    return lax.dot_general(left, right, dims, preferred_element_type=F32)


def normalize(values):
    center = values - jnp.mean(values, axis=-1, keepdims=True)
    rstd = lax.rsqrt(jnp.mean(center * center, axis=-1, keepdims=True) + EPS)
    return (center * rstd, rstd)


def lane(shape):
    return lax.broadcasted_iota(jnp.int32, shape, len(shape) - 1)


def quadrant_pick(transposed=False):
    row = lax.broadcasted_iota(jnp.int32, (128, 128), 1 if transposed else 0)
    column = lax.broadcasted_iota(jnp.int32, (128, 128), 0 if transposed else 1)
    high = (row & 64) >> 1
    low = (row & 32) >> 3
    spot = high + low + ((row & 12) << 1) + (row & 3) + ((row & 16) << 2)
    return jnp.where(spot == column, 1.0, 0.0).astype(BF16)


def head_mask():
    row = lax.broadcasted_iota(jnp.int32, (LANES, WIDE), 0)
    return jnp.where(row // SPOTS == lane((LANES, WIDE)) // HEAD_DIM, 1.0, 0.0).astype(BF16)


def expand(value, mask_ref):
    return jnp.concatenate([value] * HEADS, axis=0) * mask_ref[...]


def fold(full):
    head = lane((SPOTS, WIDE)) // HEAD_DIM
    out = jnp.zeros((SPOTS, WIDE), F32)
    for h in range(HEADS):
        out = out + jnp.where(head == h, full[h * SPOTS : (h + 1) * SPOTS], 0.0)
    return out


def softmax_down(scores):
    expo = jnp.exp(scores - jnp.max(scores, axis=0, keepdims=True))
    return expo / jnp.sum(expo, axis=0, keepdims=True)


def attention_back(query, key, value, d_mixed, probs, query_wide, mask_ref):
    weights = probs.astype(BF16)
    d_wide = expand(d_mixed, mask_ref)
    d_probs = dot(value, d_wide, NT)
    d_value = dot(weights, d_wide).astype(BF16)
    d_scores = (probs * (d_probs - jnp.sum(probs * d_probs, axis=0, keepdims=True))).astype(BF16)
    d_key = (dot(d_scores, query_wide) * SCALE).astype(BF16)
    d_query = (fold(dot(d_scores, key, TN)) * SCALE).astype(BF16)
    return (d_query, d_key, d_value)


def copy_all(pairs, sems, first=0):
    moves = [
        pltpu.make_async_copy(source, target, sems.at[first + i])
        for i, (source, target) in enumerate(pairs)
    ]
    for move in moves:
        move.start()
    return moves


def wait_all(moves):
    for move in moves:
        move.wait()


def prepare(core_ref, qkv, proj, out, block, sems):
    start = pl.multiple_of(core_ref[0] * HALF, 128)
    block[0:SHARE] = qkv[:, pl.ds(start, HALF)]
    block[SHARE : SHARE + ROWS] = proj[:, pl.ds(start, HALF)]
    wait_all(copy_all([(block, out.at[i]) for i in range(8)], sems))


def biases(
    edge_ref,
    table_p,
    table_s,
    tok,
    cot,
    to_p,
    to_s,
    to_rows,
    to_cot,
    out_p,
    out_s,
    tables,
    wide,
    rows,
    quads,
    sems,
):
    rows[...] = normalize(tok[...].astype(F32))[0].astype(BF16)
    quads[...] = dot(quadrant_pick(), cot[...]).astype(BF16)
    stores = copy_all([(rows, to_rows), (quads, to_cot)], sems)
    tables[...] = jnp.zeros_like(tables)
    tables[0:HEADS, 0:REL] = table_p[...]
    tables[HEADS : 2 * HEADS, 0:REL] = table_s[...]
    values = tables[...]
    high = values.astype(BF16)
    rest = values - high.astype(F32)
    middle = rest.astype(BF16)
    low = (rest - middle.astype(F32)).astype(BF16)
    ones = offset_pick()
    spread = (dot(high, ones) + dot(middle, ones)) + dot(low, ones)
    for row in range(2 * HEADS):
        for d in range(WIN):
            wide[row * WIN + d : row * WIN + d + 1] = spread[row : row + 1, d * 128 : (d + 1) * 128]
    left = lane((WIN, 128)) < SPOTS
    for c in range(WIN):
        move = (7 - c) * WIN
        for pair in range(HEADS // 2):
            for t, out in ((0, out_p), (1, out_s)):
                even = (t * HEADS + 2 * pair) * WIN
                first = pltpu.roll(wide[even : even + WIN], (128 - move) % 128, 1)
                second = pltpu.roll(wide[even + WIN : even + 2 * WIN], (SPOTS - move) % 128, 1)
                out[c * WIN : (c + 1) * WIN, pair * 128 : (pair + 1) * 128] = jnp.where(left, first, second)
    at = lane((SPOTS, LANES))
    key_at = lax.broadcasted_iota(jnp.int32, (SPOTS, LANES), 0)
    cross = at ^ key_at
    barred = (cross & 32) * edge_ref[0] + (cross & 4) * edge_ref[1]
    out_s[...] = jnp.where(barred != 0, NEG, out_s[...])
    wait_all(stores + copy_all([(out_p, to_p), (out_s, to_s)], sems, 2))


def project(rows_ref, w_mine, w_other, mine, other):
    return dot(rows_ref[:, pl.ds(mine, HALF)], w_mine, NT) + dot(
        rows_ref[:, pl.ds(other, HALF)], w_other, NT
    )


def sides(core_ref):
    mine = pl.multiple_of(core_ref[0] * HALF, 128)
    return (mine, pl.multiple_of(HALF - mine, 128))


def qkv_of(ref):
    return ref[:, 0:SHARE].reshape(3 * WIDE, HALF)


def proj_of(ref):
    return ref[:, SHARE : SHARE + ROWS].reshape(WIDE, HALF)


def input_grad(grad, normed, rstd, d_packed, w_mine, w_other, mine, other, sums):
    sums[:, pl.ds(mine, HALF)] = dot(d_packed, w_mine)
    sums[:, pl.ds(other, HALF)] = dot(d_packed, w_other)
    d_normed = sums[...]
    d_input = rstd * (
        d_normed
        - jnp.mean(d_normed, axis=-1, keepdims=True)
        - normed * jnp.mean(d_normed * normed, axis=-1, keepdims=True)
    )
    return (grad + d_input).astype(BF16)


def plain_forward(
    core_ref,
    tok_far,
    cot_far,
    bias_far,
    rows_far,
    w_mine_ref,
    w_other_ref,
    out_o,
    out_r,
    out_b,
    out_d,
    tok,
    bias_p,
    packets,
    rows,
    sums,
    mask,
    sems,
):
    mine, other = sides(core_ref)
    loads = copy_all(
        [
            (rows_far, rows),
            (bias_far, bias_p),
            (tok_far, tok),
            (cot_far, packets.at[:, D + WIDE :]),
        ],
        sems,
    )
    mask[...] = head_mask()
    loads[0].wait()
    w_mine, w_other = qkv_of(w_mine_ref), qkv_of(w_other_ref)
    packed = project(rows, w_mine, w_other, mine, other).astype(BF16)
    loads[1].wait()
    mixed = []
    for s in range(2):
        part = packed[s * SPOTS : (s + 1) * SPOTS]
        query, key, value = part[:, :WIDE], part[:, WIDE : 2 * WIDE], part[:, 2 * WIDE :]
        probs = softmax_down(dot(key, expand(query, mask), NT) * SCALE + bias_p[...])
        mixed.append(fold(dot(probs.astype(BF16), value, TN)).astype(BF16))
    mixed = jnp.concatenate(mixed, axis=0)
    sums[:, pl.ds(mine, HALF)] = dot(mixed, proj_of(w_mine_ref))
    sums[:, pl.ds(other, HALF)] = dot(mixed, proj_of(w_other_ref))
    wait_all(loads[2:])
    block_out = (tok[...].astype(F32) + sums[...]).astype(BF16)
    pick = quadrant_pick()
    for whole, first in ((block_out, 0), (mixed, D)):
        packets[:, first : first + whole.shape[1]] = dot(pick, whole).astype(BF16)
    outs = (out_d, out_b, out_r, out_o)
    wait_all(copy_all([(packets.at[i * 32 : (i + 1) * 32], out) for i, out in enumerate(outs)], sems, 4))


def main_begin(
    core_ref,
    own_far,
    bias_far,
    right,
    below,
    diag,
    w_mine_ref,
    out_grads,
    out_normed,
    out_rows,
    out_rstd,
    out_mixed,
    out_packed,
    out_d_mixed,
    out_bias,
    staged,
    sems,
):
    mine, _ = sides(core_ref)
    loads = copy_all([(own_far, staged.at[0:32]), (bias_far, out_bias)], sems)
    for i, part in ((1, right), (2, below), (3, diag)):
        staged[i * 32 : (i + 1) * 32] = part[...]
    pick = quadrant_pick(True)
    loads[0].wait()
    out_grads[...] = dot(pick, staged[:, D + WIDE :]).astype(BF16)
    block_out = dot(pick, staged[:, 0:D])
    out_mixed[...] = dot(pick, staged[:, D : D + WIDE]).astype(BF16)
    normed, rstd = normalize(block_out)
    out_normed[...] = normed
    out_rstd[...] = jnp.broadcast_to(rstd, (128, 128))
    out_rows[...] = normed.astype(BF16)
    out_packed[...] = dot(out_rows[:, pl.ds(mine, HALF)], qkv_of(w_mine_ref), NT)
    out_d_mixed[...] = dot(out_grads[:, pl.ds(mine, HALF)], proj_of(w_mine_ref), NT)
    loads[1].wait()


def main_kernel(
    grad_scale,
    core_ref,
    grads,
    normed_ref,
    rows,
    rstd_ref,
    mixed_ref,
    packed_ref,
    d_mixed_ref,
    bias_s,
    w_mine_ref,
    w_other_ref,
    to_own,
    to_column,
    to_below,
    out_keep,
    out_send,
    quads,
    rows_small,
    sums,
    mask,
    sems,
):
    mine, other = sides(core_ref)
    mask[...] = head_mask()
    normed, rstd = normed_ref[...], rstd_ref[:, 0:1]
    mixed_plain = mixed_ref[...]
    w_mine, w_other = qkv_of(w_mine_ref), qkv_of(w_other_ref)
    packed = packed_ref[...] + dot(rows[:, pl.ds(other, HALF)], w_other, NT)
    packed = packed.astype(BF16)
    d_mixed = d_mixed_ref[...] + dot(grads[:, pl.ds(other, HALF)], proj_of(w_other_ref), NT)
    d_mixed = d_mixed.astype(BF16)
    mixed, d_packed = [], []
    for s in range(2):
        part = packed[s * SPOTS : (s + 1) * SPOTS]
        query, key, value = part[:, :WIDE], part[:, WIDE : 2 * WIDE], part[:, 2 * WIDE :]
        query_wide = expand(query, mask)
        probs = softmax_down(dot(key, query_wide, NT) * SCALE + bias_s[...])
        mixed.append(fold(dot(probs.astype(BF16), value, TN)).astype(BF16))
        back = attention_back(
            query, key, value, d_mixed[s * SPOTS : (s + 1) * SPOTS], probs, query_wide, mask
        )
        d_packed.append(jnp.concatenate(back, axis=1))
    mixed_shift = jnp.concatenate(mixed, axis=0)
    d_packed = jnp.concatenate(d_packed, axis=0)
    grad = input_grad(
        grads[...].astype(F32), normed, rstd, d_packed, w_mine, w_other, mine, other, sums
    )
    quads[...] = dot(quadrant_pick(), grad).astype(BF16)
    stores = copy_all(
        [
            (quads.at[0:32], to_own),
            (quads.at[32:64], to_column.at[0:32]),
            (quads.at[96:128], to_column.at[32:64]),
            (quads.at[64:96], to_below),
        ],
        sems,
    )
    rows_small[...] = grad
    for out, start in ((out_send, other), (out_keep, mine)):
        part = dot(mixed_shift, grads[:, pl.ds(start, HALF)], TN) * grad_scale
        out[:, 1] = part.astype(BF16).reshape(8, ROWS, HALF)
        part = dot(mixed_plain, rows_small[:, pl.ds(start, HALF)], TN) * grad_scale
        out[:, 0] = part.astype(BF16).reshape(8, ROWS, HALF)
    wait_all(stores)


def sum_copies(parts, out):
    value = jnp.sum(parts[...].astype(F32), axis=0).astype(BF16)
    for i in range(out.shape[0]):
        out[i] = value


def finish(parts, out_plain, out_shift):
    for i, out in enumerate((out_plain, out_shift)):
        out[:, 0:HALF] = parts[0, i].astype(F32)
        out[:, HALF:D] = parts[1, i].astype(F32)


def plain_back(
    core_ref,
    tok_far,
    own_far,
    bias_far,
    mine_far,
    other_far,
    column,
    row,
    out,
    tok,
    bias_p,
    w_mine_ref,
    w_other_ref,
    staged,
    rows,
    grads,
    sums,
    mask,
    sems,
):
    mine, other = sides(core_ref)
    loads = copy_all(
        [
            (tok_far, tok),
            (mine_far, w_mine_ref),
            (other_far, w_other_ref),
            (own_far, staged.at[96:128]),
            (bias_far, bias_p),
        ],
        sems,
    )
    mask[...] = head_mask()
    staged[0:32] = row[32:64]
    staged[32:64] = row[0:32]
    staged[64:96] = column[0:32]
    loads[0].wait()
    normed, rstd = normalize(tok[...].astype(F32))
    rows[...] = normed.astype(BF16)
    wait_all(loads[1:])
    w_mine, w_other = qkv_of(w_mine_ref), qkv_of(w_other_ref)
    packed = project(rows, w_mine, w_other, mine, other).astype(BF16)
    gathered = dot(quadrant_pick(True), staged[...])
    grads[...] = gathered.astype(BF16)
    d_mixed = project(grads, proj_of(w_mine_ref), proj_of(w_other_ref), mine, other).astype(BF16)
    d_packed = []
    for s in range(2):
        part = packed[s * SPOTS : (s + 1) * SPOTS]
        query, key, value = part[:, :WIDE], part[:, WIDE : 2 * WIDE], part[:, 2 * WIDE :]
        query_wide = expand(query, mask)
        probs = softmax_down(dot(key, query_wide, NT) * SCALE + bias_p[...])
        back = attention_back(
            query, key, value, d_mixed[s * SPOTS : (s + 1) * SPOTS], probs, query_wide, mask
        )
        d_packed.append(jnp.concatenate(back, axis=1))
    d_packed = jnp.concatenate(d_packed, axis=0)
    out[...] = input_grad(gathered, normed, rstd, d_packed, w_mine, w_other, mine, other, sums)


VMEM = pl.BlockSpec(memory_space=pltpu.VMEM)
SMEM = pl.BlockSpec(memory_space=pltpu.SMEM)
HBM = pl.BlockSpec(memory_space=pltpu.HBM)


def params(size=32):
    return pltpu.CompilerParams(vmem_limit_bytes=size * 1024 * 1024)


def far(value):
    return pltpu.with_memory_space_constraint(value, pltpu.HBM)


def cost(flops, size):
    return pl.CostEstimate(flops=flops, bytes_accessed=size, transcendentals=0)


def tm_groups(bits):
    size = lax.axis_size("tm")
    step = {"core": 1, "y_hi": 2, "z": 8}[bits]
    count = {"core": 2, "y_hi": 4, "z": 8}[bits]
    groups = []
    for first in range(size):
        if (first // step) % count == 0:
            groups.append([first + step * i for i in range(count)])
    return groups


def swap(value, axis, groups=None):
    return lax.all_to_all(value, axis, 0, 0, axis_index_groups=groups)


def from_offset(value, along_tm, along_freq):
    n_tm, n_freq = lax.axis_size("tm"), lax.axis_size("freq")
    pairs = []
    for t in range(n_tm):
        for f in range(n_freq):
            source = ((t + along_tm) % n_tm) * n_freq + (f + along_freq) % n_freq
            pairs.append((source, t * n_freq + f))
    return lax.ppermute(value, ("tm", "freq"), pairs)


def other_core(value):
    return lax.ppermute(value, "tm", [(i, i ^ 1) for i in range(lax.axis_size("tm"))])


def summed(parts, count):
    return pl.pallas_call(
        sum_copies,
        out_shape=jax.ShapeDtypeStruct((count,) + parts.shape[1:], BF16),
        in_specs=[VMEM],
        out_specs=VMEM,
        compiler_params=params(),
        name="sum_copies",
    )(parts)


def shards(
    tokens, cotangent, qkv_plain, qkv_shift, proj_plain, proj_shift, table_plain, table_shift
):
    core = (lax.axis_index("tm") % 2).astype(jnp.int32).reshape(1)
    last_freq = lax.axis_index("freq") == lax.axis_size("freq") - 1
    last_time = lax.axis_index("tm") == lax.axis_size("tm") - 1
    edge = jnp.stack([last_freq, last_time]).astype(jnp.int32)
    grad_scale = 1.0 / math.sqrt(128 * lax.axis_size("tm") * lax.axis_size("freq"))
    tok = tokens.reshape(128, D)
    cot = cotangent.reshape(128, D)

    def share(qkv, proj):
        return pl.pallas_call(
            prepare,
            out_shape=pltpu.HBM((8, SHARE + ROWS, HALF), BF16),
            in_specs=[SMEM, VMEM, VMEM],
            out_specs=HBM,
            scratch_shapes=[
                pltpu.VMEM((SHARE + ROWS, HALF), BF16),
                pltpu.SemaphoreType.DMA((8,)),
            ],
            compiler_params=params(60),
            name="prepare",
        )(core, qkv.T, proj)

    first_mine = swap(share(qkv_plain, proj_plain), "freq")
    second_share = share(qkv_shift, proj_shift)
    table = pltpu.HBM((SPOTS, LANES), F32)
    tile = pltpu.HBM((128, D), BF16)
    bias_p, bias_s, rows, cot_quads = pl.pallas_call(
        biases,
        out_shape=(table, table, tile, tile),
        in_specs=[SMEM] + [VMEM] * 4,
        out_specs=[HBM] * 4,
        scratch_shapes=[
            pltpu.VMEM((SPOTS, LANES), F32),
            pltpu.VMEM((SPOTS, LANES), F32),
            pltpu.VMEM((32, 256), F32),
            pltpu.VMEM((2 * HEADS * WIN, 128), F32),
            pltpu.VMEM((128, D), BF16),
            pltpu.VMEM((128, D), BF16),
            pltpu.SemaphoreType.DMA((4,)),
        ],
        compiler_params=params(),
        name="biases",
    )(edge, table_plain, table_shift, tok, cot)

    first_mine, second_share, bias_p, bias_s = lax.optimization_barrier(
        (first_mine, second_share, bias_p, bias_s)
    )
    second_mine = swap(second_share, "freq")
    first_other = other_core(first_mine)
    packet = pltpu.HBM((32, 2 * D + WIDE), BF16)
    own, to_left, to_above, to_diag = pl.pallas_call(
        plain_forward,
        out_shape=(packet,) * 4,
        in_specs=[SMEM] + [HBM] * 4 + [VMEM] * 2,
        out_specs=[HBM] * 4,
        scratch_shapes=[
            pltpu.VMEM((128, D), BF16),
            pltpu.VMEM((SPOTS, LANES), F32),
            pltpu.VMEM((128, 2 * D + WIDE), BF16),
            pltpu.VMEM((128, D), BF16),
            pltpu.VMEM((128, D), F32),
            pltpu.VMEM((LANES, WIDE), BF16),
            pltpu.SemaphoreType.DMA((8,)),
        ],
        compiler_params=params(),
        cost_estimate=cost(20_000_000_000, 1_000_000),
        name="plain_forward",
    )(core, far(tok), far(cot_quads), far(bias_p), far(rows), first_mine, first_other)
    right = from_offset(to_left, 1, 0)
    below = from_offset(to_above, 0, 1)
    diag = from_offset(to_diag, 1, 1)
    second_mine, right, below, diag = lax.optimization_barrier(
        (second_mine, right, below, diag)
    )
    second_other = other_core(second_mine)
    piece = pltpu.HBM((32, D), BF16)
    column = pltpu.HBM((64, D), BF16)
    local = jax.ShapeDtypeStruct((8, 2, ROWS, HALF), BF16)
    def near(shape, dtype):
        return jax.ShapeDtypeStruct(shape, dtype)

    begun = pl.pallas_call(
        main_begin,
        out_shape=(
            near((128, D), BF16),
            near((128, D), F32),
            near((128, D), BF16),
            near((128, 128), F32),
            near((128, WIDE), BF16),
            near((128, 3 * WIDE), F32),
            near((128, WIDE), F32),
            near((SPOTS, LANES), F32),
        ),
        in_specs=[SMEM] + [HBM] * 2 + [VMEM] * 4,
        out_specs=[VMEM] * 8,
        scratch_shapes=[
            pltpu.VMEM((128, 2 * D + WIDE), BF16),
            pltpu.SemaphoreType.DMA((2,)),
        ],
        compiler_params=params(),
        cost_estimate=cost(5_000_000_000, 1_000_000),
        name="main_begin",
    )(core, far(own), far(bias_s), right, below, diag, second_mine)
    g_own, to_right, to_below, keep, send = pl.pallas_call(
        lambda *refs: main_kernel(grad_scale, *refs),
        out_shape=(piece, column, piece, local, local),
        in_specs=[SMEM] + [VMEM] * 10,
        out_specs=[HBM] * 3 + [VMEM] * 2,
        scratch_shapes=[
            pltpu.VMEM((128, D), BF16),
            pltpu.VMEM((128, D), BF16),
            pltpu.VMEM((128, D), F32),
            pltpu.VMEM((LANES, WIDE), BF16),
            pltpu.SemaphoreType.DMA((4,)),
        ],
        compiler_params=params(),
        cost_estimate=cost(1_000_000, 1_000_000),
        name="main",
    )(core, *begun, second_mine, second_other)

    part = (keep.astype(F32) + other_core(send).astype(F32)).astype(BF16)
    part, to_right, to_below = lax.optimization_barrier((part, to_right, to_below))
    part = swap(part, "freq")
    column = from_offset(to_right, -1, 0)
    part, column, to_below = lax.optimization_barrier((part, column, to_below))
    part = swap(summed(part, 4), "tm", tm_groups("y_hi"))
    row = from_offset(jnp.concatenate([to_below, column[32:64]], axis=0), 0, -1)
    part, row = lax.optimization_barrier((part, row))
    part = swap(summed(part, 8), "tm", tm_groups("z"))
    grad_tokens = pl.pallas_call(
        plain_back,
        out_shape=jax.ShapeDtypeStruct((128, D), BF16),
        in_specs=[SMEM] + [HBM] * 5 + [VMEM] * 2,
        out_specs=VMEM,
        scratch_shapes=[
            pltpu.VMEM((128, D), BF16),
            pltpu.VMEM((SPOTS, LANES), F32),
            pltpu.VMEM((8, SHARE + ROWS, HALF), BF16),
            pltpu.VMEM((8, SHARE + ROWS, HALF), BF16),
            pltpu.VMEM((128, D), BF16),
            pltpu.VMEM((128, D), BF16),
            pltpu.VMEM((128, D), BF16),
            pltpu.VMEM((128, D), F32),
            pltpu.VMEM((LANES, WIDE), BF16),
            pltpu.SemaphoreType.DMA((5,)),
        ],
        compiler_params=params(),
        cost_estimate=cost(4_000_000_000, 4_000_000),
        name="plain_back",
    )(core, far(tok), far(g_own), far(bias_p), far(first_mine), far(first_other), column, row)
    part, grad_tokens = lax.optimization_barrier((part, grad_tokens))
    part = summed(part, 1)[0]
    part = lax.all_gather(part, "tm", axis_index_groups=tm_groups("core"))
    grad_plain, grad_shift = pl.pallas_call(
        finish,
        out_shape=(jax.ShapeDtypeStruct((ROWS, D), F32),) * 2,
        in_specs=[VMEM],
        out_specs=[VMEM] * 2,
        compiler_params=params(),
        name="finish",
    )(part)
    return (grad_tokens.reshape(tokens.shape), grad_plain, grad_shift)


def solution(mesh):
    placed = (
        P(None, "freq", "tm", None),
        P(None, "freq", "tm", None),
        P(None, "freq"),
        P(None, "freq"),
        P("freq", None),
        P("freq", None),
        P(),
        P(),
    )
    return jax.shard_map(
        shards,
        mesh=mesh,
        in_specs=placed,
        out_specs=(P(None, "freq", "tm", None), P("freq", None), P("freq", None)),
        check_vma=False,
    )
```

```python
import math

import jax
import jax.numpy as jnp
from jax import lax
from jax.experimental import pallas as pl
from jax.experimental.pallas import tpu as pltpu
from jax.sharding import PartitionSpec as P

D = 768
HEADS = 12
HEAD_DIM = 32
WIN = 8
SPOTS = 64
REL = 225
WIDE = HEADS * HEAD_DIM
LANES = HEADS * SPOTS
HALF = D // 2
SHARE = 144
ROWS = 48

NEG = -1e30
EPS = 1e-05
SCALE = HEAD_DIM ** (-0.5)

NN = (((1,), (0,)), ((), ()))
NT = (((1,), (1,)), ((), ()))
TN = (((0,), (0,)), ((), ()))

F32 = jnp.float32
BF16 = jnp.bfloat16


def offset_pick():
    column = lane((256, WIN * 128))
    entry = ((column >> 3) & 15) * 15 + (column & 7) - (column >> 7) + 7
    row = lax.broadcasted_iota(jnp.int32, (256, WIN * 128), 0)
    return jnp.where(row == entry, 1.0, 0.0).astype(BF16)


def dot(left, right, dims=NN):
    return lax.dot_general(left, right, dims, preferred_element_type=F32)


def normalize(values):
    center = values - jnp.mean(values, axis=-1, keepdims=True)
    rstd = lax.rsqrt(jnp.mean(center * center, axis=-1, keepdims=True) + EPS)
    return (center * rstd, rstd)


def lane(shape):
    return lax.broadcasted_iota(jnp.int32, shape, len(shape) - 1)


def quadrant_pick(transposed=False):
    row = lax.broadcasted_iota(jnp.int32, (128, 128), 1 if transposed else 0)
    column = lax.broadcasted_iota(jnp.int32, (128, 128), 0 if transposed else 1)
    high = (row & 64) >> 1
    low = (row & 32) >> 3
    spot = high + low + ((row & 12) << 1) + (row & 3) + ((row & 16) << 2)
    return jnp.where(spot == column, 1.0, 0.0).astype(BF16)


def head_mask():
    row = lax.broadcasted_iota(jnp.int32, (LANES, WIDE), 0)
    return jnp.where(row // SPOTS == lane((LANES, WIDE)) // HEAD_DIM, 1.0, 0.0).astype(BF16)


def expand(value, mask_ref):
    return jnp.concatenate([value] * HEADS, axis=0) * mask_ref[...]


def fold(full):
    head = lane((SPOTS, WIDE)) // HEAD_DIM
    out = jnp.zeros((SPOTS, WIDE), F32)
    for h in range(HEADS):
        out = out + jnp.where(head == h, full[h * SPOTS : (h + 1) * SPOTS], 0.0)
    return out


def softmax_down(scores):
    expo = jnp.exp(scores - jnp.max(scores, axis=0, keepdims=True))
    return expo / jnp.sum(expo, axis=0, keepdims=True)


def attention_back(query, key, value, d_mixed, probs, query_wide, mask_ref):
    weights = probs.astype(BF16)
    d_wide = expand(d_mixed, mask_ref)
    d_probs = dot(value, d_wide, NT)
    d_value = dot(weights, d_wide).astype(BF16)
    d_scores = (probs * (d_probs - jnp.sum(probs * d_probs, axis=0, keepdims=True))).astype(BF16)
    d_key = (dot(d_scores, query_wide) * SCALE).astype(BF16)
    d_query = (fold(dot(d_scores, key, TN)) * SCALE).astype(BF16)
    return (d_query, d_key, d_value)


def copy_all(pairs, sems, first=0):
    moves = [
        pltpu.make_async_copy(source, target, sems.at[first + i])
        for i, (source, target) in enumerate(pairs)
    ]
    for move in moves:
        move.start()
    return moves


def wait_all(moves):
    for move in moves:
        move.wait()


def prepare(core_ref, qkv, proj, out, block, sems):
    start = pl.multiple_of(core_ref[0] * HALF, 128)
    block[0:SHARE] = qkv[:, pl.ds(start, HALF)]
    block[SHARE : SHARE + ROWS] = proj[:, pl.ds(start, HALF)]
    wait_all(copy_all([(block, out.at[i]) for i in range(8)], sems))


def biases(
    edge_ref,
    table_p,
    table_s,
    tok,
    cot,
    to_p,
    to_s,
    to_rows,
    to_cot,
    out_p,
    out_s,
    tables,
    wide,
    rows,
    quads,
    sems,
):
    rows[...] = normalize(tok[...].astype(F32))[0].astype(BF16)
    quads[...] = dot(quadrant_pick(), cot[...]).astype(BF16)
    stores = copy_all([(rows, to_rows), (quads, to_cot)], sems)
    tables[...] = jnp.zeros_like(tables)
    tables[0:HEADS, 0:REL] = table_p[...]
    tables[HEADS : 2 * HEADS, 0:REL] = table_s[...]
    values = tables[...]
    high = values.astype(BF16)
    rest = values - high.astype(F32)
    middle = rest.astype(BF16)
    low = (rest - middle.astype(F32)).astype(BF16)
    ones = offset_pick()
    spread = (dot(high, ones) + dot(middle, ones)) + dot(low, ones)
    for row in range(2 * HEADS):
        for d in range(WIN):
            wide[row * WIN + d : row * WIN + d + 1] = spread[row : row + 1, d * 128 : (d + 1) * 128]
    left = lane((WIN, 128)) < SPOTS
    for c in range(WIN):
        move = (7 - c) * WIN
        for pair in range(HEADS // 2):
            for t, out in ((0, out_p), (1, out_s)):
                even = (t * HEADS + 2 * pair) * WIN
                first = pltpu.roll(wide[even : even + WIN], (128 - move) % 128, 1)
                second = pltpu.roll(wide[even + WIN : even + 2 * WIN], (SPOTS - move) % 128, 1)
                out[c * WIN : (c + 1) * WIN, pair * 128 : (pair + 1) * 128] = jnp.where(left, first, second)
    at = lane((SPOTS, LANES))
    key_at = lax.broadcasted_iota(jnp.int32, (SPOTS, LANES), 0)
    cross = at ^ key_at
    barred = (cross & 32) * edge_ref[0] + (cross & 4) * edge_ref[1]
    out_s[...] = jnp.where(barred != 0, NEG, out_s[...])
    wait_all(stores + copy_all([(out_p, to_p), (out_s, to_s)], sems, 2))


def project(rows_ref, w_mine, w_other, mine, other):
    return dot(rows_ref[:, pl.ds(mine, HALF)], w_mine, NT) + dot(
        rows_ref[:, pl.ds(other, HALF)], w_other, NT
    )


def sides(core_ref):
    mine = pl.multiple_of(core_ref[0] * HALF, 128)
    return (mine, pl.multiple_of(HALF - mine, 128))


def qkv_of(ref):
    return ref[:, 0:SHARE].reshape(3 * WIDE, HALF)


def proj_of(ref):
    return ref[:, SHARE : SHARE + ROWS].reshape(WIDE, HALF)


def input_grad(grad, normed, rstd, d_packed, w_mine, w_other, mine, other, sums):
    sums[:, pl.ds(mine, HALF)] = dot(d_packed, w_mine)
    sums[:, pl.ds(other, HALF)] = dot(d_packed, w_other)
    d_normed = sums[...]
    d_input = rstd * (
        d_normed
        - jnp.mean(d_normed, axis=-1, keepdims=True)
        - normed * jnp.mean(d_normed * normed, axis=-1, keepdims=True)
    )
    return (grad + d_input).astype(BF16)


def plain_forward(
    core_ref,
    tok_far,
    cot_far,
    bias_far,
    rows_far,
    w_mine_ref,
    w_other_ref,
    out_o,
    out_r,
    out_b,
    out_d,
    tok,
    bias_p,
    packets,
    rows,
    sums,
    mask,
    sems,
):
    mine, other = sides(core_ref)
    loads = copy_all(
        [
            (rows_far, rows),
            (bias_far, bias_p),
            (tok_far, tok),
            (cot_far, packets.at[:, D + WIDE :]),
        ],
        sems,
    )
    mask[...] = head_mask()
    loads[0].wait()
    w_mine, w_other = qkv_of(w_mine_ref), qkv_of(w_other_ref)
    packed = project(rows, w_mine, w_other, mine, other).astype(BF16)
    loads[1].wait()
    mixed = []
    for s in range(2):
        part = packed[s * SPOTS : (s + 1) * SPOTS]
        query, key, value = part[:, :WIDE], part[:, WIDE : 2 * WIDE], part[:, 2 * WIDE :]
        probs = softmax_down(dot(key, expand(query, mask), NT) * SCALE + bias_p[...])
        mixed.append(fold(dot(probs.astype(BF16), value, TN)).astype(BF16))
    mixed = jnp.concatenate(mixed, axis=0)
    sums[:, pl.ds(mine, HALF)] = dot(mixed, proj_of(w_mine_ref))
    sums[:, pl.ds(other, HALF)] = dot(mixed, proj_of(w_other_ref))
    wait_all(loads[2:])
    block_out = (tok[...].astype(F32) + sums[...]).astype(BF16)
    pick = quadrant_pick()
    for whole, first in ((block_out, 0), (mixed, D)):
        packets[:, first : first + whole.shape[1]] = dot(pick, whole).astype(BF16)
    outs = (out_d, out_b, out_r, out_o)
    wait_all(copy_all([(packets.at[i * 32 : (i + 1) * 32], out) for i, out in enumerate(outs)], sems, 4))


def main_begin(
    core_ref,
    own_far,
    bias_far,
    right,
    below,
    diag,
    w_mine_ref,
    out_grads,
    out_normed,
    out_rows,
    out_rstd,
    out_mixed,
    out_packed,
    out_d_mixed,
    out_bias,
    out_mask,
    staged,
    sems,
):
    mine, _ = sides(core_ref)
    loads = copy_all([(own_far, staged.at[0:32]), (bias_far, out_bias)], sems)
    for i, part in ((1, right), (2, below), (3, diag)):
        staged[i * 32 : (i + 1) * 32] = part[...]
    pick = quadrant_pick(True)
    out_mask[...] = head_mask()
    loads[0].wait()
    out_grads[...] = dot(pick, staged[:, D + WIDE :]).astype(BF16)
    block_out = dot(pick, staged[:, 0:D])
    out_mixed[...] = dot(pick, staged[:, D : D + WIDE]).astype(BF16)
    normed, rstd = normalize(block_out)
    out_normed[...] = normed
    out_rstd[...] = jnp.broadcast_to(rstd, (128, 128))
    out_rows[...] = normed.astype(BF16)
    out_packed[...] = dot(out_rows[:, pl.ds(mine, HALF)], qkv_of(w_mine_ref), NT)
    out_d_mixed[...] = dot(out_grads[:, pl.ds(mine, HALF)], proj_of(w_mine_ref), NT)
    loads[1].wait()


def main_kernel(
    grad_scale,
    core_ref,
    grads,
    normed_ref,
    rows,
    rstd_ref,
    mixed_ref,
    packed_ref,
    d_mixed_ref,
    bias_s,
    mask,
    w_mine_ref,
    w_other_ref,
    to_own,
    to_column,
    to_below,
    out_keep,
    out_send,
    quads,
    rows_small,
    sums,
    sems,
):
    mine, other = sides(core_ref)
    normed, rstd = normed_ref[...], rstd_ref[:, 0:1]
    mixed_plain = mixed_ref[...]
    w_mine, w_other = qkv_of(w_mine_ref), qkv_of(w_other_ref)
    packed = packed_ref[...] + dot(rows[:, pl.ds(other, HALF)], w_other, NT)
    packed = packed.astype(BF16)
    d_mixed = d_mixed_ref[...] + dot(grads[:, pl.ds(other, HALF)], proj_of(w_other_ref), NT)
    d_mixed = d_mixed.astype(BF16)
    mixed, d_packed = [], []
    for s in range(2):
        part = packed[s * SPOTS : (s + 1) * SPOTS]
        query, key, value = part[:, :WIDE], part[:, WIDE : 2 * WIDE], part[:, 2 * WIDE :]
        query_wide = expand(query, mask)
        probs = softmax_down(dot(key, query_wide, NT) * SCALE + bias_s[...])
        mixed.append(fold(dot(probs.astype(BF16), value, TN)).astype(BF16))
        back = attention_back(
            query, key, value, d_mixed[s * SPOTS : (s + 1) * SPOTS], probs, query_wide, mask
        )
        d_packed.append(jnp.concatenate(back, axis=1))
    mixed_shift = jnp.concatenate(mixed, axis=0)
    d_packed = jnp.concatenate(d_packed, axis=0)
    grad = input_grad(
        grads[...].astype(F32), normed, rstd, d_packed, w_mine, w_other, mine, other, sums
    )
    quads[...] = dot(quadrant_pick(), grad).astype(BF16)
    stores = copy_all(
        [
            (quads.at[0:32], to_own),
            (quads.at[32:64], to_column.at[0:32]),
            (quads.at[96:128], to_column.at[32:64]),
            (quads.at[64:96], to_below),
        ],
        sems,
    )
    rows_small[...] = grad
    for out, start in ((out_send, other), (out_keep, mine)):
        part = dot(mixed_shift, grads[:, pl.ds(start, HALF)], TN) * grad_scale
        out[:, 1] = part.astype(BF16).reshape(8, ROWS, HALF)
        part = dot(mixed_plain, rows_small[:, pl.ds(start, HALF)], TN) * grad_scale
        out[:, 0] = part.astype(BF16).reshape(8, ROWS, HALF)
    wait_all(stores)


def sum_copies(parts, out):
    value = jnp.sum(parts[...].astype(F32), axis=0).astype(BF16)
    for i in range(out.shape[0]):
        out[i] = value


def finish(parts, out_plain, out_shift):
    for i, out in enumerate((out_plain, out_shift)):
        out[:, 0:HALF] = parts[0, i].astype(F32)
        out[:, HALF:D] = parts[1, i].astype(F32)


def plain_back(
    core_ref,
    tok_far,
    own_far,
    bias_far,
    mine_far,
    other_far,
    column,
    row,
    out,
    tok,
    bias_p,
    w_mine_ref,
    w_other_ref,
    staged,
    rows,
    grads,
    sums,
    mask,
    sems,
):
    mine, other = sides(core_ref)
    loads = copy_all(
        [
            (tok_far, tok),
            (mine_far, w_mine_ref),
            (other_far, w_other_ref),
            (own_far, staged.at[96:128]),
            (bias_far, bias_p),
        ],
        sems,
    )
    mask[...] = head_mask()
    staged[0:32] = row[32:64]
    staged[32:64] = row[0:32]
    staged[64:96] = column[0:32]
    loads[0].wait()
    normed, rstd = normalize(tok[...].astype(F32))
    rows[...] = normed.astype(BF16)
    wait_all(loads[1:])
    w_mine, w_other = qkv_of(w_mine_ref), qkv_of(w_other_ref)
    packed = project(rows, w_mine, w_other, mine, other).astype(BF16)
    gathered = dot(quadrant_pick(True), staged[...])
    grads[...] = gathered.astype(BF16)
    d_mixed = project(grads, proj_of(w_mine_ref), proj_of(w_other_ref), mine, other).astype(BF16)
    d_packed = []
    for s in range(2):
        part = packed[s * SPOTS : (s + 1) * SPOTS]
        query, key, value = part[:, :WIDE], part[:, WIDE : 2 * WIDE], part[:, 2 * WIDE :]
        query_wide = expand(query, mask)
        probs = softmax_down(dot(key, query_wide, NT) * SCALE + bias_p[...])
        back = attention_back(
            query, key, value, d_mixed[s * SPOTS : (s + 1) * SPOTS], probs, query_wide, mask
        )
        d_packed.append(jnp.concatenate(back, axis=1))
    d_packed = jnp.concatenate(d_packed, axis=0)
    out[...] = input_grad(gathered, normed, rstd, d_packed, w_mine, w_other, mine, other, sums)


VMEM = pl.BlockSpec(memory_space=pltpu.VMEM)
SMEM = pl.BlockSpec(memory_space=pltpu.SMEM)
HBM = pl.BlockSpec(memory_space=pltpu.HBM)


def params(size=32):
    return pltpu.CompilerParams(vmem_limit_bytes=size * 1024 * 1024)


def far(value):
    return pltpu.with_memory_space_constraint(value, pltpu.HBM)


def cost(flops, size):
    return pl.CostEstimate(flops=flops, bytes_accessed=size, transcendentals=0)


def tm_groups(bits):
    size = lax.axis_size("tm")
    step = {"core": 1, "y_hi": 2, "z": 8}[bits]
    count = {"core": 2, "y_hi": 4, "z": 8}[bits]
    groups = []
    for first in range(size):
        if (first // step) % count == 0:
            groups.append([first + step * i for i in range(count)])
    return groups


def swap(value, axis, groups=None):
    return lax.all_to_all(value, axis, 0, 0, axis_index_groups=groups)


def from_offset(value, along_tm, along_freq):
    n_tm, n_freq = lax.axis_size("tm"), lax.axis_size("freq")
    pairs = []
    for t in range(n_tm):
        for f in range(n_freq):
            source = ((t + along_tm) % n_tm) * n_freq + (f + along_freq) % n_freq
            pairs.append((source, t * n_freq + f))
    return lax.ppermute(value, ("tm", "freq"), pairs)


def other_core(value):
    return lax.ppermute(value, "tm", [(i, i ^ 1) for i in range(lax.axis_size("tm"))])


def summed(parts, count):
    return pl.pallas_call(
        sum_copies,
        out_shape=jax.ShapeDtypeStruct((count,) + parts.shape[1:], BF16),
        in_specs=[VMEM],
        out_specs=VMEM,
        compiler_params=params(),
        name="sum_copies",
    )(parts)


def shards(
    tokens, cotangent, qkv_plain, qkv_shift, proj_plain, proj_shift, table_plain, table_shift
):
    core = (lax.axis_index("tm") % 2).astype(jnp.int32).reshape(1)
    last_freq = lax.axis_index("freq") == lax.axis_size("freq") - 1
    last_time = lax.axis_index("tm") == lax.axis_size("tm") - 1
    edge = jnp.stack([last_freq, last_time]).astype(jnp.int32)
    grad_scale = 1.0 / math.sqrt(128 * lax.axis_size("tm") * lax.axis_size("freq"))
    tok = tokens.reshape(128, D)
    cot = cotangent.reshape(128, D)

    def share(qkv, proj):
        return pl.pallas_call(
            prepare,
            out_shape=pltpu.HBM((8, SHARE + ROWS, HALF), BF16),
            in_specs=[SMEM, VMEM, VMEM],
            out_specs=HBM,
            scratch_shapes=[
                pltpu.VMEM((SHARE + ROWS, HALF), BF16),
                pltpu.SemaphoreType.DMA((8,)),
            ],
            compiler_params=params(60),
            name="prepare",
        )(core, qkv.T, proj)

    first_mine = swap(share(qkv_plain, proj_plain), "freq")
    second_share = share(qkv_shift, proj_shift)
    table = pltpu.HBM((SPOTS, LANES), F32)
    tile = pltpu.HBM((128, D), BF16)
    bias_p, bias_s, rows, cot_quads = pl.pallas_call(
        biases,
        out_shape=(table, table, tile, tile),
        in_specs=[SMEM] + [VMEM] * 4,
        out_specs=[HBM] * 4,
        scratch_shapes=[
            pltpu.VMEM((SPOTS, LANES), F32),
            pltpu.VMEM((SPOTS, LANES), F32),
            pltpu.VMEM((32, 256), F32),
            pltpu.VMEM((2 * HEADS * WIN, 128), F32),
            pltpu.VMEM((128, D), BF16),
            pltpu.VMEM((128, D), BF16),
            pltpu.SemaphoreType.DMA((4,)),
        ],
        compiler_params=params(),
        name="biases",
    )(edge, table_plain, table_shift, tok, cot)

    first_mine, second_share, bias_p, bias_s = lax.optimization_barrier(
        (first_mine, second_share, bias_p, bias_s)
    )
    second_mine = swap(second_share, "freq")
    first_other = other_core(first_mine)
    packet = pltpu.HBM((32, 2 * D + WIDE), BF16)
    own, to_left, to_above, to_diag = pl.pallas_call(
        plain_forward,
        out_shape=(packet,) * 4,
        in_specs=[SMEM] + [HBM] * 4 + [VMEM] * 2,
        out_specs=[HBM] * 4,
        scratch_shapes=[
            pltpu.VMEM((128, D), BF16),
            pltpu.VMEM((SPOTS, LANES), F32),
            pltpu.VMEM((128, 2 * D + WIDE), BF16),
            pltpu.VMEM((128, D), BF16),
            pltpu.VMEM((128, D), F32),
            pltpu.VMEM((LANES, WIDE), BF16),
            pltpu.SemaphoreType.DMA((8,)),
        ],
        compiler_params=params(),
        cost_estimate=cost(20_000_000_000, 1_000_000),
        name="plain_forward",
    )(core, far(tok), far(cot_quads), far(bias_p), far(rows), first_mine, first_other)
    right = from_offset(to_left, 1, 0)
    below = from_offset(to_above, 0, 1)
    diag = from_offset(to_diag, 1, 1)
    second_mine, right, below, diag = lax.optimization_barrier(
        (second_mine, right, below, diag)
    )
    second_other = other_core(second_mine)
    piece = pltpu.HBM((32, D), BF16)
    column = pltpu.HBM((64, D), BF16)
    local = jax.ShapeDtypeStruct((8, 2, ROWS, HALF), BF16)
    def near(shape, dtype):
        return jax.ShapeDtypeStruct(shape, dtype)

    begun = pl.pallas_call(
        main_begin,
        out_shape=(
            near((128, D), BF16),
            near((128, D), F32),
            near((128, D), BF16),
            near((128, 128), F32),
            near((128, WIDE), BF16),
            near((128, 3 * WIDE), F32),
            near((128, WIDE), F32),
            near((SPOTS, LANES), F32),
            near((LANES, WIDE), BF16),
        ),
        in_specs=[SMEM] + [HBM] * 2 + [VMEM] * 4,
        out_specs=[VMEM] * 9,
        scratch_shapes=[
            pltpu.VMEM((128, 2 * D + WIDE), BF16),
            pltpu.SemaphoreType.DMA((2,)),
        ],
        compiler_params=params(),
        cost_estimate=cost(5_000_000_000, 1_000_000),
        name="main_begin",
    )(core, far(own), far(bias_s), right, below, diag, second_mine)
    g_own, to_right, to_below, keep, send = pl.pallas_call(
        lambda *refs: main_kernel(grad_scale, *refs),
        out_shape=(piece, column, piece, local, local),
        in_specs=[SMEM] + [VMEM] * 11,
        out_specs=[HBM] * 3 + [VMEM] * 2,
        scratch_shapes=[
            pltpu.VMEM((128, D), BF16),
            pltpu.VMEM((128, D), BF16),
            pltpu.VMEM((128, D), F32),
            pltpu.SemaphoreType.DMA((4,)),
        ],
        compiler_params=params(),
        cost_estimate=cost(1_000_000, 1_000_000),
        name="main",
    )(core, *begun, second_mine, second_other)

    part = (keep.astype(F32) + other_core(send).astype(F32)).astype(BF16)
    part, to_right, to_below = lax.optimization_barrier((part, to_right, to_below))
    part = swap(part, "freq")
    column = from_offset(to_right, -1, 0)
    part, column, to_below = lax.optimization_barrier((part, column, to_below))
    part = swap(summed(part, 4), "tm", tm_groups("y_hi"))
    row = from_offset(jnp.concatenate([to_below, column[32:64]], axis=0), 0, -1)
    part, row = lax.optimization_barrier((part, row))
    part = swap(summed(part, 8), "tm", tm_groups("z"))
    grad_tokens = pl.pallas_call(
        plain_back,
        out_shape=jax.ShapeDtypeStruct((128, D), BF16),
        in_specs=[SMEM] + [HBM] * 5 + [VMEM] * 2,
        out_specs=VMEM,
        scratch_shapes=[
            pltpu.VMEM((128, D), BF16),
            pltpu.VMEM((SPOTS, LANES), F32),
            pltpu.VMEM((8, SHARE + ROWS, HALF), BF16),
            pltpu.VMEM((8, SHARE + ROWS, HALF), BF16),
            pltpu.VMEM((128, D), BF16),
            pltpu.VMEM((128, D), BF16),
            pltpu.VMEM((128, D), BF16),
            pltpu.VMEM((128, D), F32),
            pltpu.VMEM((LANES, WIDE), BF16),
            pltpu.SemaphoreType.DMA((5,)),
        ],
        compiler_params=params(),
        cost_estimate=cost(4_000_000_000, 4_000_000),
        name="plain_back",
    )(core, far(tok), far(g_own), far(bias_p), far(first_mine), far(first_other), column, row)
    part, grad_tokens = lax.optimization_barrier((part, grad_tokens))
    part = summed(part, 1)[0]
    part = lax.all_gather(part, "tm", axis_index_groups=tm_groups("core"))
    grad_plain, grad_shift = pl.pallas_call(
        finish,
        out_shape=(jax.ShapeDtypeStruct((ROWS, D), F32),) * 2,
        in_specs=[VMEM],
        out_specs=[VMEM] * 2,
        compiler_params=params(),
        name="finish",
    )(part)
    return (grad_tokens.reshape(tokens.shape), grad_plain, grad_shift)


def solution(mesh):
    placed = (
        P(None, "freq", "tm", None),
        P(None, "freq", "tm", None),
        P(None, "freq"),
        P(None, "freq"),
        P("freq", None),
        P("freq", None),
        P(),
        P(),
    )
    return jax.shard_map(
        shards,
        mesh=mesh,
        in_specs=placed,
        out_specs=(P(None, "freq", "tm", None), P("freq", None), P("freq", None)),
        check_vma=False,
    )
```
